32 devices in a mesh: clip: 8 (over z, x), tm: 4 (over y, core).
Axes of the slice: x: 2, y: 2, z: 4, core: 2. Of those that a mesh axis runs over, the one named last changes fastest.
Arguments:
- inputs: bfloat16 [32768, 512], P(('clip', 'tm')), may hold values from -6 to 6
- codes: int32 [32768, 8], P(('clip', 'tm')), may hold values from 0 to 2047
- levels: int32 [8], P('clip'), may hold values from 1 to 8, as said below
- attention_master: float32 [4, 512, 512], P(None, ('clip', 'tm'))
- attention_first: float32 [4, 512, 512], P(None, ('clip', 'tm'))
- attention_second: float32 [4, 512, 512], P(None, ('clip', 'tm'))
- feedforward_master: float32 [2, 512, 2048], P(None, ('clip', 'tm'))
- feedforward_first: float32 [2, 512, 2048], P(None, ('clip', 'tm'))
- feedforward_second: float32 [2, 512, 2048], P(None, ('clip', 'tm'))
- projection_master: float32 [512, 256], P(('clip', 'tm')), may hold values from -0.25 to 0.25
- projection_first: float32 [512, 256], P(('clip', 'tm'))
- projection_second: float32 [512, 256], P(('clip', 'tm'))
- codebook_master: float32 [8, 2048, 256], P(None, ('clip', 'tm')), may hold values from -3 to 3
- codebook_first: float32 [8, 2048, 256], P(None, ('clip', 'tm'))
- codebook_second: float32 [8, 2048, 256], P(None, ('clip', 'tm'))
- scales_master: float32 [6, 512], P(None, ('clip', 'tm'))
- scales_first: float32 [6, 512], P(None, ('clip', 'tm'))
- scales_second: float32 [6, 512], P(None, ('clip', 'tm'))
Outputs:
- latent: float32 [32768, 256], P(('clip', 'tm'))
- input_gradient: float32 [32768, 512], P(('clip', 'tm'))
- gradient_norm: float32 [], replicated
- attention_momentum: float32 [4, 512, 512], P(None, ('clip', 'tm'))
- attention_variance: float32 [4, 512, 512], P(None, ('clip', 'tm'))
- attention_updated: float32 [4, 512, 512], P(None, ('clip', 'tm'))
- attention_bfloat: bfloat16 [4, 512, 512], P(None, ('clip', 'tm'))
- feedforward_momentum: float32 [2, 512, 2048], P(None, ('clip', 'tm'))
- feedforward_variance: float32 [2, 512, 2048], P(None, ('clip', 'tm'))
- feedforward_updated: float32 [2, 512, 2048], P(None, ('clip', 'tm'))
- feedforward_bfloat: bfloat16 [2, 512, 2048], P(None, ('clip', 'tm'))
- projection_momentum: float32 [512, 256], P(('clip', 'tm'))
- projection_variance: float32 [512, 256], P(('clip', 'tm'))
- projection_updated: float32 [512, 256], P(('clip', 'tm'))
- projection_bfloat: bfloat16 [512, 256], P(('clip', 'tm'))
- codebook_momentum: float32 [8, 2048, 256], P(None, ('clip', 'tm'))
- codebook_variance: float32 [8, 2048, 256], P(None, ('clip', 'tm'))
- codebook_updated: float32 [8, 2048, 256], P(None, ('clip', 'tm'))
- codebook_bfloat: bfloat16 [8, 2048, 256], P(None, ('clip', 'tm'))
- scales_momentum: float32 [6, 512], P(None, ('clip', 'tm'))
- scales_variance: float32 [6, 512], P(None, ('clip', 'tm'))
- scales_updated: float32 [6, 512], P(None, ('clip', 'tm'))
- scales_bfloat: bfloat16 [6, 512], P(None, ('clip', 'tm'))
The draws below stay inside these ranges and needn't reach their ends.
Inputs may be any that keep to these rules, and one draw needn't show every extreme that they name: Some clip has 8 active levels and some clip has 1.
All inputs are finite; a program needn't handle non-finite values.
Results may differ from the reference program's by a relative error of at most 0.01.
The reference program's roundings to bfloat16 on the way count: a program that leaves them out, or rounds other values in their place, can miss the bound.
Values may be sent and summed in bfloat16 or wider, within the bound.
No kernel may reach another device: no remote copies, remote signals or barrier semaphores. Data moves between devices by JAX's collectives and lax.ppermute only.
A program may use at most 192 MiB of HBM per device.

```python
import math
import jax
import jax.numpy as jnp
from jax import lax

D = 512
HEADS = 8
FF = 2048
LAT = 256
BOOK = 2048
LEVELS = 8
WINDOW = 250
STEP = 10
CLIPS = 8
LEN = 4096
TOKENS = 32768
NPARAMS = 7474176


def moment_draw(key, shape, unit):
    return 0.111 * unit * jax.random.normal(key, shape, jnp.float32)


def square_draw(key, shape, unit):
    return 0.0526 * unit * unit * jnp.exp(jax.random.uniform(key, shape, jnp.float32, 0.0, math.log(4.0)))


def common_unit(boost):
    return boost / math.sqrt(NPARAMS)


def book_unit():
    return 0.4 / (BOOK * math.sqrt(D * LAT))


def draw_codes(key, part):
    key = jax.random.fold_in(key, 1)
    left_key, right_key = jax.random.split(key)
    left_draw = jax.random.randint(left_key, (TOKENS, LEVELS), 0, BOOK)
    right_draw = jax.random.randint(right_key, (TOKENS, LEVELS), 0, BOOK)
    return jnp.maximum(left_draw, right_draw).astype(jnp.int32)


def draw_levels(key, part):
    key = jax.random.fold_in(key, 2)
    count_key, top_key, bottom_key = jax.random.split(key, 3)
    counts = jax.random.randint(count_key, (CLIPS,), 1, LEVELS + 1)
    top_clip = jax.random.randint(top_key, (), 0, CLIPS)
    bottom_clip = (top_clip + 1 + jax.random.randint(bottom_key, (), 0, CLIPS - 1)) % CLIPS
    counts = counts.at[top_clip].set(LEVELS).at[bottom_clip].set(1)
    return counts.astype(jnp.int32)


def draw_attention_master(key, part):
    key = jax.random.fold_in(key, 3)
    factors = jnp.array([1.0, 1.0, 1.0, 4.0], jnp.float32)[:, None, None] / math.sqrt(D)
    return factors * jax.random.normal(key, (4, D, D), jnp.float32)


def draw_feedforward_master(key, part):
    key = jax.random.fold_in(key, 4)
    factors = jnp.array([1.0 / math.sqrt(D), 1.0 / math.sqrt(FF)], jnp.float32)[:, None, None]
    return factors * jax.random.normal(key, (2, D, FF), jnp.float32)


def draw_scales_master(key, part):
    key = jax.random.fold_in(key, 5)
    gain_key, shift_key, layer_key = jax.random.split(key, 3)
    ramp = 0.6 + 1.2 * jnp.arange(D, dtype=jnp.float32) / (D - 1)
    rough = jax.random.uniform(gain_key, (2, D), jnp.float32, 0.8, 1.25)
    shifts = 0.3 * jax.random.normal(shift_key, (2, D), jnp.float32)
    layer_scales = jax.random.uniform(layer_key, (2, D), jnp.float32, 0.5, 1.5)
    return jnp.stack([ramp * rough[0], shifts[0], ramp * rough[1], shifts[1], layer_scales[0], layer_scales[1]])


def draw_attention_first(key, part):
    key = jax.random.fold_in(key, 11)
    return moment_draw(key, (4, D, D), common_unit(1.0))


def draw_attention_second(key, part):
    key = jax.random.fold_in(key, 12)
    return square_draw(key, (4, D, D), common_unit(1.0))


def draw_feedforward_first(key, part):
    key = jax.random.fold_in(key, 13)
    return moment_draw(key, (2, D, FF), common_unit(1.0))


def draw_feedforward_second(key, part):
    key = jax.random.fold_in(key, 14)
    return square_draw(key, (2, D, FF), common_unit(1.0))


def draw_projection_first(key, part):
    key = jax.random.fold_in(key, 15)
    return moment_draw(key, (D, LAT), common_unit(1.0))


def draw_projection_second(key, part):
    key = jax.random.fold_in(key, 16)
    return square_draw(key, (D, LAT), common_unit(1.0))


def draw_codebook_first(key, part):
    key = jax.random.fold_in(key, 17)
    return moment_draw(key, (LEVELS, BOOK, LAT), book_unit())


def draw_codebook_second(key, part):
    key = jax.random.fold_in(key, 18)
    return square_draw(key, (LEVELS, BOOK, LAT), book_unit())


def draw_scales_first(key, part):
    key = jax.random.fold_in(key, 19)
    return moment_draw(key, (6, D), common_unit(4.0))


def draw_scales_second(key, part):
    key = jax.random.fold_in(key, 20)
    return square_draw(key, (6, D), common_unit(4.0))


def block_scale(rng, dims, pieces, least, largest):
    loudness, own = 1.0, jax.random.fold_in(rng, 6)
    for axis_at, blocks in pieces:
        heights = jnp.exp(jax.random.uniform(jax.random.fold_in(own, axis_at), (blocks,), jnp.float32, least / len(pieces), largest / len(pieces)))
        loudness = loudness * jnp.repeat(heights, dims[axis_at] // blocks).reshape([-1 if axis == axis_at else 1 for axis in range(len(dims))])
    return loudness


def normal_values(stream_key, shape, deviation, limit, pieces=(), held_as=jnp.bfloat16):
    level = block_scale(stream_key, shape, pieces, -0.22, 0.18) if pieces else 1.0
    values = jax.random.normal(stream_key, shape, jnp.float32) * deviation * level
    return jnp.minimum(jnp.maximum(values, -limit), limit).astype(held_as)


def setup_inputs(seed: int = 0) -> dict:
    splits = jax.random.split(jax.random.key(seed), 19)
    inputs = normal_values(splits[0], (TOKENS, D), 1.0, 6.0, ((0, 32),))
    codes = draw_codes(jax.random.fold_in(splits[18], 71), 0)
    levels = draw_levels(jax.random.fold_in(splits[18], 71), 0)
    attention_master = draw_attention_master(jax.random.fold_in(splits[18], 71), 0)
    attention_first = draw_attention_first(jax.random.fold_in(splits[18], 71), 0)
    attention_second = draw_attention_second(jax.random.fold_in(splits[18], 71), 0)
    feedforward_master = draw_feedforward_master(jax.random.fold_in(splits[18], 71), 0)
    feedforward_first = draw_feedforward_first(jax.random.fold_in(splits[18], 71), 0)
    feedforward_second = draw_feedforward_second(jax.random.fold_in(splits[18], 71), 0)
    projection_master = normal_values(splits[9], (D, LAT), D ** -0.5, 0.25, ((0, 32),), jnp.float32)
    projection_first = draw_projection_first(jax.random.fold_in(splits[18], 71), 0)
    projection_second = draw_projection_second(jax.random.fold_in(splits[18], 71), 0)
    codebook_master = normal_values(splits[12], (LEVELS, BOOK, LAT), 0.5, 3.0, ((1, 32),), jnp.float32)
    codebook_first = draw_codebook_first(jax.random.fold_in(splits[18], 71), 0)
    codebook_second = draw_codebook_second(jax.random.fold_in(splits[18], 71), 0)
    scales_master = draw_scales_master(jax.random.fold_in(splits[18], 71), 0)
    scales_first = draw_scales_first(jax.random.fold_in(splits[18], 71), 0)
    scales_second = draw_scales_second(jax.random.fold_in(splits[18], 71), 0)
    return {"inputs": inputs, "codes": codes, "levels": levels, "attention_master": attention_master, "attention_first": attention_first, "attention_second": attention_second, "feedforward_master": feedforward_master, "feedforward_first": feedforward_first, "feedforward_second": feedforward_second, "projection_master": projection_master, "projection_first": projection_first, "projection_second": projection_second, "codebook_master": codebook_master, "codebook_first": codebook_first, "codebook_second": codebook_second, "scales_master": scales_master, "scales_first": scales_first, "scales_second": scales_second}


@jax.custom_vjp
def low(v):
    return lax.optimization_barrier(v.astype(jnp.bfloat16)).astype(jnp.float32)

@jax.custom_vjp
def low_back(v):
    return v

def low_keep(v):
    return (low(v), None)

def low_pass(kept, grad):
    return (grad,)

def back_keep(v):
    return (v, None)

def back_low(kept, grad):
    return (low(grad),)
low.defvjp(low_keep, low_pass)
low_back.defvjp(back_keep, back_low)
highest = lax.Precision.HIGHEST
clip_level = 1.0
beta_first = 0.9
beta_second = 0.95
adam_floor = 1e-08
weight_decay = 0.1
group_rates = (0.05, 0.03, 0.05, 0.5, 0.5)
masked_score = -1e+30

def product(left_side, right_side):
    return jnp.dot(left_side, right_side, precision=highest, preferred_element_type=jnp.float32)

def normalize(values, gain, shift):
    centre = lax.optimization_barrier(jnp.mean(values, axis=-1, keepdims=True))
    centred = values - centre
    spread = lax.optimization_barrier(jnp.mean(centred * centred, axis=-1, keepdims=True))
    return centred * lax.rsqrt(spread + 1e-05) * gain + shift

def rotary(values, positions, turning):
    half_depth = values.shape[-1] // 2
    freqs_table = jnp.exp(-math.log(10000.0) * jnp.arange(half_depth, dtype=jnp.float32) * 2.0 / values.shape[-1])
    angles = positions.astype(jnp.float32)[:, None] * freqs_table[None, :]
    cosine = jnp.cos(angles)[:, None, :]
    sine = turning * jnp.sin(angles)[:, None, :]
    former = values[..., :half_depth]
    latter = values[..., half_depth:]
    return jnp.concatenate([former * cosine - latter * sine, former * sine + latter * cosine], axis=-1)

def attend(queries, keyset, valueset):
    length = queries.shape[0]
    block_rows = min(512, length)
    margin = (WINDOW + 127) // 128 * 128
    key_span = block_rows + margin
    filler = jnp.zeros((margin,) + keyset.shape[1:], jnp.float32)
    keys_padded = jnp.concatenate([filler, keyset], axis=0)
    values_padded = jnp.concatenate([filler, valueset], axis=0)
    score_scale = 1.0 / math.sqrt(queries.shape[-1])
    query_place = jnp.arange(block_rows, dtype=jnp.int32)[:, None]
    key_place = jnp.arange(key_span, dtype=jnp.int32)[None, :]

    def one_block(block_start):
        query_block = lax.dynamic_slice_in_dim(queries, block_start, block_rows, 0)
        key_block = lax.dynamic_slice_in_dim(keys_padded, block_start, key_span, 0)
        value_block = lax.dynamic_slice_in_dim(values_padded, block_start, key_span, 0)
        scores = low_back(jnp.einsum('qhd,khd->hqk', query_block, key_block, precision=highest) * score_scale)
        distance = margin + query_place - key_place
        allowed = (distance >= 0) & (distance <= WINDOW) & (block_start + key_place - margin >= 0)
        scores = jnp.where(allowed[None], scores, masked_score)
        highest_score = lax.optimization_barrier(jnp.max(scores, axis=-1, keepdims=True))
        raised = jnp.exp(scores - highest_score)
        weights = low(raised / lax.optimization_barrier(jnp.sum(raised, axis=-1, keepdims=True)))
        return jnp.einsum('hqk,khd->qhd', weights, value_block, precision=highest)
    starts = jnp.arange(length // block_rows, dtype=jnp.int32) * block_rows
    output = lax.map(jax.checkpoint(one_block), starts)
    return output.reshape(queries.shape)

def clip_forward(weights, frames, clip_codes, clip_active):
    attention, feedforward, projection, codebook, scales = weights
    frame_count = frames.shape[0]
    head_shape = (frame_count, HEADS, D // HEADS)
    positions = jnp.arange(frame_count, dtype=jnp.int32)
    normed_first = low(normalize(frames, scales[0], scales[1]))
    queries = low(rotary(low_back(product(normed_first, attention[0])).reshape(head_shape), positions, 1.0))
    keyset = low(rotary(low_back(product(normed_first, attention[1])).reshape(head_shape), positions, 1.0))
    valueset = low(low_back(product(normed_first, attention[2]))).reshape(head_shape)
    mixed_heads = low(low_back(attend(queries, keyset, valueset).reshape(frame_count, D)))
    after_first = frames + scales[4] * low_back(product(mixed_heads, attention[3]))
    normed_second = low(normalize(after_first, scales[2], scales[3]))
    pre_gelu = low_back(product(normed_second, feedforward[0]))
    hidden = low(jax.nn.gelu(pre_gelu, approximate=False))
    after_second = after_first + scales[5] * low_back(product(hidden, feedforward[1].T))
    latent = low_back(product(low(after_second), projection))
    residue = latent
    energy = jnp.zeros((), jnp.float32)
    for level_index in range(LEVELS):
        factor_level = jnp.where(level_index < clip_active, 1.0, 0.0).astype(jnp.float32)
        code_rows = jnp.take(codebook[level_index], clip_codes[:, level_index], axis=0)
        residue = residue - factor_level * code_rows
        energy = energy + 0.5 * factor_level * jnp.sum(residue * residue)
    return (energy, latent)

def adam_update(master, first, second, gradient, factor, rate):
    clipped = gradient * factor
    momentum = beta_first * first + (1.0 - beta_first) * clipped
    variance = beta_second * second + (1.0 - beta_second) * clipped * clipped
    corrected = momentum / (1.0 - beta_first ** STEP)
    divisor = jnp.sqrt(variance / (1.0 - beta_second ** STEP)) + adam_floor
    updated = master - rate * (corrected / divisor + weight_decay * master)
    return (momentum, variance, updated, updated.astype(jnp.bfloat16))

def reference(inputs, codes, levels, attention_master, attention_first, attention_second, feedforward_master, feedforward_first, feedforward_second, projection_master, projection_first, projection_second, codebook_master, codebook_first, codebook_second, scales_master, scales_first, scales_second):
    masters = (attention_master, feedforward_master, projection_master, codebook_master, scales_master)
    firsts = (attention_first, feedforward_first, projection_first, codebook_first, scales_first)
    seconds = (attention_second, feedforward_second, projection_second, codebook_second, scales_second)
    frames_all = inputs.astype(jnp.float32)

    def whole(weights_master, frame_rows):
        weights = tuple((low(master) for master in weights_master))

        def per_clip(carry, operands):
            clip_rows, clip_codes, clip_active = operands
            energy, latent = jax.checkpoint(clip_forward)(weights, clip_rows, clip_codes, clip_active)
            return (carry + energy, latent)
        energy, latents = lax.scan(per_clip, jnp.zeros((), jnp.float32), (frame_rows.reshape(CLIPS, LEN, D), codes.reshape(CLIPS, LEN, LEVELS), levels))
        return (energy, latents.reshape(TOKENS, LAT))
    energy, pullback, latent = jax.vjp(whole, masters, frames_all, has_aux=True)
    gradients, input_gradient = pullback(jnp.ones((), jnp.float32))
    squares = jnp.zeros((), jnp.float32)
    for gradient in gradients:
        squares = squares + jnp.sum(gradient * gradient)
    gradient_norm = jnp.sqrt(squares)
    factor = clip_level / jnp.maximum(gradient_norm, clip_level)
    attention_new = adam_update(masters[0], firsts[0], seconds[0], gradients[0], factor, group_rates[0])
    feedforward_new = adam_update(masters[1], firsts[1], seconds[1], gradients[1], factor, group_rates[1])
    projection_new = adam_update(masters[2], firsts[2], seconds[2], gradients[2], factor, group_rates[2])
    codebook_new = adam_update(masters[3], firsts[3], seconds[3], gradients[3], factor, group_rates[3])
    scales_new = adam_update(masters[4], firsts[4], seconds[4], gradients[4], factor, group_rates[4])
    return (latent, input_gradient, gradient_norm, attention_new[0], attention_new[1], attention_new[2], attention_new[3], feedforward_new[0], feedforward_new[1], feedforward_new[2], feedforward_new[3], projection_new[0], projection_new[1], projection_new[2], projection_new[3], codebook_new[0], codebook_new[1], codebook_new[2], codebook_new[3], scales_new[0], scales_new[1], scales_new[2], scales_new[3])
```

```python
import math

import jax
import jax.numpy as jnp
import numpy as np
from jax import lax
from jax.experimental import pallas as pl
from jax.experimental.pallas import tpu as pltpu
from jax.sharding import PartitionSpec as P

HEADS = 8
LEVELS = 8
WINDOW = 250
STEP = 10
AXES = ("clip", "tm")

clip_level = 1.0
beta_first = 0.9
beta_second = 0.95
adam_floor = 1e-08
weight_decay = 0.1
group_rates = (0.05, 0.03, 0.05, 0.5, 0.5)
masked_score = -1e30

f32 = jnp.float32
bf16 = jnp.bfloat16
MARGIN = (WINDOW + 127) // 128 * 128
QROWS = 128
SPAN = QROWS + MARGIN
ROWS = 256
MIB = 1 << 20


def dot(left, right, contract=((1,), (0,))):
    return lax.dot_general(left, right, (contract, ((), ())), preferred_element_type=f32)


def dot_nt(left, right):
    return dot(left, right, ((1,), (1,)))


def flip(block):
    return block.astype(f32).T.astype(bf16)


def params(mib):
    return pltpu.CompilerParams(vmem_limit_bytes=mib * MIB)


def whole(shape):
    return pl.BlockSpec(tuple(shape), lambda *_: (0,) * len(shape))


def smem():
    return pl.BlockSpec(memory_space=pltpu.SMEM)


def cost(share, length=1):
    return pl.CostEstimate(flops=share * 500000000, bytes_accessed=length * 3 * MIB, transcendentals=0)


def after(value, *earlier):
    return lax.optimization_barrier((value, earlier))[0]


def digit_plan(count, kind):
    bits = count.bit_length() - 1
    if kind == 2:
        plan, shift = [(0, 2)], 1
    else:
        middle = [(shift, 2) for shift in range(1, min(3, bits))]
        plan, shift = [(0, 2)] + (middle[::-1] if kind % 2 else middle), 3
    while shift < bits:
        width = 1 if kind > 2 else min(2, bits - shift)
        plan.append((shift, 1 << width))
        shift += width
    return plan


def swap(block, count, mask):
    return lax.ppermute(block, AXES, [(i, i ^ mask) for i in range(count)])


def gather_swaps(block, count, kind, stage):
    shift, radix = digit_plan(count, kind)[stage]
    return [swap(block, count, k << shift) for k in range(1, radix)]


def join(block, others, axis=0):
    return jnp.concatenate([block] + list(others), axis=axis)


def place_of(device, count, kind):
    place, weight = 0, 1
    for shift, radix in reversed(digit_plan(count, kind)):
        place = place + ((device >> shift) & (radix - 1)) * weight
        weight *= radix
    return place


def device_of_places(count, kind):
    table = np.zeros(count, np.int32)
    for device in range(count):
        table[place_of(device, count, kind)] = device
    return table


def swap_parts(parts, count, kind, stage):
    shift, _ = digit_plan(count, kind)[stage]
    return [swap(part, count, (k + 1) << shift) for k, part in enumerate(parts)]


def reduce_add(keep, parts):
    total = keep.astype(f32)
    for part in parts:
        total = total + part.astype(f32)
    return total


def split_kernel(radix, *refs):
    outs, operands = refs[-radix:], refs[:-radix]
    total = operands[0][...].astype(f32)
    for operand in operands[1:]:
        total = total + operand[...].astype(f32)
    size = total.shape[1] // radix
    for k, out in enumerate(outs):
        out[...] = total[:, k * size : (k + 1) * size, :].astype(out.dtype)


def reduce_split(keep, parts, count, kind, stage):
    _, radix = digit_plan(count, kind)[stage]
    lead, rows, columns = keep.shape
    size = rows // radix
    if lead > 1:
        steps, block, index = lead, (1, rows, columns), lambda i: (i, 0, 0)
    else:
        steps = 2 if columns % 256 == 0 else 1
        block, index = (1, rows, columns // steps), lambda i: (0, 0, i)
    shares = (block[0], size, block[2])
    kinds = [f32] + [bf16] * (radix - 1)
    outs = pl.pallas_call(
        lambda *refs: split_kernel(radix, *refs),
        grid=(steps,),
        in_specs=[pl.BlockSpec(block, index)] * (1 + len(parts)),
        out_specs=[pl.BlockSpec(shares, index)] * radix,
        out_shape=[jax.ShapeDtypeStruct((lead, size, columns), kind) for kind in kinds],
        compiler_params=params(32),
        cost_estimate=cost(0, 1),
        name="split_sums",
    )(keep, *parts)
    return outs[0], swap_parts(outs[1:], count, kind, stage)


def merge_kernel(axis, radix, groups, *refs):
    outs = refs[-radix:]
    base = left = 0
    for size in groups:
        total = refs[base][...].astype(f32)
        for operand in refs[base + 1 : base + size]:
            total = total + operand[...].astype(f32)
        base += size
        rows = total.shape[1] // radix
        for k, out in enumerate(outs):
            share = total[:, k * rows : (k + 1) * rows, :].astype(out.dtype)
            if axis == 0:
                out[left : left + total.shape[0]] = share
            else:
                out[:, :, left : left + total.shape[2]] = share
        left += total.shape[axis]


def merge_split(groups, axis, count, kind, stage, share=0):
    _, radix = digit_plan(count, kind)[stage]
    operands = [array for keep, parts in groups for array in (keep, *parts)]
    shape = list(groups[0][0].shape)
    shape[axis] = sum(keep.shape[axis] for keep, _ in groups)
    shape[1] //= radix
    sizes = [1 + len(parts) for _, parts in groups]
    kinds = [f32] + [bf16] * (radix - 1)
    outs = pl.pallas_call(
        lambda *refs: merge_kernel(axis, radix, sizes, *refs),
        grid=(1,),
        in_specs=[whole(operand.shape) for operand in operands],
        out_specs=[whole(shape)] * radix,
        out_shape=[jax.ShapeDtypeStruct(shape, kind) for kind in kinds],
        compiler_params=params(32),
        cost_estimate=cost(share, 1),
        name="split_sums",
    )(*operands)
    return outs[0], swap_parts(outs[1:], count, kind, stage)


def one_hot_rows(rowmap, size):
    place = lax.broadcasted_iota(jnp.int32, (size, size), 0)
    return jnp.where(place == rowmap, 1.0, 0.0).astype(bf16)


def unpack_rows(starts_ref, rowmap_ref, pieces, out_ref):
    half = pieces[0].shape[0]
    count = starts_ref.shape[0]
    rows = 2 * half // count
    if rows % 16 == 0:
        for place in range(count):
            piece = pieces[place * rows // half]
            inner = place * rows % half
            start = pl.multiple_of(starts_ref[place], rows)
            out_ref[pl.ds(start, rows), :] = piece[inner : inner + rows, :]
    else:
        spread = one_hot_rows(rowmap_ref[0:1, :], 2 * half)
        columns = out_ref.shape[1]
        for left in range(0, columns, 128):
            joined = jnp.concatenate([p[:, left : left + 128] for p in pieces], axis=0)
            out_ref[:, left : left + 128] = dot(spread, joined).astype(bf16)


def pack_rows(starts_ref, rowmap_ref, work_ref, outs):
    size, columns = work_ref.shape
    half = size // 2
    count = starts_ref.shape[0]
    rows = size // count
    if rows % 16 == 0:
        for place in range(count):
            start = pl.multiple_of(starts_ref[place], rows)
            out, inner = outs[place * rows // half], place * rows % half
            out[0, inner : inner + rows, :] = work_ref[pl.ds(start, rows), :]
    else:
        spread = one_hot_rows(rowmap_ref[0:1, :], size)
        for left in range(0, columns, 128):
            lanes = slice(left, left + 128)
            joined = dot(spread, work_ref[:, lanes], ((0,), (0,))).astype(bf16)
            for index, out in enumerate(outs):
                out[0, :, lanes] = joined[index * half : (index + 1) * half]


def centre_rows(values):
    centred = values - jnp.mean(values, axis=-1, keepdims=True)
    spread = jnp.mean(centred * centred, axis=-1, keepdims=True)
    rstd = lax.rsqrt(spread + 1e-05)
    return centred * rstd, rstd


def norm_back(normal, rstd, gain, grad):
    inner = grad * gain
    first = jnp.mean(inner, axis=-1, keepdims=True)
    second = jnp.mean(inner * normal, axis=-1, keepdims=True)
    return rstd * (inner - first - normal * second)


def column_sum(values):
    return jnp.sum(values, axis=0, keepdims=True)


def turn(values, cosine, sine):
    lanes = values.shape[1]
    ahead = pltpu.roll(values, lanes - 32, 1)
    behind = pltpu.roll(values, 32, 1)
    lane = lax.broadcasted_iota(jnp.int32, values.shape, 1)
    partner = jnp.where(lane % 64 < 32, ahead, behind)
    repeats = lanes // cosine.shape[1]
    if repeats > 1:
        cosine = jnp.concatenate([cosine] * repeats, axis=1)
        sine = jnp.concatenate([sine] * repeats, axis=1)
    return values * cosine + partner * sine


def head_columns(flipped):
    zero = jnp.zeros((64, flipped.shape[1]), flipped.dtype)
    return jnp.concatenate(
        [
            jnp.concatenate([flipped[:64], zero], axis=1),
            jnp.concatenate([zero, flipped[64:]], axis=1),
        ],
        axis=0,
    )


def head_rows(block):
    lane = lax.broadcasted_iota(jnp.int32, block.shape, 1)
    zero = jnp.zeros_like(block)
    return jnp.concatenate(
        [jnp.where(lane < 64, block, zero), jnp.where(lane < 64, zero, block)], axis=0
    )


def qkv_kernel(
    starts, rowmap, halo, inputs, piece_a, piece_b, cosine, sine, normed, q, k, v, scales, weights
):
    step = pl.program_id(0)
    width = inputs.shape[1]

    @pl.when(step == 0)
    def _():
        unpack_rows(starts, rowmap, (piece_a, piece_b), weights)
        scales[...] = weights[:, 3 * width :].astype(f32).T[:8]

    frames = jnp.where(step == 0, halo[...].astype(f32), inputs[...].astype(f32))
    normal, _ = centre_rows(frames)
    low = (normal * scales[0:1, :] + scales[1:2, :]).astype(bf16)
    normed[...] = low
    turned = turn(dot(low, weights[:, :width]), cosine[...], sine[...])
    q[...] = (turned.astype(bf16).astype(f32) * 0.125).astype(bf16)
    k[...] = turn(dot(low, weights[:, width : 2 * width]), cosine[...], sine[...]).astype(bf16)
    v[...] = dot(low, weights[:, 2 * width : 3 * width]).astype(bf16)


def qkv_call(starts, rowmap, halo, inputs, pieces, cosine, sine):
    count, width = inputs.shape
    columns = pieces[0].shape[1]
    steps = count // ROWS + 1
    late = lambda i: (jnp.maximum(i - 1, 0), 0)
    here = lambda i: (i, 0)
    return pl.pallas_call(
        qkv_kernel,
        grid=(steps,),
        in_specs=[
            smem(),
            whole(rowmap.shape),
            whole(halo.shape),
            pl.BlockSpec((ROWS, width), late),
            whole(pieces[0].shape),
            whole(pieces[1].shape),
            pl.BlockSpec((ROWS, 128), here),
            pl.BlockSpec((ROWS, 128), here),
        ],
        out_specs=[
            pl.BlockSpec((ROWS, width), late),
            pl.BlockSpec((ROWS, width), late),
            pl.BlockSpec((ROWS, width), here),
            pl.BlockSpec((ROWS, width), here),
            whole((8, width)),
            whole((width, columns)),
        ],
        out_shape=[
            jax.ShapeDtypeStruct((count, width), bf16),
            jax.ShapeDtypeStruct((count, width), bf16),
            jax.ShapeDtypeStruct((count + MARGIN, width), bf16),
            jax.ShapeDtypeStruct((count + MARGIN, width), bf16),
            jax.ShapeDtypeStruct((8, width), f32),
            jax.ShapeDtypeStruct((width, columns), bf16),
        ],
        compiler_params=params(48),
        cost_estimate=cost(4, 8),
        name="project_rows",
    )(starts, rowmap, halo, inputs, *pieces, cosine, sine)


def attend_kernel(q, k, v, bias, mixed, logsum, v_flipped):
    step = pl.program_id(0)
    pairs = q.shape[1] // 128

    @pl.when(step == 0)
    def _():
        for pair in range(pairs):
            lanes = slice(pair * 128, (pair + 1) * 128)
            v_flipped[lanes, :] = flip(v[:, lanes])

    start = pl.multiple_of(step * QROWS, QROWS)
    allowed = jnp.concatenate([bias[0], bias[0]], axis=1)
    rows = []
    for pair in range(pairs):
        lanes = slice(pair * 128, (pair + 1) * 128)
        columns = head_columns(flip(q[:, lanes]))
        scores = dot(k[pl.ds(start, SPAN), lanes], columns) + allowed
        highest = jnp.max(scores, axis=0, keepdims=True)
        raised = jnp.exp(scores - highest)
        total = column_sum(raised)
        joined = dot(v_flipped[lanes, pl.ds(start, SPAN)], raised.astype(bf16))
        joined = joined * (1.0 / total)
        output = jnp.concatenate([joined[:64, :QROWS], joined[64:, QROWS:]], axis=0)
        mixed[:, lanes] = output.T.astype(bf16)
        record = highest + jnp.log(total)
        rows += [record[:, :QROWS], record[:, QROWS:]]
    logsum[...] = jnp.concatenate(rows, axis=0)


def attend_call(q, k, v, bias):
    count, width = q.shape
    return pl.pallas_call(
        attend_kernel,
        grid=(count // QROWS,),
        in_specs=[
            pl.BlockSpec((QROWS, width), lambda i: (i, 0)),
            whole(k.shape),
            whole(v.shape),
            pl.BlockSpec((1, SPAN, QROWS), lambda i: (i, 0, 0)),
        ],
        out_specs=[
            pl.BlockSpec((QROWS, width), lambda i: (i, 0)),
            pl.BlockSpec((HEADS, QROWS), lambda i: (0, i)),
        ],
        out_shape=[
            jax.ShapeDtypeStruct((count, width), bf16),
            jax.ShapeDtypeStruct((HEADS, count), f32),
        ],
        scratch_shapes=[pltpu.VMEM((width, k.shape[0]), bf16)],
        compiler_params=params(40),
        cost_estimate=cost(4, 14),
        name="attend_rows",
    )(q, k, v, bias)


def forward_kernel(
    starts_a, rowmap_a, starts_b, rowmap_b, inputs, mixed, scales, own_a, other_a, own_b, other_b,
    branch_first, after_first, normed, hidden, slope, branch_second, low_out, latent, weights,
):
    step = pl.program_id(0)
    width = inputs.shape[1]
    units = hidden.shape[1]

    @pl.when(step == 0)
    def _():
        unpack_rows(starts_a, rowmap_a, (own_a, other_a), weights.at[:, :units])
        unpack_rows(starts_b, rowmap_b, (own_b, other_b), weights.at[:, units:])

    up, down = 0, units
    proj = 2 * units
    last = proj + latent.shape[1]
    first = dot(mixed[...], weights[:, last : last + width])
    branch_first[...] = first
    after = inputs[...].astype(f32) + scales[4:5, :] * first
    after_first[...] = after
    normal, _ = centre_rows(after)
    low = (normal * scales[2:3, :] + scales[3:4, :]).astype(bf16)
    normed[...] = low
    second = jnp.zeros(after.shape, f32)
    chunk = 512
    for left in range(0, units, chunk):
        pre = dot(low, weights[:, up + left : up + left + chunk])
        share = 0.5 + 0.5 * lax.erf(pre * (1.0 / math.sqrt(2.0)))
        bell = jnp.exp(-0.5 * pre * pre) * (1.0 / math.sqrt(2.0 * math.pi))
        part = (pre * share).astype(bf16)
        hidden[:, left : left + chunk] = part
        slope[:, left : left + chunk] = (share + pre * bell).astype(bf16)
        second = second + dot_nt(part, weights[:, down + left : down + left + chunk])
    branch_second[...] = second
    rounded = (after + scales[5:6, :] * second).astype(bf16)
    low_out[...] = rounded
    latent[...] = dot(rounded, weights[:, proj:last])


def forward_call(orders, inputs, mixed, scales, pieces, units, depth):
    count, width = inputs.shape
    columns = pieces[0].shape[1] + pieces[2].shape[1]
    row = lambda size: pl.BlockSpec((ROWS, size), lambda i: (i, 0))
    kept = ((width, f32), (width, f32), (width, bf16), (units, bf16), (units, bf16),
            (width, f32), (width, bf16), (depth, f32))
    (starts_a, rowmap_a), (starts_b, rowmap_b) = orders
    return pl.pallas_call(
        forward_kernel,
        grid=(count // ROWS,),
        in_specs=[smem(), whole(rowmap_a.shape)] * 2
        + [row(width), row(width), whole(scales.shape)]
        + [whole(piece.shape) for piece in pieces],
        out_specs=[row(size) for size, _ in kept] + [whole((width, columns))],
        out_shape=[jax.ShapeDtypeStruct((count, size), kind) for size, kind in kept]
        + [jax.ShapeDtypeStruct((width, columns), bf16)],
        compiler_params=params(56),
        cost_estimate=cost(4, 17),
        name="feed_rows",
    )(starts_a, rowmap_a, starts_b, rowmap_b, inputs, mixed, scales, *pieces)


def fetch_kernel(active, codes, latent, book, carried, residue, steps):
    level = pl.program_id(0)
    count, depth = latent.shape
    tiles = book.shape[1] // 256

    @pl.when(level == 0)
    def _():
        residue[...] = latent[...]

    factor = jnp.where(level < active[0], 1.0, 0.0).astype(f32)
    lane = lax.broadcasted_iota(jnp.int32, (ROWS, LEVELS), 1)
    place = lax.broadcasted_iota(jnp.int32, (ROWS, 256), 1).astype(f32)
    for top in range(0, count, ROWS):
        rows = slice(top, top + ROWS)
        code = jnp.where(lane == level, codes[rows, :].astype(f32), 0.0)
        code = jnp.sum(code, axis=1, keepdims=True)
        high = jnp.floor(code * (1.0 / 256.0))
        hit = jnp.where(place == code - 256.0 * high, 1.0, 0.0).astype(bf16)
        picks = [hit * jnp.where(high == j, 1.0, 0.0).astype(bf16) for j in range(tiles)]
        found = dot(jnp.concatenate(picks, axis=1), book[0])
        left = residue[rows, :] - factor * found
        residue[rows, :] = left
        steps[level, rows, :] = factor * left

    @pl.when(level == LEVELS - 1)
    def _():
        for top in range(0, count, ROWS):
            rows = slice(top, top + ROWS)
            total = jnp.zeros((ROWS, depth), f32)
            for index in reversed(range(LEVELS)):
                total = total + steps[index, rows, :]
                live = jnp.where(index < active[0], 1.0, 0.0).astype(f32)
                carried[index, rows, :] = (live * total).astype(bf16)


def fetch_call(active, codes, latent, book):
    count, depth = latent.shape
    entries = book.shape[1]
    return pl.pallas_call(
        fetch_kernel,
        grid=(LEVELS,),
        in_specs=[
            smem(),
            whole(codes.shape),
            whole(latent.shape),
            pl.BlockSpec((1, entries, depth), lambda i: (i, 0, 0)),
        ],
        out_specs=whole((LEVELS, count, depth)),
        out_shape=jax.ShapeDtypeStruct((LEVELS, count, depth), bf16),
        scratch_shapes=[
            pltpu.VMEM((count, depth), f32),
            pltpu.VMEM((LEVELS, count, depth), f32),
        ],
        compiler_params=params(48),
        cost_estimate=cost(4, 13),
        name="fetch_codes",
    )(active, codes, latent, book)


def spread_kernel(first, codes, carried, keep, send):
    level = pl.program_id(0) + first
    count = carried.shape[1]
    half = keep.shape[1]
    code = codes[pl.ds(level, 1), :]
    high = code >> 8
    place = lax.broadcasted_iota(jnp.int32, (256, count), 0)
    hit = jnp.where(place == (code & 255), -1.0, 0.0).astype(bf16)
    for j in range(2 * half // 256):
        pick = hit * jnp.where(high == j, 1.0, 0.0).astype(bf16)
        out, inner = (keep, send)[j * 256 // half], j * 256 % half
        out[0, inner : inner + 256, :] = dot(pick, carried[0]).astype(bf16)


def spread_call(first, levels, codes, carried, entries):
    _, count, depth = carried.shape
    half = entries // 2
    return pl.pallas_call(
        lambda *refs: spread_kernel(first, *refs),
        grid=(levels,),
        in_specs=[
            whole(codes.shape),
            pl.BlockSpec((1, count, depth), lambda i: (i + first, 0, 0)),
        ],
        out_specs=[pl.BlockSpec((1, half, depth), lambda i: (i, 0, 0))] * 2,
        out_shape=[jax.ShapeDtypeStruct((levels, half, depth), bf16)] * 2,
        compiler_params=params(32),
        cost_estimate=cost(1, 5),
        name="spread_codes",
    )(codes, carried)


def backward_kernel(
    carried, branch_second, slope, after_first, branch_first, scales, weights,
    out_second, out_pre, out_after, out_first, out_mixed, sums,
):
    step = pl.program_id(0)
    width = after_first.shape[1]
    units = slope.shape[1]
    proj = 2 * units
    last = proj + carried.shape[2]

    @pl.when(step == 0)
    def _():
        sums[...] = jnp.zeros(sums.shape, f32)

    grad_after = dot_nt(carried[0], weights[:, proj:last])
    sums[5:6, :] += column_sum(grad_after * branch_second[...])
    low = (grad_after * scales[5:6, :]).astype(bf16)
    out_second[...] = low
    grad_normed = jnp.zeros(grad_after.shape, f32)
    chunk = 512
    for left in range(0, units, chunk):
        grad_hidden = dot(low, weights[:, units + left : units + left + chunk])
        part = (grad_hidden * slope[:, left : left + chunk].astype(f32)).astype(bf16)
        out_pre[:, left : left + chunk] = part
        grad_normed = grad_normed + dot_nt(part, weights[:, left : left + chunk])
    normal, rstd = centre_rows(after_first[...])
    sums[2:3, :] += column_sum(grad_normed * normal)
    sums[3:4, :] += column_sum(grad_normed)
    grad_first = grad_after + norm_back(normal, rstd, scales[2:3, :], grad_normed)
    out_after[...] = grad_first
    sums[4:5, :] += column_sum(grad_first * branch_first[...])
    low_first = (grad_first * scales[4:5, :]).astype(bf16)
    out_first[...] = low_first
    out_mixed[...] = dot_nt(low_first, weights[:, last : last + width]).astype(bf16)


def backward_call(carried, branch_second, slope, after_first, branch_first, scales, weights):
    count, width = after_first.shape
    units, depth = slope.shape[1], carried.shape[2]
    row = lambda size: pl.BlockSpec((ROWS, size), lambda i: (i, 0))
    kept = ((width, bf16), (units, bf16), (width, f32), (width, bf16), (width, bf16))
    return pl.pallas_call(
        backward_kernel,
        grid=(count // ROWS,),
        in_specs=[
            pl.BlockSpec((1, ROWS, depth), lambda i: (0, i, 0)),
            row(width),
            row(units),
            row(width),
            row(width),
            whole(scales.shape),
            whole(weights.shape),
        ],
        out_specs=[row(size) for size, _ in kept] + [whole((8, width))],
        out_shape=[jax.ShapeDtypeStruct((count, size), kind) for size, kind in kept]
        + [jax.ShapeDtypeStruct((8, width), f32)],
        compiler_params=params(48),
        cost_estimate=cost(1, 13),
        name="feed_back",
    )(carried, branch_second, slope, after_first, branch_first, scales, weights)


def weight_kernel(
    starts_a, rowmap_a, starts_b, rowmap_b,
    normed, grad_pre, grad_second, hidden, low_out, carried, mixed, grad_first,
    keep_a, send_a, keep_b, send_b, work,
):
    units = hidden.shape[1]
    proj = 2 * units
    last = proj + carried.shape[2]
    chunk = 512
    for left_ref, right_ref, base in ((normed, grad_pre, 0), (grad_second, hidden, units)):
        flipped = flip(left_ref[...])
        for left in range(0, units, chunk):
            work[:, base + left : base + left + chunk] = dot(
                flipped, right_ref[:, left : left + chunk]
            ).astype(bf16)
    work[:, proj:last] = dot(flip(low_out[...]), carried[0]).astype(bf16)
    work[:, last:] = dot(flip(mixed[...]), grad_first[...]).astype(bf16)
    half = keep_a.shape[2]
    pack_rows(starts_a, rowmap_a, work.at[:, :half], (keep_a, send_a))
    pack_rows(starts_b, rowmap_b, work.at[:, half:], (keep_b, send_b))


def weight_call(
    orders, normed, grad_pre, grad_second, hidden, low_out, carried, mixed, grad_first
):
    count, width = normed.shape
    depth = carried.shape[2]
    columns = 2 * hidden.shape[1] + depth + width
    operands = (normed, grad_pre, grad_second, hidden, low_out)
    (starts_a, rowmap_a), (starts_b, rowmap_b) = orders
    piece = (1, width // 2, columns // 2)
    return pl.pallas_call(
        weight_kernel,
        grid=(1,),
        in_specs=[smem(), whole(rowmap_a.shape)] * 2
        + [whole(operand.shape) for operand in operands]
        + [whole((1, count, depth)), whole(mixed.shape), whole(grad_first.shape)],
        out_specs=[whole(piece)] * 4,
        out_shape=[jax.ShapeDtypeStruct(piece, bf16)] * 4,
        scratch_shapes=[pltpu.VMEM((width, columns), bf16)],
        compiler_params=params(58),
        cost_estimate=cost(1, 13),
        name="weight_sums",
    )(starts_a, rowmap_a, starts_b, rowmap_b, *operands, carried, mixed, grad_first)


def attend_back_kernel(
    offset, q, k, v, grad, logsum, bias, cosine, sine, start_k, start_v,
    grad_q, grad_k, grad_v, halo, k_flipped,
):
    step = pl.program_id(0)
    pairs = q.shape[1] // 128

    @pl.when(step == 0)
    def _():
        for pair in range(pairs):
            lanes = slice(pair * 128, (pair + 1) * 128)
            k_flipped[lanes, :] = flip(k[:, lanes])
        grad_k[:MARGIN, :] = start_k[...]
        grad_v[:MARGIN, :] = start_v[...]
        grad_k[MARGIN:, :] = jnp.zeros_like(grad_k[MARGIN:, :])
        grad_v[MARGIN:, :] = jnp.zeros_like(grad_v[MARGIN:, :])

    start = pl.multiple_of((step + offset) * QROWS, QROWS)
    own = pl.multiple_of(step * QROWS, QROWS)
    allowed = jnp.concatenate([bias[0], bias[0]], axis=1)
    back = -sine[...]
    for pair in range(pairs):
        lanes = slice(pair * 128, (pair + 1) * 128)
        heads = (2 * pair, 2 * pair + 1)
        record = jnp.concatenate([logsum[h : h + 1, :] for h in heads], axis=1)
        scores = dot(k[pl.ds(start, SPAN), lanes], head_columns(flip(q[:, lanes]))) + allowed
        weights = jnp.exp(scores - record)
        grad_weights = dot(v[pl.ds(start, SPAN), lanes], head_columns(flip(grad[:, lanes])))
        product = weights * grad_weights
        inner = column_sum(product)
        grad_scores = (product - weights * inner).astype(bf16)
        grad_v[pl.ds(own, SPAN), lanes] += dot(weights.astype(bf16), head_rows(grad[:, lanes]))
        grad_k[pl.ds(own, SPAN), lanes] += dot(grad_scores, head_rows(q[:, lanes]))
        joined = dot(k_flipped[lanes, pl.ds(start, SPAN)], grad_scores)
        flat = jnp.concatenate([joined[:64, :QROWS], joined[64:, QROWS:]], axis=0).T * 0.125
        grad_q[:, lanes] = turn(flat, cosine[...], back).astype(bf16)

    @pl.when(step == pl.num_programs(0) - 1)
    def _():
        halo[:MARGIN, :] = grad_k[:MARGIN, :].astype(bf16)
        halo[MARGIN:, :] = grad_v[:MARGIN, :].astype(bf16)


def attend_back_call(offset, blocks, q, k, v, grad, logsum, bias, cosine, sine, start_k, start_v):
    width = q.shape[1]
    keys = blocks * QROWS + MARGIN
    lead = MARGIN // QROWS
    there = lambda i: (i + offset, 0)
    table = lambda i: (i + offset + lead, 0)
    return pl.pallas_call(
        lambda *refs: attend_back_kernel(offset, *refs),
        grid=(blocks,),
        in_specs=[
            pl.BlockSpec((QROWS, width), there),
            whole(k.shape),
            whole(v.shape),
            pl.BlockSpec((QROWS, width), there),
            pl.BlockSpec((HEADS, QROWS), lambda i: (0, i + offset)),
            pl.BlockSpec((1, SPAN, QROWS), lambda i: (i + offset, 0, 0)),
            pl.BlockSpec((QROWS, 128), table),
            pl.BlockSpec((QROWS, 128), table),
            pl.BlockSpec((MARGIN, width), lambda i: (start_k.shape[0] // MARGIN - 1, 0)),
            pl.BlockSpec((MARGIN, width), lambda i: (start_v.shape[0] // MARGIN - 1, 0)),
        ],
        out_specs=[
            pl.BlockSpec((QROWS, width), lambda i: (i, 0)),
            whole((keys, width)),
            whole((keys, width)),
            whole((2 * MARGIN, width)),
        ],
        out_shape=[
            jax.ShapeDtypeStruct((blocks * QROWS, width), bf16),
            jax.ShapeDtypeStruct((keys, width), f32),
            jax.ShapeDtypeStruct((keys, width), f32),
            jax.ShapeDtypeStruct((2 * MARGIN, width), bf16),
        ],
        scratch_shapes=[pltpu.VMEM((width, k.shape[0]), bf16)],
        compiler_params=params(48),
        cost_estimate=cost(1 if offset == MARGIN // QROWS else 8, 2 * blocks),
        name="attend_back",
    )(q, k, v, grad, logsum, bias, cosine, sine, start_k, start_v)


def finish_kernel(
    starts, rowmap, inputs, normed, q_a, q_b, q_c, k_a, k_b, v_a, v_b, halo, cosine, sine,
    grad_after, scales, sums_second, weights,
    out, keep, send, work, turned_q, turned_k, turned_v, sums,
):
    step = pl.program_id(0)
    last = pl.num_programs(0) - 1
    count, width = normed.shape

    @pl.when(step == 0)
    def _():
        sums[...] = jnp.zeros(sums.shape, f32)
        sums[:8, :] = sums_second[...]
        left = 0
        for piece in (q_a, q_b, q_c):
            turned_q[left : left + piece.shape[0], :] = piece[...]
            left += piece.shape[0]

    rows = pl.ds(pl.multiple_of(step * ROWS, ROWS), ROWS)
    near = jnp.where(step == last, 1.0, 0.0).astype(f32)
    part_k = jnp.where(step == 0, k_a[...], k_b[...]) + near * halo[:MARGIN, :].astype(f32)
    part_v = jnp.where(step == 0, v_a[...], v_b[...]) + near * halo[MARGIN:, :].astype(f32)
    turned = turn(part_k, cosine[...], -sine[...]).astype(bf16)
    turned_k[rows, :] = turned
    value = part_v.astype(bf16)
    turned_v[rows, :] = value
    grad = dot_nt(turned_q[rows, :], weights[:, :width])
    grad = grad + dot_nt(turned, weights[:, width : 2 * width])
    grad = grad + dot_nt(value, weights[:, 2 * width : 3 * width])
    normal, rstd = centre_rows(inputs[...].astype(f32))
    sums[0:1, :] += column_sum(grad * normal)
    sums[1:2, :] += column_sum(grad)
    out[...] = grad_after[...] + norm_back(normal, rstd, scales[0:1, :], grad)

    @pl.when(step == last)
    def _():
        flipped = flip(normed[...])
        for index, turned_ref in enumerate((turned_q, turned_k, turned_v)):
            lanes = slice(index * width, (index + 1) * width)
            work[:, lanes] = dot(flipped, turned_ref[...]).astype(bf16)
        work[:, 3 * width :] = sums[...].T.astype(bf16)
        pack_rows(starts, rowmap, work, (keep, send))


def finish_call(
    starts, rowmap, inputs, normed, grad_q, grad_k, grad_v, halo, cosine, sine,
    grad_after, scales, sums_second, weights,
):
    count, width = normed.shape
    columns = 3 * width + 128
    row = pl.BlockSpec((ROWS, width), lambda i: (i, 0))
    first = pl.BlockSpec((ROWS, width), lambda i: (0, 0))
    rest = pl.BlockSpec((ROWS, width), lambda i: (jnp.maximum(i - 1, 0), 0))
    table = pl.BlockSpec((ROWS, 128), lambda i: (i + MARGIN // ROWS, 0))
    shapes = [jax.ShapeDtypeStruct((count, width), f32)] + [
        jax.ShapeDtypeStruct((1, width // 2, columns), bf16)
    ] * 2
    return pl.pallas_call(
        finish_kernel,
        grid=(count // ROWS,),
        in_specs=[smem(), whole(rowmap.shape), row, whole(normed.shape)]
        + [whole(piece.shape) for piece in grad_q]
        + [first, rest, first, rest]
        + [whole(halo.shape), table, table, row]
        + [whole(scales.shape), whole(sums_second.shape), whole(weights.shape)],
        out_specs=[row, whole(shapes[1].shape), whole(shapes[2].shape)],
        out_shape=shapes,
        scratch_shapes=[
            pltpu.VMEM((width, columns), bf16),
            pltpu.VMEM((count, width), bf16),
            pltpu.VMEM((count, width), bf16),
            pltpu.VMEM((count, width), bf16),
            pltpu.VMEM((128, width), f32),
        ],
        compiler_params=params(48),
        cost_estimate=cost(0, 10),
        name="finish_rows",
    )(
        starts, rowmap, inputs, normed, *grad_q, *grad_k, *grad_v, halo, cosine, sine,
        grad_after, scales, sums_second, weights,
    )


def adam_update(master, first, second, gradient, factor, rate):
    clipped = gradient * factor
    momentum = beta_first * first + (1.0 - beta_first) * clipped
    variance = beta_second * second + (1.0 - beta_second) * clipped * clipped
    corrected = momentum / (1.0 - beta_first**STEP)
    divisor = jnp.sqrt(variance / (1.0 - beta_second**STEP)) + adam_floor
    updated = master - rate * (corrected / divisor + weight_decay * master)
    return (momentum, variance, updated, updated.astype(bf16))


def adam_kernel(factor_ref, grad_feed, grad_qkv, grad_book, *refs):
    factor = factor_ref[0]
    masters, firsts, seconds = refs[0:15:3], refs[1:15:3], refs[2:15:3]
    outs = [refs[15 + 4 * group : 19 + 4 * group] for group in range(5)]

    def update(group, index, gradient):
        results = adam_update(
            masters[group][index], firsts[group][index], seconds[group][index],
            gradient, factor, group_rates[group],
        )
        for out, result in zip(outs[group], results):
            out[index] = result

    width = (grad_qkv.shape[1] - 128) // 3
    units = masters[1].shape[2]
    depth = masters[2].shape[1]
    for k in range(3):
        update(0, k, grad_qkv[:, k * width : (k + 1) * width])
    update(0, 3, grad_feed[:, 2 * units + depth :])
    for k in range(2):
        update(1, k, grad_feed[:, k * units : (k + 1) * units])
    update(2, Ellipsis, grad_feed[:, 2 * units : 2 * units + depth])
    for level in range(LEVELS):
        update(3, level, grad_book[level])
    update(4, Ellipsis, grad_qkv[:, 3 * width :].T[:6])


def adam_call(factor, gradients, states):
    operands = list(gradients) + [array for group in states for array in group]
    shapes = [
        jax.ShapeDtypeStruct(group[0].shape, kind)
        for group in states
        for kind in (f32, f32, f32, bf16)
    ]
    return pl.pallas_call(
        adam_kernel,
        grid=(1,),
        in_specs=[smem()] + [whole(operand.shape) for operand in operands],
        out_specs=[whole(shape.shape) for shape in shapes],
        out_shape=shapes,
        compiler_params=params(40),
        cost_estimate=cost(3, 2),
        name="adam_step",
    )(factor, *operands)


def turn_tables(positions, depth):
    half = depth // 2
    freqs = jnp.exp(-math.log(10000.0) * jnp.arange(half, dtype=f32) * 2.0 / depth)
    angles = positions.astype(f32)[:, None] * freqs[None, :]
    cosine, sine = jnp.cos(angles), jnp.sin(angles)
    return (
        jnp.concatenate([cosine] * 4, axis=1),
        jnp.concatenate([-sine, sine, -sine, sine], axis=1),
    )


def score_bias(count, offset):
    block = jnp.arange(count // QROWS, dtype=jnp.int32)[:, None, None]
    key_place = jnp.arange(SPAN, dtype=jnp.int32)[None, :, None]
    query_place = jnp.arange(QROWS, dtype=jnp.int32)[None, None, :]
    distance = MARGIN + query_place - key_place
    reach = offset + block * QROWS + key_place - MARGIN
    allowed = (distance >= 0) & (distance <= WINDOW) & (reach >= 0)
    return jnp.where(allowed, 0.0, masked_score).astype(f32)


def body(
    inputs, codes, levels,
    attention_master, attention_first, attention_second,
    feedforward_master, feedforward_first, feedforward_second,
    projection_master, projection_first, projection_second,
    codebook_master, codebook_first, codebook_second,
    scales_master, scales_first, scales_second,
):
    spans = lax.axis_size("tm")
    devices = lax.axis_size("clip") * spans
    me = lax.axis_index("clip") * spans + lax.axis_index("tm")
    frame_count, width = inputs.shape
    units = feedforward_master.shape[2]
    depth = projection_master.shape[1]
    rows = projection_master.shape[0]
    entries = codebook_master.shape[1] * devices

    early = jnp.concatenate(
        [
            attention_master[0],
            attention_master[1],
            attention_master[2],
            jnp.pad(scales_master.T, ((0, 0), (0, 128 - scales_master.shape[0]))),
        ],
        axis=1,
    ).astype(bf16)
    feed = jnp.concatenate(
        [feedforward_master[0], feedforward_master[1], projection_master, attention_master[3]],
        axis=1,
    ).astype(bf16)
    mid = LEVELS // 2
    book = lax.all_gather(codebook_master.astype(bf16), AXES, axis=1, tiled=True)
    stages = len(digit_plan(devices, 4))
    halo = lax.ppermute(
        inputs[frame_count - MARGIN :], "tm", [(i, i + 1) for i in range(spans - 1)]
    )
    for stage in reversed(range(2, len(digit_plan(devices, 2)))):
        early = join(early, gather_swaps(early, devices, 2, stage))
    for stage in reversed(range(4, stages)):
        feed = join(feed, after(gather_swaps(feed, devices, 4, stage), early))
    early = join(early, gather_swaps(early, devices, 2, 1))
    come = after(gather_swaps(feed, devices, 4, 3), early)
    early_pieces = (early, swap(early, devices, 1))
    feed_a = join(feed[:, :units], [part[:, :units] for part in come])
    feed_b = join(feed[:, units:], [part[:, units:] for part in come])
    come_a = gather_swaps(feed_a, devices, 4, 2)
    come_b = gather_swaps(feed_b, devices, 5, 2)

    def order(kind):
        owners = jnp.asarray(device_of_places(devices, kind)) ^ me
        starts = (owners * rows).astype(jnp.int32)
        rowmap = (starts[:, None] + jnp.arange(rows, dtype=jnp.int32)[None, :]).reshape(1, width)
        return starts, jnp.broadcast_to(rowmap, (8, width))

    orders = [order(kind) for kind in range(6)]
    offset = lax.axis_index("tm") * frame_count
    positions = offset - MARGIN + jnp.arange(frame_count + MARGIN, dtype=jnp.int32)
    cosine, sine = turn_tables(positions, width // HEADS)
    bias = score_bias(frame_count, offset)
    share = entries // devices
    owners = (codes // share) ^ me
    places = jnp.where(
        jnp.arange(LEVELS)[None, :] < mid,
        place_of(owners, devices, 4),
        place_of(owners, devices, 5),
    )
    flat_codes = (places * share + codes % share).astype(jnp.int32).T

    normed_first, q, k, v, scales, qkv_weights = qkv_call(
        *orders[2], halo, inputs, early_pieces, cosine, sine
    )
    come_a, come_b = after((come_a, come_b), q)
    feed_a, feed_b = join(feed_a, come_a), join(feed_b, come_b)
    come_a = gather_swaps(feed_a, devices, 4, 1)
    come_b = gather_swaps(feed_b, devices, 5, 1)
    mixed, logsum = attend_call(q, after(k, feed_a, feed_b), v, bias)
    come_a, come_b = after((come_a, come_b), mixed)
    feed_a, feed_b = join(feed_a, come_a), join(feed_b, come_b)
    feed_pieces = (feed_a, swap(feed_a, devices, 1), feed_b, swap(feed_b, devices, 1))
    (
        branch_first, after_first, normed_second, hidden, slope, branch_second, low_out, latent,
        feed_weights,
    ) = forward_call(orders[4:], inputs, mixed, scales, feed_pieces, units, depth)

    carried = fetch_call(levels, codes, latent, book)
    keep_high, send_high = spread_call(mid, mid, flat_codes, carried, entries)
    come_high = swap_parts([send_high], devices, 5, 0)
    carried = after(carried, keep_high)
    keep_low, send_low = spread_call(0, mid, flat_codes, carried, entries)
    come_low = swap_parts([send_low], devices, 4, 0)
    keep_high, come_high = reduce_split(keep_high, after(come_high, keep_low), devices, 5, 1)
    keep_low, come_low = reduce_split(keep_low, after(come_low, keep_high), devices, 4, 1)

    carried = after(carried, keep_high, keep_low)
    grad_second, grad_pre, grad_after, grad_first, grad_mixed, sums_second = backward_call(
        carried, branch_second, slope, after_first, branch_first, scales, feed_weights
    )
    keep_a, send_a, keep_b, send_b = weight_call(
        orders[4:], normed_second, grad_pre, grad_second, hidden, low_out, carried, mixed,
        grad_first,
    )
    come_a = swap_parts([send_a], devices, 4, 0)
    come_b = swap_parts([send_b], devices, 5, 0)
    come_high, come_low = after((come_high, come_low), keep_a)
    keep_high, come_high = reduce_split(keep_high, come_high, devices, 5, 2)
    keep_low, come_low = reduce_split(keep_low, come_low, devices, 4, 2)

    lead = MARGIN // QROWS
    blocks = frame_count // QROWS
    zeros = jnp.zeros((MARGIN, width), f32)
    grad_mixed = after(grad_mixed, keep_high, keep_low)
    fixed = (logsum, bias, cosine, sine)
    q_a, k_a, v_a, halo = attend_back_call(0, lead, q, k, v, grad_mixed, *fixed, zeros, zeros)
    halo = lax.ppermute(halo, "tm", [(i + 1, i) for i in range(spans - 1)])
    come_a, come_b = after((come_a, come_b), k_a)
    keep_a, come_a = reduce_split(keep_a, come_a, devices, 4, 1)
    keep_b, come_b = reduce_split(keep_b, come_b, devices, 5, 1)
    grad_mixed = after(grad_mixed, keep_a, keep_b)
    q_b, k_b, v_b, _ = attend_back_call(lead, lead, q, k, v, grad_mixed, *fixed, k_a, v_a)
    come_high, come_low = after((come_high, come_low), k_b)
    keep_book, come_book = merge_split(
        ((keep_low, come_low), (keep_high, come_high)), 0, devices, 4, 3
    )
    grad_mixed = after(grad_mixed, keep_book)
    q_c, k_c, v_c, _ = attend_back_call(
        2 * lead, blocks - 2 * lead, q, k, v, grad_mixed, *fixed, k_b, v_b
    )
    come_a, come_b, come_book = after((come_a, come_b, come_book), k_c)
    for stage in range(4, stages):
        keep_book, come_book = reduce_split(keep_book, come_book, devices, 4, stage)
    keep_a, come_a = reduce_split(keep_a, come_a, devices, 4, 2)
    keep_b, come_b = reduce_split(keep_b, come_b, devices, 5, 2)
    input_gradient, keep_qkv, send_qkv = finish_call(
        *orders[2], inputs, normed_first, (q_a, q_b, q_c), (k_b, after(k_c, keep_a, keep_b, keep_book)),
        (v_b, v_c), halo, cosine, sine, grad_after, scales, sums_second, qkv_weights,
    )
    come_qkv = swap_parts([send_qkv], devices, 2, 0)
    grad_book = reduce_add(keep_book, after(come_book, keep_qkv))
    come_a, come_b = after((come_a, come_b), grad_book)
    keep_feed, come_feed = merge_split(
        ((keep_a, come_a), (keep_b, come_b)), 2, devices, 4, 3, 20
    )
    keep_qkv, come_qkv = reduce_split(keep_qkv, after(come_qkv, keep_feed), devices, 2, 1)
    for stage in range(4, stages):
        keep_feed, come_feed = reduce_split(keep_feed, come_feed, devices, 4, stage)
    for stage in range(2, len(digit_plan(devices, 2))):
        keep_qkv, come_qkv = reduce_split(keep_qkv, come_qkv, devices, 2, stage)
    grad_feed = reduce_add(keep_feed, after(come_feed, keep_qkv))[0]
    grad_qkv = reduce_add(keep_qkv, come_qkv)[0]

    gradients = (grad_feed, grad_qkv, grad_book)
    squares = jnp.zeros((), f32)
    for gradient in gradients:
        squares = squares + jnp.sum(gradient * gradient)
    shared = lax.all_to_all(jnp.broadcast_to(squares, (devices, 128)), AXES, 0, 0, tiled=True)
    gradient_norm = jnp.sqrt(jnp.sum(shared[:, 0]))
    factor = clip_level / jnp.maximum(gradient_norm, clip_level)
    updated = adam_call(
        factor.reshape(1),
        gradients,
        (
            (attention_master, attention_first, attention_second),
            (feedforward_master, feedforward_first, feedforward_second),
            (projection_master, projection_first, projection_second),
            (codebook_master, codebook_first, codebook_second),
            (scales_master, scales_first, scales_second),
        ),
    )
    return (latent, input_gradient, gradient_norm, *updated)


def solution(mesh):
    rows = P(AXES, None)
    middle = P(None, AXES, None)
    scale = P(None, AXES)
    in_specs = (rows, rows, P("clip")) + (middle,) * 6 + (rows,) * 3 + (middle,) * 3 + (scale,) * 3
    out_specs = (rows, rows, P()) + (middle,) * 8 + (rows,) * 4 + (middle,) * 4 + (scale,) * 4
    return jax.shard_map(body, mesh=mesh, in_specs=in_specs, out_specs=out_specs, check_vma=False)
```

```python
import math

import jax
import jax.numpy as jnp
import numpy as np
from jax import lax
from jax.experimental import pallas as pl
from jax.experimental.pallas import tpu as pltpu
from jax.sharding import PartitionSpec as P

HEADS = 8
LEVELS = 8
WINDOW = 250
STEP = 10
AXES = ("clip", "tm")

clip_level = 1.0
beta_first = 0.9
beta_second = 0.95
adam_floor = 1e-08
weight_decay = 0.1
group_rates = (0.05, 0.03, 0.05, 0.5, 0.5)
masked_score = -1e30

f32 = jnp.float32
bf16 = jnp.bfloat16
MARGIN = (WINDOW + 127) // 128 * 128
QROWS = 128
SPAN = QROWS + MARGIN
ROWS = 256
MIB = 1 << 20
FEED_SHARE, BOOK_SHARE = 4, 2


def dot(left, right, contract=((1,), (0,))):
    return lax.dot_general(left, right, (contract, ((), ())), preferred_element_type=f32)


def dot_nt(left, right):
    return dot(left, right, ((1,), (1,)))


def flip(block):
    return block.astype(f32).T.astype(bf16)


def params(mib):
    return pltpu.CompilerParams(vmem_limit_bytes=mib * MIB)


def whole(shape):
    return pl.BlockSpec(tuple(shape), lambda *_: (0,) * len(shape))


def smem():
    return pl.BlockSpec(memory_space=pltpu.SMEM)


def cost(share, length=1):
    return pl.CostEstimate(flops=int(share * 500000000), bytes_accessed=length * 3 * MIB, transcendentals=0)


def after(value, *earlier):
    return lax.optimization_barrier((value, earlier))[0]


def digit_plan(count, kind):
    bits = count.bit_length() - 1
    middle = [(1, 4)] if kind < 4 else [(1, 2), (2, 2)] if kind == 4 else [(2, 2), (1, 2)]
    plan, shift = [(0, 2)] + middle, 3
    while shift < bits:
        width = min(2, bits - shift) if kind == 2 else 1
        plan.append((shift, 1 << width))
        shift += width
    return plan


def swap(block, count, mask):
    return lax.ppermute(block, AXES, [(i, i ^ mask) for i in range(count)])


def gather_swaps(block, count, kind, stage):
    shift, radix = digit_plan(count, kind)[stage]
    return [swap(block, count, k << shift) for k in range(1, radix)]


def join_kernel(count, widths, *refs):
    outs = refs[count:]
    top = 0
    for part in refs[:count]:
        rows, left = part.shape[0], 0
        for out, width in zip(outs, widths):
            out[top : top + rows, :] = part[:, left : left + width]
            left += width
        top += rows


def join(block, others, widths=None, share=0):
    parts = [block, *others]
    rows, columns = block.shape
    widths = widths or (columns,)
    if rows % 16:
        whole_block = jnp.concatenate(parts, axis=0)
        edges = [sum(widths[:index]) for index in range(len(widths) + 1)]
        outs = [whole_block[:, left:right] for left, right in zip(edges, edges[1:])]
    else:
        outs = pl.pallas_call(
            lambda *refs: join_kernel(len(parts), widths, *refs),
            grid=(1,),
            in_specs=[whole(part.shape) for part in parts],
            out_specs=[whole((len(parts) * rows, width)) for width in widths],
            out_shape=[
                jax.ShapeDtypeStruct((len(parts) * rows, width), block.dtype) for width in widths
            ],
            compiler_params=params(16),
            cost_estimate=cost(share, 1),
            name="join_rows",
        )(*parts)
    return outs[0] if len(widths) == 1 else outs


def place_of(device, count, kind):
    place, weight = 0, 1
    for shift, radix in reversed(digit_plan(count, kind)):
        place = place + ((device >> shift) & (radix - 1)) * weight
        weight *= radix
    return place


def device_of_places(count, kind):
    table = np.zeros(count, np.int32)
    for device in range(count):
        table[place_of(device, count, kind)] = device
    return table


def swap_parts(parts, count, kind, stage):
    shift, _ = digit_plan(count, kind)[stage]
    return [swap(part, count, (k + 1) << shift) for k, part in enumerate(parts)]


def reduce_add(keep, parts):
    total = keep.astype(f32)
    for part in parts:
        total = total + part.astype(f32)
    return total


def split_kernel(radix, *refs):
    outs, operands = refs[-radix:], refs[:-radix]
    total = operands[0][...].astype(f32)
    for operand in operands[1:]:
        total = total + operand[...].astype(f32)
    size = total.shape[1] // radix
    for k, out in enumerate(outs):
        out[...] = total[:, k * size : (k + 1) * size, :].astype(out.dtype)


def reduce_split(keep, parts, count, kind, stage, share=0, held=f32):
    _, radix = digit_plan(count, kind)[stage]
    lead, rows, columns = keep.shape
    size = rows // radix
    if lead > 1:
        steps, block, index = lead, (1, rows, columns), lambda i: (i, 0, 0)
    else:
        steps = 2 if columns % 256 == 0 else 1
        block, index = (1, rows, columns // steps), lambda i: (0, 0, i)
    shares = (block[0], size, block[2])
    kinds = [held] + [bf16] * (radix - 1)
    outs = pl.pallas_call(
        lambda *refs: split_kernel(radix, *refs),
        grid=(steps,),
        in_specs=[pl.BlockSpec(block, index)] * (1 + len(parts)),
        out_specs=[pl.BlockSpec(shares, index)] * radix,
        out_shape=[jax.ShapeDtypeStruct((lead, size, columns), kind) for kind in kinds],
        compiler_params=params(20),
        cost_estimate=cost(share, 1),
        name="split_sums",
    )(keep, *parts)
    return outs[0], swap_parts(outs[1:], count, kind, stage)


def pair_kernel(radix, *refs):
    outs, operands = refs[-2 * radix :], refs[: -2 * radix]
    half = len(operands) // 2
    for index in range(2):
        split_kernel(
            radix,
            *operands[index * half : (index + 1) * half],
            *outs[index * radix : (index + 1) * radix],
        )


def pair_split(low, high, count, kinds, stage):
    _, radix = digit_plan(count, kinds[0])[stage]
    lead, rows, columns = low[0].shape
    spec = lambda size: pl.BlockSpec((1, size, columns), lambda i: (i, 0, 0))
    operands = [low[0], *low[1], high[0], *high[1]]
    types = ([f32] + [bf16] * (radix - 1)) * 2
    outs = pl.pallas_call(
        lambda *refs: pair_kernel(radix, *refs),
        grid=(lead,),
        in_specs=[spec(rows)] * len(operands),
        out_specs=[spec(rows // radix)] * len(types),
        out_shape=[jax.ShapeDtypeStruct((lead, rows // radix, columns), kind) for kind in types],
        compiler_params=params(20),
        cost_estimate=cost(0, 2),
        name="split_sums",
    )(*operands)
    return (
        (outs[0], swap_parts(outs[1:radix], count, kinds[0], stage)),
        (outs[radix], swap_parts(outs[radix + 1 :], count, kinds[1], stage)),
    )


def merge_kernel(radix, groups, *refs):
    outs = refs[-radix:]
    base = left = 0
    for size in groups:
        total = refs[base][...].astype(f32)
        for operand in refs[base + 1 : base + size]:
            total = total + operand[...].astype(f32)
        base += size
        rows = total.shape[1] // radix
        for k, out in enumerate(outs):
            share = total[:, k * rows : (k + 1) * rows, :].astype(out.dtype)
            out[:, :, left : left + total.shape[2]] = share
        left += total.shape[2]


def merge_split(groups, count, kind, stage, share=0):
    _, radix = digit_plan(count, kind)[stage]
    operands = [array for keep, parts in groups for array in (keep, *parts)]
    _, rows, _ = groups[0][0].shape
    shape = (1, rows // radix, sum(keep.shape[2] for keep, _ in groups))
    sizes = [1 + len(parts) for _, parts in groups]
    kinds = [f32] + [bf16] * (radix - 1)
    outs = pl.pallas_call(
        lambda *refs: merge_kernel(radix, sizes, *refs),
        grid=(1,),
        in_specs=[whole(operand.shape) for operand in operands],
        out_specs=[whole(shape)] * radix,
        out_shape=[jax.ShapeDtypeStruct(shape, kind) for kind in kinds],
        compiler_params=params(20),
        cost_estimate=cost(share, 1),
        name="split_sums",
    )(*operands)
    return outs[0], swap_parts(outs[1:], count, kind, stage)


def stack_kernel(radix, half, *refs):
    outs, operands = refs[-radix:], refs[:-radix]
    size = operands[0].shape[1] // radix

    def add(parts):
        total = sum(part[...].astype(f32) for part in parts)
        for k, out in enumerate(outs):
            out[...] = total[:, k * size : (k + 1) * size, :].astype(out.dtype)

    @pl.when(pl.program_id(0) < half)
    def _():
        add(operands[: len(operands) // 2])

    @pl.when(pl.program_id(0) >= half)
    def _():
        add(operands[len(operands) // 2 :])


def stack_split(low, high, count, kind, stage, share=0):
    _, radix = digit_plan(count, kind)[stage]
    operands = [low[0], *low[1], high[0], *high[1]]
    half, rows, columns = low[0].shape
    kinds = [f32] + [bf16] * (radix - 1)
    block = (1, rows, columns)
    below = pl.BlockSpec(block, lambda i: (jnp.minimum(i, half - 1), 0, 0))
    above = pl.BlockSpec(block, lambda i: (jnp.maximum(i - half, 0), 0, 0))
    outs = pl.pallas_call(
        lambda *refs: stack_kernel(radix, half, *refs),
        grid=(2 * half,),
        in_specs=[below] * (1 + len(low[1])) + [above] * (1 + len(high[1])),
        out_specs=[pl.BlockSpec((1, rows // radix, columns), lambda i: (i, 0, 0))] * radix,
        out_shape=[
            jax.ShapeDtypeStruct((2 * half, rows // radix, columns), kind) for kind in kinds
        ],
        compiler_params=params(20),
        cost_estimate=cost(share, 2),
        name="split_sums",
    )(*operands)
    return outs[0], swap_parts(outs[1:], count, kind, stage)


def one_hot_rows(rowmap, size):
    place = lax.broadcasted_iota(jnp.int32, (size, size), 0)
    return jnp.where(place == rowmap, 1.0, 0.0).astype(bf16)


def unpack_rows(starts_ref, rowmap_ref, pieces, out_ref):
    half = pieces[0].shape[0]
    count = starts_ref.shape[0]
    rows = 2 * half // count
    if rows % 16 == 0:
        for place in range(count):
            piece = pieces[place * rows // half]
            inner = place * rows % half
            start = pl.multiple_of(starts_ref[place], rows)
            out_ref[pl.ds(start, rows), :] = piece[inner : inner + rows, :]
    else:
        spread = one_hot_rows(rowmap_ref[0:1, :], 2 * half)
        columns = out_ref.shape[1]
        for left in range(0, columns, 128):
            joined = jnp.concatenate([p[:, left : left + 128] for p in pieces], axis=0)
            out_ref[:, left : left + 128] = dot(spread, joined).astype(bf16)


def pack_rows(starts_ref, rowmap_ref, work_ref, outs):
    size, columns = work_ref.shape
    half = size // 2
    count = starts_ref.shape[0]
    rows = size // count
    if rows % 16 == 0:
        for place in range(count):
            start = pl.multiple_of(starts_ref[place], rows)
            out, inner = outs[place * rows // half], place * rows % half
            out[0, inner : inner + rows, :] = work_ref[pl.ds(start, rows), :]
    else:
        spread = one_hot_rows(rowmap_ref[0:1, :], size)
        for left in range(0, columns, 128):
            lanes = slice(left, left + 128)
            joined = dot(spread, work_ref[:, lanes], ((0,), (0,))).astype(bf16)
            for index, out in enumerate(outs):
                out[0, :, lanes] = joined[index * half : (index + 1) * half]


def centre_rows(values):
    centred = values - jnp.mean(values, axis=-1, keepdims=True)
    spread = jnp.mean(centred * centred, axis=-1, keepdims=True)
    rstd = lax.rsqrt(spread + 1e-05)
    return centred * rstd, rstd


def norm_back(normal, rstd, gain, grad):
    inner = grad * gain
    first = jnp.mean(inner, axis=-1, keepdims=True)
    second = jnp.mean(inner * normal, axis=-1, keepdims=True)
    return rstd * (inner - first - normal * second)


def column_sum(values):
    return jnp.sum(values, axis=0, keepdims=True)


def turn(values, cosine, sine):
    lanes = values.shape[1]
    ahead = pltpu.roll(values, lanes - 32, 1)
    behind = pltpu.roll(values, 32, 1)
    lane = lax.broadcasted_iota(jnp.int32, values.shape, 1)
    partner = jnp.where(lane % 64 < 32, ahead, behind)
    repeats = lanes // cosine.shape[1]
    if repeats > 1:
        cosine = jnp.concatenate([cosine] * repeats, axis=1)
        sine = jnp.concatenate([sine] * repeats, axis=1)
    return values * cosine + partner * sine


def head_columns(flipped):
    zero = jnp.zeros((64, flipped.shape[1]), flipped.dtype)
    return jnp.concatenate(
        [
            jnp.concatenate([flipped[:64], zero], axis=1),
            jnp.concatenate([zero, flipped[64:]], axis=1),
        ],
        axis=0,
    )


def head_rows(block):
    lane = lax.broadcasted_iota(jnp.int32, block.shape, 1)
    zero = jnp.zeros_like(block)
    return jnp.concatenate(
        [jnp.where(lane < 64, block, zero), jnp.where(lane < 64, zero, block)], axis=0
    )


def lower_kernel(attention, feed, projection, book, scales, early, later, low_book, work):
    width = attention.shape[2]
    units = feed.shape[2]
    rows = attention.shape[1]
    for k in range(3):
        early[:, k * width : (k + 1) * width] = attention[k].astype(bf16)
    work[...] = jnp.zeros(work.shape, f32)
    work[: scales.shape[0], :rows] = scales[...]
    early[:, 3 * width :] = work[...].T[:rows].astype(bf16)
    for k in range(2):
        later[:, k * units : (k + 1) * units] = feed[k].astype(bf16)
    last = 2 * units + projection.shape[1]
    later[:, 2 * units : last] = projection[...].astype(bf16)
    later[:, last:] = attention[3].astype(bf16)
    low_book[...] = book[...].astype(bf16)


def lower_call(attention, feed, projection, book, scales):
    _, rows, width = attention.shape
    columns = 2 * feed.shape[2] + projection.shape[1] + width
    shapes = ((rows, 3 * width + 128), (rows, columns), book.shape)
    operands = (attention, feed, projection, book, scales)
    return pl.pallas_call(
        lower_kernel,
        grid=(1,),
        in_specs=[whole(operand.shape) for operand in operands],
        out_specs=[whole(shape) for shape in shapes],
        out_shape=[jax.ShapeDtypeStruct(shape, bf16) for shape in shapes],
        scratch_shapes=[pltpu.VMEM((128, 128), f32)],
        compiler_params=params(62),
        cost_estimate=cost(0, 1),
        name="lower_weights",
    )(*operands)


def qkv_kernel(
    starts, rowmap, halo, inputs, piece_a, piece_b, cosine, sine, normed, q, k, v, scales, weights
):
    step = pl.program_id(0)
    width = inputs.shape[1]

    @pl.when(step == 0)
    def _():
        unpack_rows(starts, rowmap, (piece_a, piece_b), weights)
        scales[...] = weights[:, 3 * width :].astype(f32).T[:8]

    frames = jnp.where(step == 0, halo[...].astype(f32), inputs[...].astype(f32))
    normal, _ = centre_rows(frames)
    low = (normal * scales[0:1, :] + scales[1:2, :]).astype(bf16)
    normed[...] = low
    turned = turn(dot(low, weights[:, :width]), cosine[...], sine[...])
    q[...] = (turned.astype(bf16).astype(f32) * 0.125).astype(bf16)
    k[...] = turn(dot(low, weights[:, width : 2 * width]), cosine[...], sine[...]).astype(bf16)
    v[...] = dot(low, weights[:, 2 * width : 3 * width]).astype(bf16)


def qkv_call(starts, rowmap, halo, inputs, pieces, cosine, sine):
    count, width = inputs.shape
    columns = pieces[0].shape[1]
    steps = count // ROWS + 1
    late = lambda i: (jnp.maximum(i - 1, 0), 0)
    here = lambda i: (i, 0)
    return pl.pallas_call(
        qkv_kernel,
        grid=(steps,),
        in_specs=[
            smem(),
            whole(rowmap.shape),
            whole(halo.shape),
            pl.BlockSpec((ROWS, width), late),
            whole(pieces[0].shape),
            whole(pieces[1].shape),
            pl.BlockSpec((ROWS, 128), here),
            pl.BlockSpec((ROWS, 128), here),
        ],
        out_specs=[
            pl.BlockSpec((ROWS, width), late),
            pl.BlockSpec((ROWS, width), late),
            pl.BlockSpec((ROWS, width), here),
            pl.BlockSpec((ROWS, width), here),
            whole((8, width)),
            whole((width, columns)),
        ],
        out_shape=[
            jax.ShapeDtypeStruct((count, width), bf16),
            jax.ShapeDtypeStruct((count, width), bf16),
            jax.ShapeDtypeStruct((count + MARGIN, width), bf16),
            jax.ShapeDtypeStruct((count + MARGIN, width), bf16),
            jax.ShapeDtypeStruct((8, width), f32),
            jax.ShapeDtypeStruct((width, columns), bf16),
        ],
        compiler_params=params(48),
        cost_estimate=cost(4, 8),
        name="project_rows",
    )(starts, rowmap, halo, inputs, *pieces, cosine, sine)


def attend_kernel(q, k, v, bias, mixed, logsum, v_flipped):
    step = pl.program_id(0)
    pairs = q.shape[1] // 128

    @pl.when(step == 0)
    def _():
        for pair in range(pairs):
            lanes = slice(pair * 128, (pair + 1) * 128)
            v_flipped[lanes, :] = flip(v[:, lanes])

    start = pl.multiple_of(step * QROWS, QROWS)
    allowed = jnp.concatenate([bias[0], bias[0]], axis=1)
    rows = []
    for pair in range(pairs):
        lanes = slice(pair * 128, (pair + 1) * 128)
        columns = head_columns(flip(q[:, lanes]))
        scores = dot(k[pl.ds(start, SPAN), lanes], columns) + allowed
        highest = jnp.max(scores, axis=0, keepdims=True)
        raised = jnp.exp(scores - highest)
        total = column_sum(raised)
        joined = dot(v_flipped[lanes, pl.ds(start, SPAN)], raised.astype(bf16))
        joined = joined * (1.0 / total)
        output = jnp.concatenate([joined[:64, :QROWS], joined[64:, QROWS:]], axis=0)
        mixed[:, lanes] = output.T.astype(bf16)
        record = highest + jnp.log(total)
        rows += [record[:, :QROWS], record[:, QROWS:]]
    logsum[...] = jnp.concatenate(rows, axis=0)


def attend_call(q, k, v, bias):
    count, width = q.shape
    return pl.pallas_call(
        attend_kernel,
        grid=(count // QROWS,),
        in_specs=[
            pl.BlockSpec((QROWS, width), lambda i: (i, 0)),
            whole(k.shape),
            whole(v.shape),
            pl.BlockSpec((1, SPAN, QROWS), lambda i: (i, 0, 0)),
        ],
        out_specs=[
            pl.BlockSpec((QROWS, width), lambda i: (i, 0)),
            pl.BlockSpec((HEADS, QROWS), lambda i: (0, i)),
        ],
        out_shape=[
            jax.ShapeDtypeStruct((count, width), bf16),
            jax.ShapeDtypeStruct((HEADS, count), f32),
        ],
        scratch_shapes=[pltpu.VMEM((width, k.shape[0]), bf16)],
        compiler_params=params(40),
        cost_estimate=cost(4, 14),
        name="attend_rows",
    )(q, k, v, bias)


def forward_kernel(
    starts_a, rowmap_a, starts_b, rowmap_b, inputs, mixed, scales, own_a, other_a, own_b, other_b,
    branch_first, after_first, normed, hidden, slope, branch_second, low_out, latent, weights,
):
    step = pl.program_id(0)
    width = inputs.shape[1]
    units = hidden.shape[1]

    @pl.when(step == 0)
    def _():
        unpack_rows(starts_a, rowmap_a, (own_a, other_a), weights.at[:, :units])
        unpack_rows(starts_b, rowmap_b, (own_b, other_b), weights.at[:, units:])

    up, down = 0, units
    proj = 2 * units
    last = proj + latent.shape[1]
    first = dot(mixed[...], weights[:, last : last + width])
    branch_first[...] = first
    after = inputs[...].astype(f32) + scales[4:5, :] * first
    after_first[...] = after
    normal, _ = centre_rows(after)
    low = (normal * scales[2:3, :] + scales[3:4, :]).astype(bf16)
    normed[...] = low
    second = jnp.zeros(after.shape, f32)
    chunk = 512
    for left in range(0, units, chunk):
        pre = dot(low, weights[:, up + left : up + left + chunk])
        share = 0.5 + 0.5 * lax.erf(pre * (1.0 / math.sqrt(2.0)))
        bell = jnp.exp(-0.5 * pre * pre) * (1.0 / math.sqrt(2.0 * math.pi))
        part = (pre * share).astype(bf16)
        hidden[:, left : left + chunk] = part
        slope[:, left : left + chunk] = (share + pre * bell).astype(bf16)
        second = second + dot_nt(part, weights[:, down + left : down + left + chunk])
    branch_second[...] = second
    rounded = (after + scales[5:6, :] * second).astype(bf16)
    low_out[...] = rounded
    latent[...] = dot(rounded, weights[:, proj:last])


def forward_call(orders, inputs, mixed, scales, pieces, units, depth):
    count, width = inputs.shape
    columns = pieces[0].shape[1] + pieces[2].shape[1]
    row = lambda size: pl.BlockSpec((ROWS, size), lambda i: (i, 0))
    kept = ((width, f32), (width, f32), (width, bf16), (units, bf16), (units, bf16),
            (width, f32), (width, bf16), (depth, f32))
    (starts_a, rowmap_a), (starts_b, rowmap_b) = orders
    return pl.pallas_call(
        forward_kernel,
        grid=(count // ROWS,),
        in_specs=[smem(), whole(rowmap_a.shape)] * 2
        + [row(width), row(width), whole(scales.shape)]
        + [whole(piece.shape) for piece in pieces],
        out_specs=[row(size) for size, _ in kept] + [whole((width, columns))],
        out_shape=[jax.ShapeDtypeStruct((count, size), kind) for size, kind in kept]
        + [jax.ShapeDtypeStruct((width, columns), bf16)],
        compiler_params=params(56),
        cost_estimate=cost(4, 17),
        name="feed_rows",
    )(starts_a, rowmap_a, starts_b, rowmap_b, inputs, mixed, scales, *pieces)


def fetch_kernel(active, codes, latent, book, carried, residue, steps, columns):
    level = pl.program_id(0)
    count, depth = latent.shape
    tiles = book.shape[1] // 256

    @pl.when(level == 0)
    def _():
        residue[...] = latent[...]
        columns[...] = codes[...].astype(f32).T

    factor = jnp.where(level < active[0], 1.0, 0.0).astype(f32)
    lane = lax.broadcasted_iota(jnp.int32, (ROWS, LEVELS), 1)
    place = lax.broadcasted_iota(jnp.int32, (ROWS, 256), 1).astype(f32)
    for top in range(0, count, ROWS):
        rows = slice(top, top + ROWS)
        code = jnp.where(lane == level, columns[rows, :], 0.0)
        code = jnp.sum(code, axis=1, keepdims=True)
        high = jnp.floor(code * (1.0 / 256.0))
        hit = jnp.where(place == code - 256.0 * high, 1.0, 0.0).astype(bf16)
        picks = [hit * jnp.where(high == j, 1.0, 0.0).astype(bf16) for j in range(tiles)]
        found = dot(jnp.concatenate(picks, axis=1), book[0])
        left = residue[rows, :] - factor * found
        residue[rows, :] = left
        steps[level, rows, :] = factor * left

    @pl.when(level == LEVELS - 1)
    def _():
        for top in range(0, count, ROWS):
            rows = slice(top, top + ROWS)
            total = jnp.zeros((ROWS, depth), f32)
            for index in reversed(range(LEVELS)):
                total = total + steps[index, rows, :]
                live = jnp.where(index < active[0], 1.0, 0.0).astype(f32)
                carried[index, rows, :] = (live * total).astype(bf16)


def fetch_call(active, codes, latent, book):
    count, depth = latent.shape
    entries = book.shape[1]
    return pl.pallas_call(
        fetch_kernel,
        grid=(LEVELS,),
        in_specs=[
            smem(),
            whole(codes.shape),
            whole(latent.shape),
            pl.BlockSpec((1, entries, depth), lambda i: (i, 0, 0)),
        ],
        out_specs=whole((LEVELS, count, depth)),
        out_shape=jax.ShapeDtypeStruct((LEVELS, count, depth), bf16),
        scratch_shapes=[
            pltpu.VMEM((count, depth), f32),
            pltpu.VMEM((LEVELS, count, depth), f32),
            pltpu.VMEM((count, LEVELS), f32),
        ],
        compiler_params=params(48),
        cost_estimate=cost(4, 13),
        name="fetch_codes",
    )(active, codes, latent, book)


def spread_kernel(first, codes, carried, keep, send):
    level = pl.program_id(0) + first
    count = carried.shape[1]
    half = keep.shape[1]
    code = codes[pl.ds(level, 1), :]
    high = code >> 8
    place = lax.broadcasted_iota(jnp.int32, (256, count), 0)
    hit = jnp.where(place == (code & 255), -1.0, 0.0).astype(bf16)
    for j in range(2 * half // 256):
        pick = hit * jnp.where(high == j, 1.0, 0.0).astype(bf16)
        out, inner = (keep, send)[j * 256 // half], j * 256 % half
        out[0, inner : inner + 256, :] = dot(pick, carried[0]).astype(bf16)


def spread_call(first, levels, codes, carried, entries):
    _, count, depth = carried.shape
    half = entries // 2
    return pl.pallas_call(
        lambda *refs: spread_kernel(first, *refs),
        grid=(levels,),
        in_specs=[
            whole(codes.shape),
            pl.BlockSpec((1, count, depth), lambda i: (i + first, 0, 0)),
        ],
        out_specs=[pl.BlockSpec((1, half, depth), lambda i: (i, 0, 0))] * 2,
        out_shape=[jax.ShapeDtypeStruct((levels, half, depth), bf16)] * 2,
        compiler_params=params(16),
        cost_estimate=cost(1, 5),
        name="spread_codes",
    )(codes, carried)


def backward_kernel(
    starts_a, rowmap_a, starts_b, rowmap_b, carried, branch_second, slope, after_first, branch_first, normed, hidden, low_out, mixed,
    scales, weights,
    out_after, out_mixed, sums, keep_a, send_a, keep_b, send_b,
    work, grad_pre, kept_hidden, kept_carried, grad_branch, flipped,
):
    step = pl.program_id(0)
    last_step = pl.num_programs(0) - 1
    width = after_first.shape[1]
    units = slope.shape[1]
    proj = 2 * units
    last = proj + carried.shape[2]
    chunk = 512
    rows = pl.ds(pl.multiple_of(step * ROWS, ROWS), ROWS)

    @pl.when(step == 0)
    def _():
        sums[...] = jnp.zeros(sums.shape, f32)

    grad_after = dot_nt(carried[0], weights[:, proj:last])
    sums[5:6, :] += column_sum(grad_after * branch_second[...])
    low = (grad_after * scales[5:6, :]).astype(bf16)
    grad_normed = jnp.zeros(grad_after.shape, f32)
    for left in range(0, units, chunk):
        grad_hidden = dot(low, weights[:, units + left : units + left + chunk])
        part = (grad_hidden * slope[:, left : left + chunk].astype(f32)).astype(bf16)
        grad_pre[rows, left : left + chunk] = part
        grad_normed = grad_normed + dot_nt(part, weights[:, left : left + chunk])
    normal, rstd = centre_rows(after_first[...])
    sums[2:3, :] += column_sum(grad_normed * normal)
    sums[3:4, :] += column_sum(grad_normed)
    grad_first = grad_after + norm_back(normal, rstd, scales[2:3, :], grad_normed)
    out_after[...] = grad_first
    sums[4:5, :] += column_sum(grad_first * branch_first[...])
    low_first = (grad_first * scales[4:5, :]).astype(bf16)
    grad_branch[rows, :] = low_first
    out_mixed[...] = dot_nt(low_first, weights[:, last : last + width]).astype(bf16)
    kept_hidden[rows, :] = hidden[...]
    kept_carried[rows, :] = carried[0]
    for index, block in enumerate((normed[...], low, low_out[...], mixed[...])):
        flipped[index, :, rows] = flip(block)

    @pl.when(step == last_step)
    def _():
        for left in range(0, units, chunk):
            lanes = slice(left, left + chunk)
            work[:, lanes] = dot(flipped[0], grad_pre[:, lanes]).astype(bf16)
            lanes = slice(left, left + chunk)
            work[:, units + left : units + left + chunk] = dot(
                flipped[1], kept_hidden[:, lanes]
            ).astype(bf16)
        work[:, proj:last] = dot(flipped[2], kept_carried[...]).astype(bf16)
        work[:, last:] = dot(flipped[3], grad_branch[...]).astype(bf16)
        half = keep_a.shape[2]
        pack_rows(starts_a, rowmap_a, work.at[:, :half], (keep_a, send_a))
        pack_rows(starts_b, rowmap_b, work.at[:, half:], (keep_b, send_b))


def backward_call(
    orders, carried, branch_second, slope, after_first, branch_first, normed, hidden, low_out,
    mixed, scales, weights,
):
    count, width = after_first.shape
    units, depth = slope.shape[1], carried.shape[2]
    columns = weights.shape[1]
    row = lambda size: pl.BlockSpec((ROWS, size), lambda i: (i, 0))
    piece = (1, width // 2, columns // 2)
    (starts_a, rowmap_a), (starts_b, rowmap_b) = orders
    return pl.pallas_call(
        backward_kernel,
        grid=(count // ROWS,),
        in_specs=[smem(), whole(rowmap_a.shape)] * 2
        + [pl.BlockSpec((1, ROWS, depth), lambda i: (0, i, 0))]
        + [row(width), row(units), row(width), row(width), row(width), row(units), row(width)]
        + [row(width), whole(scales.shape), whole(weights.shape)],
        out_specs=[row(width), row(width), whole((8, width))] + [whole(piece)] * 4,
        out_shape=[
            jax.ShapeDtypeStruct((count, width), f32),
            jax.ShapeDtypeStruct((count, width), bf16),
            jax.ShapeDtypeStruct((8, width), f32),
        ]
        + [jax.ShapeDtypeStruct(piece, bf16)] * 4,
        scratch_shapes=[
            pltpu.VMEM((width, columns), bf16),
            pltpu.VMEM((count, units), bf16),
            pltpu.VMEM((count, units), bf16),
            pltpu.VMEM((count, depth), bf16),
            pltpu.VMEM((count, width), bf16),
            pltpu.VMEM((4, width, count), bf16),
        ],
        compiler_params=params(56),
        cost_estimate=cost(2, 25),
        name="feed_back",
    )(
        starts_a, rowmap_a, starts_b, rowmap_b, carried, branch_second, slope, after_first, branch_first, normed, hidden,
        low_out, mixed, scales, weights,
    )


def attend_back_kernel(pieces, *refs):
    k_refs, v_refs = refs[:pieces], refs[pieces : 2 * pieces]
    (q, grad, logsum, bias, cosine, sine, start_k, start_v,
     grad_q, grad_k, grad_v, halo, k, v, k_flipped) = refs[2 * pieces :]
    step = pl.program_id(0)
    pairs = q.shape[1] // 128

    @pl.when(step == 0)
    def _():
        for index in range(pieces):
            rows = slice(index * MARGIN, (index + 1) * MARGIN)
            k[rows, :] = k_refs[index][...]
            v[rows, :] = v_refs[index][...]
            for pair in range(pairs):
                lanes = slice(pair * 128, (pair + 1) * 128)
                k_flipped[lanes, rows] = flip(k_refs[index][:, lanes])
        grad_k[:MARGIN, :] = start_k[...]
        grad_v[:MARGIN, :] = start_v[...]
        grad_k[MARGIN:, :] = jnp.zeros_like(grad_k[MARGIN:, :])
        grad_v[MARGIN:, :] = jnp.zeros_like(grad_v[MARGIN:, :])

    start = pl.multiple_of(step * QROWS, QROWS)
    keys = pl.ds(start, SPAN)
    allowed = jnp.concatenate([bias[0], bias[0]], axis=1)
    back = -sine[...]
    for pair in range(pairs):
        lanes = slice(pair * 128, (pair + 1) * 128)
        heads = (2 * pair, 2 * pair + 1)
        record = jnp.concatenate([logsum[h : h + 1, :] for h in heads], axis=1)
        scores = dot(k[keys, lanes], head_columns(flip(q[:, lanes]))) + allowed
        weights = jnp.exp(scores - record)
        grad_weights = dot(v[keys, lanes], head_columns(flip(grad[:, lanes])))
        product = weights * grad_weights
        inner = column_sum(product)
        grad_scores = (product - weights * inner).astype(bf16)
        grad_v[keys, lanes] += dot(weights.astype(bf16), head_rows(grad[:, lanes]))
        grad_k[keys, lanes] += dot(grad_scores, head_rows(q[:, lanes]))
        joined = dot(k_flipped[lanes, keys], grad_scores)
        flat = jnp.concatenate([joined[:64, :QROWS], joined[64:, QROWS:]], axis=0).T * 0.125
        grad_q[:, lanes] = turn(flat, cosine[...], back).astype(bf16)

    @pl.when(step == pl.num_programs(0) - 1)
    def _():
        halo[:MARGIN, :] = grad_k[:MARGIN, :].astype(bf16)
        halo[MARGIN:, :] = grad_v[:MARGIN, :].astype(bf16)


def attend_back_call(offset, blocks, q, k, v, grad, logsum, bias, cosine, sine, start_k, start_v):
    width = q.shape[1]
    keys = blocks * QROWS + MARGIN
    lead = MARGIN // QROWS
    pieces = keys // MARGIN
    there = lambda i: (i + offset, 0)
    table = lambda i: (i + offset + lead, 0)
    fixed = lambda index: pl.BlockSpec((MARGIN, width), lambda i: (index, 0))
    return pl.pallas_call(
        lambda *refs: attend_back_kernel(pieces, *refs),
        grid=(blocks,),
        in_specs=[fixed(offset // lead + index) for index in range(pieces)] * 2
        + [
            pl.BlockSpec((QROWS, width), there),
            pl.BlockSpec((QROWS, width), there),
            pl.BlockSpec((HEADS, QROWS), lambda i: (0, i + offset)),
            pl.BlockSpec((1, SPAN, QROWS), lambda i: (i + offset, 0, 0)),
            pl.BlockSpec((QROWS, 128), table),
            pl.BlockSpec((QROWS, 128), table),
            fixed(start_k.shape[0] // MARGIN - 1),
            fixed(start_v.shape[0] // MARGIN - 1),
        ],
        out_specs=[
            pl.BlockSpec((QROWS, width), lambda i: (i, 0)),
            whole((keys, width)),
            whole((keys, width)),
            whole((2 * MARGIN, width)),
        ],
        out_shape=[
            jax.ShapeDtypeStruct((blocks * QROWS, width), bf16),
            jax.ShapeDtypeStruct((keys, width), f32),
            jax.ShapeDtypeStruct((keys, width), f32),
            jax.ShapeDtypeStruct((2 * MARGIN, width), bf16),
        ],
        scratch_shapes=[
            pltpu.VMEM((keys, width), bf16),
            pltpu.VMEM((keys, width), bf16),
            pltpu.VMEM((width, keys), bf16),
        ],
        compiler_params=params(20),
        cost_estimate=cost(0 if offset > 0 else 8, 2 * blocks),
        name="attend_back",
    )(*[k] * pieces, *[v] * pieces, q, grad, logsum, bias, cosine, sine, start_k, start_v)


def finish_kernel(
    starts, rowmap, inputs, normed, q_a, q_b, q_c, k_a, k_b, v_a, v_b, halo, cosine, sine,
    grad_after, scales, sums_second, weights,
    out, keep_a, send_a, keep_b, send_b, work, turned_q, turned_k, turned_v, sums,
):
    step = pl.program_id(0)
    last = pl.num_programs(0) - 1
    count, width = normed.shape

    @pl.when(step == 0)
    def _():
        sums[...] = jnp.zeros(sums.shape, f32)
        sums[:8, :] = sums_second[...]
        left = 0
        for piece in (q_a, q_b, q_c):
            turned_q[left : left + piece.shape[0], :] = piece[...]
            left += piece.shape[0]

    rows = pl.ds(pl.multiple_of(step * ROWS, ROWS), ROWS)
    near = jnp.where(step == last, 1.0, 0.0).astype(f32)
    part_k = jnp.where(step == 0, k_a[...], k_b[...]) + near * halo[:MARGIN, :].astype(f32)
    part_v = jnp.where(step == 0, v_a[...], v_b[...]) + near * halo[MARGIN:, :].astype(f32)
    turned = turn(part_k, cosine[...], -sine[...]).astype(bf16)
    turned_k[rows, :] = turned
    value = part_v.astype(bf16)
    turned_v[rows, :] = value
    grad = dot_nt(turned_q[rows, :], weights[:, :width])
    grad = grad + dot_nt(turned, weights[:, width : 2 * width])
    grad = grad + dot_nt(value, weights[:, 2 * width : 3 * width])
    normal, rstd = centre_rows(inputs[...].astype(f32))
    sums[0:1, :] += column_sum(grad * normal)
    sums[1:2, :] += column_sum(grad)
    out[...] = grad_after[...] + norm_back(normal, rstd, scales[0:1, :], grad)

    @pl.when(step == last)
    def _():
        flipped = flip(normed[...])
        for index, turned_ref in enumerate((turned_q, turned_k, turned_v)):
            lanes = slice(index * width, (index + 1) * width)
            work[:, lanes] = dot(flipped, turned_ref[...]).astype(bf16)
        work[:, 3 * width :] = sums[...].T.astype(bf16)
        half = keep_a.shape[2]
        pack_rows(starts, rowmap, work.at[:, :half], (keep_a, send_a))
        pack_rows(starts, rowmap, work.at[:, half:], (keep_b, send_b))


def finish_call(
    starts, rowmap, inputs, normed, grad_q, grad_k, grad_v, halo, cosine, sine,
    grad_after, scales, sums_second, weights,
):
    count, width = normed.shape
    columns = 3 * width + 256
    row = pl.BlockSpec((ROWS, width), lambda i: (i, 0))
    first = pl.BlockSpec((ROWS, width), lambda i: (0, 0))
    rest = pl.BlockSpec((ROWS, width), lambda i: (jnp.maximum(i - 1, 0), 0))
    table = pl.BlockSpec((ROWS, 128), lambda i: (i + MARGIN // ROWS, 0))
    half = columns // 256 * 128
    shapes = [jax.ShapeDtypeStruct((count, width), f32)] + [
        jax.ShapeDtypeStruct((1, width // 2, size), bf16)
        for size in (half, half, columns - half, columns - half)
    ]
    return pl.pallas_call(
        finish_kernel,
        grid=(count // ROWS,),
        in_specs=[smem(), whole(rowmap.shape), row, whole(normed.shape)]
        + [whole(piece.shape) for piece in grad_q]
        + [first, rest, first, rest]
        + [whole(halo.shape), table, table, row]
        + [whole(scales.shape), whole(sums_second.shape), whole(weights.shape)],
        out_specs=[row] + [whole(shape.shape) for shape in shapes[1:]],
        out_shape=shapes,
        scratch_shapes=[
            pltpu.VMEM((width, columns), bf16),
            pltpu.VMEM((count, width), bf16),
            pltpu.VMEM((count, width), bf16),
            pltpu.VMEM((count, width), bf16),
            pltpu.VMEM((256, width), f32),
        ],
        compiler_params=params(32),
        cost_estimate=cost(0, 10),
        name="finish_rows",
    )(
        starts, rowmap, inputs, normed, *grad_q, *grad_k, *grad_v, halo, cosine, sine,
        grad_after, scales, sums_second, weights,
    )


def adam_update(master, first, second, gradient, factor, rate):
    clipped = gradient * factor
    momentum = beta_first * first + (1.0 - beta_first) * clipped
    variance = beta_second * second + (1.0 - beta_second) * clipped * clipped
    corrected = momentum / (1.0 - beta_first**STEP)
    divisor = jnp.sqrt(variance / (1.0 - beta_second**STEP)) + adam_floor
    updated = master - rate * (corrected / divisor + weight_decay * master)
    return (momentum, variance, updated, updated.astype(bf16))


def full_sum(values):
    return jnp.sum(jnp.sum(values, axis=0, keepdims=True), axis=1, keepdims=True)


def book_kernel(keep, *refs):
    parts, (out, length) = refs[:-2], refs[-2:]
    total = keep[...]
    for part in parts:
        total = total + part[...].astype(f32)
    out[...] = total
    length[...] = full_sum(jnp.sum(total * total, axis=0))


def book_call(keep, parts):
    return pl.pallas_call(
        book_kernel,
        grid=(1,),
        in_specs=[whole(keep.shape)] * (1 + len(parts)),
        out_specs=[whole(keep.shape), whole((1, 1))],
        out_shape=[
            jax.ShapeDtypeStruct(keep.shape, f32),
            jax.ShapeDtypeStruct((1, 1), f32),
        ],
        compiler_params=params(16),
        cost_estimate=cost(BOOK_SHARE, 1),
        name="book_sums",
    )(keep, *parts)


def total_kernel(groups, squares, *refs):
    outs, shared = refs[-1 - len(groups) : -1], refs[-1]
    length = squares[...]
    base = 0
    for size, out in zip(groups, outs):
        total = refs[base][0]
        for part in refs[base + 1 : base + size]:
            total = total + part[0].astype(f32)
        base += size
        out[...] = total
        length = length + full_sum(total * total)
    shared[...] = jnp.broadcast_to(length, shared.shape)


def total_call(squares, groups, count):
    operands = [array for keep, parts in groups for array in (keep, *parts)]
    sizes = [1 + len(parts) for _, parts in groups]
    shapes = [keep.shape[1:] for keep, _ in groups] + [(count, 128)]
    return pl.pallas_call(
        lambda *refs: total_kernel(sizes, *refs),
        grid=(1,),
        in_specs=[whole((1, 1))] + [whole(operand.shape) for operand in operands],
        out_specs=[whole(shape) for shape in shapes],
        out_shape=[jax.ShapeDtypeStruct(shape, f32) for shape in shapes],
        compiler_params=params(16),
        cost_estimate=cost(0, 1),
        name="last_sums",
    )(squares, *operands)


def adam_kernel(shared, grad_feed, grad_qkv, grad_book, *refs):
    masters, firsts, seconds = refs[0:15:3], refs[1:15:3], refs[2:15:3]
    norm_ref = refs[15]
    outs = [refs[16 + 4 * group : 20 + 4 * group] for group in range(5)]
    norm = jnp.sqrt(jnp.sum(shared[:, 0:1], axis=0, keepdims=True))
    norm_ref[...] = norm
    factor = clip_level / jnp.maximum(norm, clip_level)

    def update(group, index, gradient):
        results = adam_update(
            masters[group][index], firsts[group][index], seconds[group][index],
            gradient, factor, group_rates[group],
        )
        for out, result in zip(outs[group], results):
            out[index] = result

    width = (grad_qkv.shape[1] - 256) // 3
    units = masters[1].shape[2]
    depth = masters[2].shape[1]
    for k in range(3):
        update(0, k, grad_qkv[:, k * width : (k + 1) * width])
    update(0, 3, grad_feed[:, 2 * units + depth :])
    for k in range(2):
        update(1, k, grad_feed[:, k * units : (k + 1) * units])
    update(2, Ellipsis, grad_feed[:, 2 * units : 2 * units + depth])
    for level in range(LEVELS):
        update(3, level, grad_book[level])
    update(4, Ellipsis, grad_qkv[:, 3 * width :].T[:6])


def adam_call(shared, gradients, states):
    operands = [shared, *gradients] + [array for group in states for array in group]
    shapes = [jax.ShapeDtypeStruct((1, 1), f32)] + [
        jax.ShapeDtypeStruct(group[0].shape, kind)
        for group in states
        for kind in (f32, f32, f32, bf16)
    ]
    return pl.pallas_call(
        adam_kernel,
        grid=(1,),
        in_specs=[whole(operand.shape) for operand in operands],
        out_specs=[whole(shape.shape) for shape in shapes],
        out_shape=shapes,
        compiler_params=params(40),
        cost_estimate=cost(3, 2),
        name="adam_step",
    )(*operands)


def turn_tables(positions, depth):
    half = depth // 2
    freqs = jnp.exp(-math.log(10000.0) * jnp.arange(half, dtype=f32) * 2.0 / depth)
    angles = positions.astype(f32)[:, None] * freqs[None, :]
    cosine, sine = jnp.cos(angles), jnp.sin(angles)
    return (
        jnp.concatenate([cosine] * 4, axis=1),
        jnp.concatenate([-sine, sine, -sine, sine], axis=1),
    )


def score_bias(count, offset):
    block = jnp.arange(count // QROWS, dtype=jnp.int32)[:, None, None]
    key_place = jnp.arange(SPAN, dtype=jnp.int32)[None, :, None]
    query_place = jnp.arange(QROWS, dtype=jnp.int32)[None, None, :]
    distance = MARGIN + query_place - key_place
    reach = offset + block * QROWS + key_place - MARGIN
    allowed = (distance >= 0) & (distance <= WINDOW) & (reach >= 0)
    return jnp.where(allowed, 0.0, masked_score).astype(f32)


def body(
    inputs, codes, levels,
    attention_master, attention_first, attention_second,
    feedforward_master, feedforward_first, feedforward_second,
    projection_master, projection_first, projection_second,
    codebook_master, codebook_first, codebook_second,
    scales_master, scales_first, scales_second,
):
    spans = lax.axis_size("tm")
    devices = lax.axis_size("clip") * spans
    me = lax.axis_index("clip") * spans + lax.axis_index("tm")
    frame_count, width = inputs.shape
    units = feedforward_master.shape[2]
    depth = projection_master.shape[1]
    rows = projection_master.shape[0]
    entries = codebook_master.shape[1] * devices

    early, feed, book = lower_call(
        attention_master, feedforward_master, projection_master, codebook_master, scales_master
    )
    mid = LEVELS // 2
    book = lax.all_gather(book, AXES, axis=1, tiled=True)
    stages = len(digit_plan(devices, 3))
    split_stages = len(digit_plan(devices, 4))
    halo = lax.ppermute(
        inputs[frame_count - MARGIN :], "tm", [(i, i + 1) for i in range(spans - 1)]
    )
    for stage in reversed(range(2, len(digit_plan(devices, 2)))):
        early = join(early, gather_swaps(early, devices, 2, stage))
    mark = early
    for stage in reversed(range(4, split_stages)):
        feed = join(feed, after(gather_swaps(feed, devices, 4, stage), early))
    offset = lax.axis_index("tm") * frame_count
    positions = after(offset, mark) - MARGIN + jnp.arange(frame_count + MARGIN, dtype=jnp.int32)
    cosine, sine = turn_tables(positions, width // HEADS)
    bias = score_bias(frame_count, offset)
    def order(kind):
        owners = jnp.asarray(device_of_places(devices, kind)) ^ me
        starts = (owners * rows).astype(jnp.int32)
        if rows % 16 == 0:
            return starts, jnp.zeros((1, 128), jnp.int32)
        rowmap = (starts[:, None] + jnp.arange(rows, dtype=jnp.int32)[None, :]).reshape(1, width)
        return starts, rowmap

    orders = {kind: order(kind) for kind in range(2, 6)}
    share = entries // devices
    owners = (codes // share) ^ me
    places = jnp.where(
        jnp.arange(LEVELS)[None, :] < mid,
        place_of(owners, devices, 4),
        place_of(owners, devices, 5),
    )
    flat_codes = (places * share + codes % share).astype(jnp.int32).T
    flat_codes, orders = after((flat_codes, orders), mark)
    ready = (cosine, sine, bias, flat_codes, orders)
    early = join(early, after(gather_swaps(early, devices, 2, 1), ready))
    come = after(gather_swaps(feed, devices, 4, 3), early)
    early_pieces = (early, swap(early, devices, 1))
    feed_a, feed_b = join(feed, come, (units, feed.shape[1] - units), 10)
    come_a = gather_swaps(feed_a, devices, 4, 2)
    come_b = gather_swaps(feed_b, devices, 5, 2)

    normed_first, q, k, v, scales, qkv_weights = qkv_call(
        *orders[2], halo, inputs, early_pieces, cosine, sine
    )
    come_a, come_b = after((come_a, come_b), q)
    feed_a, feed_b = join(feed_a, come_a), join(feed_b, come_b)
    come_a = gather_swaps(feed_a, devices, 4, 1)
    come_b = gather_swaps(feed_b, devices, 5, 1)
    mixed, logsum = attend_call(q, after(k, feed_a, feed_b), v, bias)
    come_a, come_b = after((come_a, come_b), mixed)
    feed_a, feed_b = join(feed_a, come_a), join(feed_b, come_b)
    feed_pieces = (feed_a, swap(feed_a, devices, 1), feed_b, swap(feed_b, devices, 1))
    (
        branch_first, after_first, normed_second, hidden, slope, branch_second, low_out, latent,
        feed_weights,
    ) = forward_call((orders[4], orders[5]), inputs, mixed, scales, feed_pieces, units, depth)

    carried = fetch_call(levels, codes.T, latent, book)
    keep_high, send_high = spread_call(mid, mid, flat_codes, carried, entries)
    come_high = swap_parts([send_high], devices, 5, 0)
    carried = after(carried, keep_high)
    keep_low, send_low = spread_call(0, mid, flat_codes, carried, entries)
    come_low = swap_parts([send_low], devices, 4, 0)
    high = reduce_split(keep_high, after(come_high, keep_low), devices, 5, 1, 0, bf16)
    low = reduce_split(keep_low, after(come_low, high[0]), devices, 4, 1, 0, bf16)

    grad_after, grad_mixed, sums_second, keep_a, send_a, keep_b, send_b = backward_call(
        (orders[4], orders[5]), after(carried, high[0], low[0]), branch_second, slope, after_first, branch_first,
        normed_second, hidden, low_out, mixed, scales, feed_weights,
    )
    come_a = swap_parts([send_a], devices, 4, 0)
    come_b = swap_parts([send_b], devices, 5, 0)
    come_low, come_high = after((low[1], high[1]), keep_a)
    low, high = pair_split((low[0], come_low), (high[0], come_high), devices, (4, 5), 2)

    lead = MARGIN // QROWS
    blocks = frame_count // QROWS
    zeros = jnp.zeros((MARGIN, width), f32)
    fixed = (logsum, bias, cosine, sine)
    grad_mixed = after(grad_mixed, low[0])
    q_a, k_a, v_a, halo = attend_back_call(0, lead, q, k, v, grad_mixed, *fixed, zeros, zeros)
    halo = lax.ppermute(halo, "tm", [(i + 1, i) for i in range(spans - 1)])
    come_a, come_b = after((come_a, come_b), k_a)
    keep_a, come_a = reduce_split(keep_a, come_a, devices, 4, 1)
    keep_b, come_b = reduce_split(keep_b, come_b, devices, 5, 1)
    grad_mixed = after(grad_mixed, keep_a, keep_b)
    q_b, k_b, v_b, _ = attend_back_call(lead, lead, q, k, v, grad_mixed, *fixed, k_a, v_a)
    come_low, come_high = after((low[1], high[1]), k_b)
    keep_book, come_book = stack_split((low[0], come_low), (high[0], come_high), devices, 4, 3)
    grad_mixed = after(grad_mixed, keep_book)
    q_c, k_c, v_c, _ = attend_back_call(
        2 * lead, blocks - 2 * lead, q, k, v, grad_mixed, *fixed, k_b, v_b
    )
    come_book, come_a, come_b = after((come_book, come_a, come_b), k_c)
    keep_a, come_a = reduce_split(keep_a, come_a, devices, 4, 2)
    keep_b, come_b = reduce_split(keep_b, come_b, devices, 5, 2)
    for stage in range(4, split_stages):
        keep_book, come_book = reduce_split(keep_book, come_book, devices, 4, stage)
    input_gradient, qkv_a, send_a, qkv_b, send_b = finish_call(
        *orders[2], inputs, normed_first, (q_a, q_b, q_c),
        (k_b, after(k_c, keep_book, keep_a, keep_b)), (v_b, v_c), halo, cosine, sine, grad_after,
        scales, sums_second, qkv_weights,
    )
    send_a = swap_parts([send_a], devices, 2, 0)
    send_b = swap_parts([send_b], devices, 2, 0)
    grad_book, squares = book_call(keep_book, after(come_book, qkv_a))
    come_a, come_b = after((come_a, come_b), grad_book)
    keep_feed, come_feed = merge_split(
        ((keep_a, come_a), (keep_b, come_b)), devices, 4, 3, FEED_SHARE
    )
    send_a, send_b = after((send_a, send_b), keep_feed)
    keep_qkv, come_qkv = merge_split(((qkv_a, send_a), (qkv_b, send_b)), devices, 2, 1)
    for stage in range(4, split_stages):
        keep_feed, come_feed = reduce_split(keep_feed, come_feed, devices, 4, stage)
    for stage in range(2, len(digit_plan(devices, 2))):
        keep_qkv, come_qkv = reduce_split(keep_qkv, come_qkv, devices, 2, stage)
    grad_feed, grad_qkv, shared = total_call(
        squares, ((keep_feed, come_feed), (keep_qkv, come_qkv)), devices
    )

    shared = lax.all_to_all(shared, AXES, 0, 0, tiled=True)
    gradient_norm, *updated = adam_call(
        shared,
        (grad_feed, grad_qkv, grad_book),
        (
            (attention_master, attention_first, attention_second),
            (feedforward_master, feedforward_first, feedforward_second),
            (projection_master, projection_first, projection_second),
            (codebook_master, codebook_first, codebook_second),
            (scales_master, scales_first, scales_second),
        ),
    )
    return (latent, input_gradient, gradient_norm[0, 0], *updated)


def solution(mesh):
    rows = P(AXES, None)
    middle = P(None, AXES, None)
    scale = P(None, AXES)
    in_specs = (rows, rows, P("clip")) + (middle,) * 6 + (rows,) * 3 + (middle,) * 3 + (scale,) * 3
    out_specs = (rows, rows, P()) + (middle,) * 8 + (rows,) * 4 + (middle,) * 4 + (scale,) * 4
    return jax.shard_map(body, mesh=mesh, in_specs=in_specs, out_specs=out_specs, check_vma=False)
```

```python
import math

import jax
import jax.numpy as jnp
import numpy as np
from jax import lax
from jax.experimental import pallas as pl
from jax.experimental.pallas import tpu as pltpu
from jax.sharding import PartitionSpec as P

HEADS = 8
LEVELS = 8
WINDOW = 250
STEP = 10
AXES = ("clip", "tm")

clip_level = 1.0
beta_first = 0.9
beta_second = 0.95
adam_floor = 1e-08
weight_decay = 0.1
group_rates = (0.05, 0.03, 0.05, 0.5, 0.5)
masked_score = -1e30

f32 = jnp.float32
bf16 = jnp.bfloat16
MARGIN = (WINDOW + 127) // 128 * 128
QROWS = 128
SPAN = QROWS + MARGIN
ROWS = 256
MIB = 1 << 20
FEED_SHARE, BOOK_SHARE = 4, 2


def dot(left, right, contract=((1,), (0,))):
    return lax.dot_general(left, right, (contract, ((), ())), preferred_element_type=f32)


def dot_nt(left, right):
    return dot(left, right, ((1,), (1,)))


def flip(block):
    return block.astype(f32).T.astype(bf16)


def params(mib):
    return pltpu.CompilerParams(vmem_limit_bytes=mib * MIB)


def whole(shape):
    return pl.BlockSpec(tuple(shape), lambda *_: (0,) * len(shape))


def smem():
    return pl.BlockSpec(memory_space=pltpu.SMEM)


def cost(share, length=1):
    return pl.CostEstimate(flops=int(share * 500000000), bytes_accessed=length * 3 * MIB, transcendentals=0)


def after(value, *earlier):
    return lax.optimization_barrier((value, earlier))[0]


def digit_plan(count, kind):
    bits = count.bit_length() - 1
    middle = [(1, 4)] if kind < 4 else [(1, 2), (2, 2)] if kind == 4 else [(2, 2), (1, 2)]
    plan, shift = [(0, 2)] + middle, 3
    while shift < bits:
        width = min(2, bits - shift) if kind == 2 else 1
        plan.append((shift, 1 << width))
        shift += width
    return plan


def swap(block, count, mask):
    return lax.ppermute(block, AXES, [(i, i ^ mask) for i in range(count)])


def gather_swaps(block, count, kind, stage):
    shift, radix = digit_plan(count, kind)[stage]
    return [swap(block, count, k << shift) for k in range(1, radix)]


def join_kernel(count, widths, *refs):
    outs = refs[count:]
    top = 0
    for part in refs[:count]:
        rows, left = part.shape[0], 0
        for out, width in zip(outs, widths):
            out[top : top + rows, :] = part[:, left : left + width]
            left += width
        top += rows


def join(block, others, widths=None, share=0):
    parts = [block, *others]
    rows, columns = block.shape
    widths = widths or (columns,)
    if rows % 16:
        whole_block = jnp.concatenate(parts, axis=0)
        edges = [sum(widths[:index]) for index in range(len(widths) + 1)]
        outs = [whole_block[:, left:right] for left, right in zip(edges, edges[1:])]
    else:
        outs = pl.pallas_call(
            lambda *refs: join_kernel(len(parts), widths, *refs),
            grid=(1,),
            in_specs=[whole(part.shape) for part in parts],
            out_specs=[whole((len(parts) * rows, width)) for width in widths],
            out_shape=[
                jax.ShapeDtypeStruct((len(parts) * rows, width), block.dtype) for width in widths
            ],
            compiler_params=params(16),
            cost_estimate=cost(share, 1),
            name="join_rows",
        )(*parts)
    return outs[0] if len(widths) == 1 else outs


def place_of(device, count, kind):
    place, weight = 0, 1
    for shift, radix in reversed(digit_plan(count, kind)):
        place = place + ((device >> shift) & (radix - 1)) * weight
        weight *= radix
    return place


def device_of_places(count, kind):
    table = np.zeros(count, np.int32)
    for device in range(count):
        table[place_of(device, count, kind)] = device
    return table


def swap_parts(parts, count, kind, stage):
    shift, _ = digit_plan(count, kind)[stage]
    return [swap(part, count, (k + 1) << shift) for k, part in enumerate(parts)]


def reduce_add(keep, parts):
    total = keep.astype(f32)
    for part in parts:
        total = total + part.astype(f32)
    return total


def split_kernel(radix, *refs):
    outs, operands = refs[-radix:], refs[:-radix]
    total = operands[0][...].astype(f32)
    for operand in operands[1:]:
        total = total + operand[...].astype(f32)
    size = total.shape[1] // radix
    for k, out in enumerate(outs):
        out[...] = total[:, k * size : (k + 1) * size, :].astype(out.dtype)


def reduce_split(keep, parts, count, kind, stage, share=0, held=f32):
    _, radix = digit_plan(count, kind)[stage]
    lead, rows, columns = keep.shape
    size = rows // radix
    if lead > 1:
        steps, block, index = lead, (1, rows, columns), lambda i: (i, 0, 0)
    else:
        steps = 2 if columns % 256 == 0 else 1
        block, index = (1, rows, columns // steps), lambda i: (0, 0, i)
    shares = (block[0], size, block[2])
    kinds = [held] + [bf16] * (radix - 1)
    outs = pl.pallas_call(
        lambda *refs: split_kernel(radix, *refs),
        grid=(steps,),
        in_specs=[pl.BlockSpec(block, index)] * (1 + len(parts)),
        out_specs=[pl.BlockSpec(shares, index)] * radix,
        out_shape=[jax.ShapeDtypeStruct((lead, size, columns), kind) for kind in kinds],
        compiler_params=params(20),
        cost_estimate=cost(share, 1),
        name="split_sums",
    )(keep, *parts)
    return outs[0], swap_parts(outs[1:], count, kind, stage)


def pair_kernel(radix, *refs):
    outs, operands = refs[-2 * radix :], refs[: -2 * radix]
    half = len(operands) // 2
    for index in range(2):
        split_kernel(
            radix,
            *operands[index * half : (index + 1) * half],
            *outs[index * radix : (index + 1) * radix],
        )


def pair_split(low, high, count, kinds, stage):
    _, radix = digit_plan(count, kinds[0])[stage]
    lead, rows, columns = low[0].shape
    spec = lambda size: pl.BlockSpec((1, size, columns), lambda i: (i, 0, 0))
    operands = [low[0], *low[1], high[0], *high[1]]
    types = ([f32] + [bf16] * (radix - 1)) * 2
    outs = pl.pallas_call(
        lambda *refs: pair_kernel(radix, *refs),
        grid=(lead,),
        in_specs=[spec(rows)] * len(operands),
        out_specs=[spec(rows // radix)] * len(types),
        out_shape=[jax.ShapeDtypeStruct((lead, rows // radix, columns), kind) for kind in types],
        compiler_params=params(20),
        cost_estimate=cost(0, 2),
        name="split_sums",
    )(*operands)
    return (
        (outs[0], swap_parts(outs[1:radix], count, kinds[0], stage)),
        (outs[radix], swap_parts(outs[radix + 1 :], count, kinds[1], stage)),
    )


def merge_kernel(radix, groups, *refs):
    outs = refs[-radix:]
    base = left = 0
    for size in groups:
        total = refs[base][...].astype(f32)
        for operand in refs[base + 1 : base + size]:
            total = total + operand[...].astype(f32)
        base += size
        rows = total.shape[1] // radix
        for k, out in enumerate(outs):
            share = total[:, k * rows : (k + 1) * rows, :].astype(out.dtype)
            out[:, :, left : left + total.shape[2]] = share
        left += total.shape[2]


def merge_split(groups, count, kind, stage, share=0):
    _, radix = digit_plan(count, kind)[stage]
    operands = [array for keep, parts in groups for array in (keep, *parts)]
    _, rows, _ = groups[0][0].shape
    shape = (1, rows // radix, sum(keep.shape[2] for keep, _ in groups))
    sizes = [1 + len(parts) for _, parts in groups]
    kinds = [f32] + [bf16] * (radix - 1)
    outs = pl.pallas_call(
        lambda *refs: merge_kernel(radix, sizes, *refs),
        grid=(1,),
        in_specs=[whole(operand.shape) for operand in operands],
        out_specs=[whole(shape)] * radix,
        out_shape=[jax.ShapeDtypeStruct(shape, kind) for kind in kinds],
        compiler_params=params(20),
        cost_estimate=cost(share, 1),
        name="split_sums",
    )(*operands)
    return outs[0], swap_parts(outs[1:], count, kind, stage)


def stack_kernel(radix, half, *refs):
    outs, operands = refs[-radix:], refs[:-radix]
    size = operands[0].shape[1] // radix

    def add(parts):
        total = sum(part[...].astype(f32) for part in parts)
        for k, out in enumerate(outs):
            out[...] = total[:, k * size : (k + 1) * size, :].astype(out.dtype)

    @pl.when(pl.program_id(0) < half)
    def _():
        add(operands[: len(operands) // 2])

    @pl.when(pl.program_id(0) >= half)
    def _():
        add(operands[len(operands) // 2 :])


def stack_split(low, high, count, kind, stage, share=0):
    _, radix = digit_plan(count, kind)[stage]
    operands = [low[0], *low[1], high[0], *high[1]]
    half, rows, columns = low[0].shape
    kinds = [f32] + [bf16] * (radix - 1)
    block = (1, rows, columns)
    below = pl.BlockSpec(block, lambda i: (jnp.minimum(i, half - 1), 0, 0))
    above = pl.BlockSpec(block, lambda i: (jnp.maximum(i - half, 0), 0, 0))
    outs = pl.pallas_call(
        lambda *refs: stack_kernel(radix, half, *refs),
        grid=(2 * half,),
        in_specs=[below] * (1 + len(low[1])) + [above] * (1 + len(high[1])),
        out_specs=[pl.BlockSpec((1, rows // radix, columns), lambda i: (i, 0, 0))] * radix,
        out_shape=[
            jax.ShapeDtypeStruct((2 * half, rows // radix, columns), kind) for kind in kinds
        ],
        compiler_params=params(20),
        cost_estimate=cost(share, 2),
        name="split_sums",
    )(*operands)
    return outs[0], swap_parts(outs[1:], count, kind, stage)


def one_hot_rows(rowmap, size):
    place = lax.broadcasted_iota(jnp.int32, (size, size), 0)
    return jnp.where(place == rowmap, 1.0, 0.0).astype(bf16)


def unpack_rows(starts_ref, rowmap_ref, pieces, out_ref):
    half = pieces[0].shape[0]
    count = starts_ref.shape[0]
    rows = 2 * half // count
    if rows % 16 == 0:
        for place in range(count):
            piece = pieces[place * rows // half]
            inner = place * rows % half
            start = pl.multiple_of(starts_ref[place], rows)
            out_ref[pl.ds(start, rows), :] = piece[inner : inner + rows, :]
    else:
        spread = one_hot_rows(rowmap_ref[0:1, :], 2 * half)
        columns = out_ref.shape[1]
        for left in range(0, columns, 128):
            joined = jnp.concatenate([p[:, left : left + 128] for p in pieces], axis=0)
            out_ref[:, left : left + 128] = dot(spread, joined).astype(bf16)


def store_flipped(dests_ref, rowmap_ref, block, out_ref, lanes):
    flipped = flip(block)
    size = flipped.shape[0]
    count = dests_ref.shape[0]
    rows = size // count
    if rows % 16 == 0:
        for index in range(count):
            start = pl.multiple_of(dests_ref[index], rows)
            out_ref[pl.ds(start, rows), lanes] = flipped[index * rows : (index + 1) * rows]
    else:
        spread = one_hot_rows(rowmap_ref[0:1, :], size)
        out_ref[:, lanes] = dot(spread, flipped, ((0,), (0,))).astype(bf16)


def store_halves(values, keep, send, lanes):
    half = keep.shape[1]
    keep[0, :, lanes] = values[:half].astype(bf16)
    send[0, :, lanes] = values[half:].astype(bf16)


def centre_rows(values):
    centred = values - jnp.mean(values, axis=-1, keepdims=True)
    spread = jnp.mean(centred * centred, axis=-1, keepdims=True)
    rstd = lax.rsqrt(spread + 1e-05)
    return centred * rstd, rstd


def norm_back(normal, rstd, gain, grad):
    inner = grad * gain
    first = jnp.mean(inner, axis=-1, keepdims=True)
    second = jnp.mean(inner * normal, axis=-1, keepdims=True)
    return rstd * (inner - first - normal * second)


def column_sum(values):
    return jnp.sum(values, axis=0, keepdims=True)


def turn(values, cosine, sine):
    lanes = values.shape[1]
    ahead = pltpu.roll(values, lanes - 32, 1)
    behind = pltpu.roll(values, 32, 1)
    lane = lax.broadcasted_iota(jnp.int32, values.shape, 1)
    partner = jnp.where(lane % 64 < 32, ahead, behind)
    repeats = lanes // cosine.shape[1]
    if repeats > 1:
        cosine = jnp.concatenate([cosine] * repeats, axis=1)
        sine = jnp.concatenate([sine] * repeats, axis=1)
    return values * cosine + partner * sine


def head_columns(flipped):
    zero = jnp.zeros((64, flipped.shape[1]), flipped.dtype)
    return jnp.concatenate(
        [
            jnp.concatenate([flipped[:64], zero], axis=1),
            jnp.concatenate([zero, flipped[64:]], axis=1),
        ],
        axis=0,
    )


def head_rows(block):
    lane = lax.broadcasted_iota(jnp.int32, block.shape, 1)
    zero = jnp.zeros_like(block)
    return jnp.concatenate(
        [jnp.where(lane < 64, block, zero), jnp.where(lane < 64, zero, block)], axis=0
    )


def lower_kernel(attention, feed, projection, book, scales, early, later, low_book, work):
    width = attention.shape[2]
    units = feed.shape[2]
    rows = attention.shape[1]
    for k in range(3):
        early[:, k * width : (k + 1) * width] = attention[k].astype(bf16)
    work[...] = jnp.zeros(work.shape, f32)
    work[: scales.shape[0], :rows] = scales[...]
    early[:, 3 * width :] = work[...].T[:rows].astype(bf16)
    for k in range(2):
        later[:, k * units : (k + 1) * units] = feed[k].astype(bf16)
    last = 2 * units + projection.shape[1]
    later[:, 2 * units : last] = projection[...].astype(bf16)
    later[:, last:] = attention[3].astype(bf16)
    low_book[...] = book[...].astype(bf16)


def lower_call(attention, feed, projection, book, scales):
    _, rows, width = attention.shape
    columns = 2 * feed.shape[2] + projection.shape[1] + width
    shapes = ((rows, 3 * width + 128), (rows, columns), book.shape)
    operands = (attention, feed, projection, book, scales)
    return pl.pallas_call(
        lower_kernel,
        grid=(1,),
        in_specs=[whole(operand.shape) for operand in operands],
        out_specs=[whole(shape) for shape in shapes],
        out_shape=[jax.ShapeDtypeStruct(shape, bf16) for shape in shapes],
        scratch_shapes=[pltpu.VMEM((128, 128), f32)],
        compiler_params=params(62),
        cost_estimate=cost(0, 1),
        name="lower_weights",
    )(*operands)


def qkv_kernel(
    starts, rowmap, halo, inputs, piece_a, piece_b, cosine, sine, normed, q, k, v, scales, weights
):
    step = pl.program_id(0)
    width = inputs.shape[1]

    @pl.when(step == 0)
    def _():
        unpack_rows(starts, rowmap, (piece_a, piece_b), weights)
        scales[...] = weights[:, 3 * width :].astype(f32).T[:8]

    frames = jnp.where(step == 0, halo[...].astype(f32), inputs[...].astype(f32))
    normal, _ = centre_rows(frames)
    low = (normal * scales[0:1, :] + scales[1:2, :]).astype(bf16)
    normed[...] = low
    turned = turn(dot(low, weights[:, :width]), cosine[...], sine[...])
    q[...] = (turned.astype(bf16).astype(f32) * 0.125).astype(bf16)
    k[...] = turn(dot(low, weights[:, width : 2 * width]), cosine[...], sine[...]).astype(bf16)
    v[...] = dot(low, weights[:, 2 * width : 3 * width]).astype(bf16)


def qkv_call(starts, rowmap, halo, inputs, pieces, cosine, sine):
    count, width = inputs.shape
    columns = pieces[0].shape[1]
    steps = count // ROWS + 1
    late = lambda i: (jnp.maximum(i - 1, 0), 0)
    here = lambda i: (i, 0)
    return pl.pallas_call(
        qkv_kernel,
        grid=(steps,),
        in_specs=[
            smem(),
            whole(rowmap.shape),
            whole(halo.shape),
            pl.BlockSpec((ROWS, width), late),
            whole(pieces[0].shape),
            whole(pieces[1].shape),
            pl.BlockSpec((ROWS, 128), here),
            pl.BlockSpec((ROWS, 128), here),
        ],
        out_specs=[
            pl.BlockSpec((ROWS, width), late),
            pl.BlockSpec((ROWS, width), late),
            pl.BlockSpec((ROWS, width), here),
            pl.BlockSpec((ROWS, width), here),
            whole((8, width)),
            whole((width, columns)),
        ],
        out_shape=[
            jax.ShapeDtypeStruct((count, width), bf16),
            jax.ShapeDtypeStruct((count, width), bf16),
            jax.ShapeDtypeStruct((count + MARGIN, width), bf16),
            jax.ShapeDtypeStruct((count + MARGIN, width), bf16),
            jax.ShapeDtypeStruct((8, width), f32),
            jax.ShapeDtypeStruct((width, columns), bf16),
        ],
        compiler_params=params(32),
        cost_estimate=cost(4, 8),
        name="project_rows",
    )(starts, rowmap, halo, inputs, *pieces, cosine, sine)


def attend_kernel(q, k, v, bias, mixed, logsum):
    step = pl.program_id(0)
    start = pl.multiple_of(step * QROWS, QROWS)
    keys = pl.ds(start, SPAN)
    allowed = jnp.concatenate([bias[0], bias[0]], axis=1)
    lane = lax.broadcasted_iota(jnp.int32, (QROWS, 128), 1)
    pairs = [slice(left, left + 128) for left in range(0, q.shape[1], 128)]
    columns = [head_columns(flip(q[:, lanes])) for lanes in pairs]
    scores = [dot(k[keys, lanes], column) + allowed for lanes, column in zip(pairs, columns)]
    highest = [jnp.max(score, axis=0, keepdims=True) for score in scores]
    raised = [jnp.exp(score - high) for score, high in zip(scores, highest)]
    totals = [column_sum(part) for part in raised]
    weights = [(part * (1.0 / total)).astype(bf16) for part, total in zip(raised, totals)]
    outputs = [
        dot(weight, v[keys, lanes], ((0,), (0,))) for weight, lanes in zip(weights, pairs)
    ]
    rows = []
    for lanes, output, high, total in zip(pairs, outputs, highest, totals):
        mixed[:, lanes] = jnp.where(lane < 64, output[:QROWS], output[QROWS:]).astype(bf16)
        record = high + jnp.log(total)
        rows += [record[:, :QROWS], record[:, QROWS:]]
    logsum[...] = jnp.concatenate(rows, axis=0)


def attend_call(q, k, v, bias):
    count, width = q.shape
    return pl.pallas_call(
        attend_kernel,
        grid=(count // QROWS,),
        in_specs=[
            pl.BlockSpec((QROWS, width), lambda i: (i, 0)),
            whole(k.shape),
            whole(v.shape),
            pl.BlockSpec((1, SPAN, QROWS), lambda i: (i, 0, 0)),
        ],
        out_specs=[
            pl.BlockSpec((QROWS, width), lambda i: (i, 0)),
            pl.BlockSpec((HEADS, QROWS), lambda i: (0, i)),
        ],
        out_shape=[
            jax.ShapeDtypeStruct((count, width), bf16),
            jax.ShapeDtypeStruct((HEADS, count), f32),
        ],
        compiler_params=params(24),
        cost_estimate=cost(4, 14),
        name="attend_rows",
    )(q, k, v, bias)


def forward_kernel(
    starts_a, rowmap_a, starts_b, rowmap_b, inputs, mixed, scales, own_a, other_a, own_b, other_b,
    branch_first, after_first, normed, hidden, slope, branch_second, low_out, latent, weights,
):
    step = pl.program_id(0)
    width = inputs.shape[1]
    units = hidden.shape[1]

    @pl.when(step == 0)
    def _():
        unpack_rows(starts_a, rowmap_a, (own_a, other_a), weights.at[:, :units])
        unpack_rows(starts_b, rowmap_b, (own_b, other_b), weights.at[:, units:])

    up, down = 0, units
    proj = 2 * units
    last = proj + latent.shape[1]
    first = dot(mixed[...], weights[:, last : last + width])
    branch_first[...] = first.astype(bf16)
    after = inputs[...].astype(f32) + scales[4:5, :] * first
    after_first[...] = after
    normal, _ = centre_rows(after)
    low = (normal * scales[2:3, :] + scales[3:4, :]).astype(bf16)
    normed[...] = low
    chunk = 512
    lefts = range(0, units, chunk)
    pres = [dot(low, weights[:, up + left : up + left + chunk]) for left in lefts]
    for left, pre in zip(lefts, pres):
        share = 0.5 + 0.5 * lax.erf(pre * (1.0 / math.sqrt(2.0)))
        bell = jnp.exp(-0.5 * pre * pre) * (1.0 / math.sqrt(2.0 * math.pi))
        hidden[:, left : left + chunk] = (pre * share).astype(bf16)
        slope[:, left : left + chunk] = (share + pre * bell).astype(bf16)
    second = dot_nt(hidden[...], weights[:, down : down + units])
    branch_second[...] = second.astype(bf16)
    rounded = (after + scales[5:6, :] * second).astype(bf16)
    low_out[...] = rounded
    latent[...] = dot(rounded, weights[:, proj:last])


def forward_call(orders, inputs, mixed, scales, pieces, units, depth):
    count, width = inputs.shape
    columns = pieces[0].shape[1] + pieces[2].shape[1]
    row = lambda size: pl.BlockSpec((ROWS, size), lambda i: (i, 0))
    kept = ((width, bf16), (width, f32), (width, bf16), (units, bf16), (units, bf16),
            (width, bf16), (width, bf16), (depth, f32))
    (starts_a, rowmap_a), (starts_b, rowmap_b) = orders
    return pl.pallas_call(
        forward_kernel,
        grid=(count // ROWS,),
        in_specs=[smem(), whole(rowmap_a.shape)] * 2
        + [row(width), row(width), whole(scales.shape)]
        + [whole(piece.shape) for piece in pieces],
        out_specs=[row(size) for size, _ in kept] + [whole((width, columns))],
        out_shape=[jax.ShapeDtypeStruct((count, size), kind) for size, kind in kept]
        + [jax.ShapeDtypeStruct((width, columns), bf16)],
        compiler_params=params(56),
        cost_estimate=cost(4, 17),
        name="feed_rows",
    )(starts_a, rowmap_a, starts_b, rowmap_b, inputs, mixed, scales, *pieces)


def fetch_kernel(active, codes, latent, book, carried, residue, steps, columns):
    level = pl.program_id(0)
    count, depth = latent.shape
    tiles = book.shape[1] // 256

    @pl.when(level == 0)
    def _():
        residue[...] = latent[...]
        columns[...] = codes[:LEVELS, :].astype(f32).T

    factor = jnp.where(level < active[0], 1.0, 0.0).astype(f32)
    lane = lax.broadcasted_iota(jnp.int32, (ROWS, LEVELS), 1)
    place = lax.broadcasted_iota(jnp.int32, (ROWS, 256), 1).astype(f32)
    blocks = [slice(top, top + ROWS) for top in range(0, count, ROWS)]
    picked = []
    for rows in blocks:
        code = jnp.where(lane == level, columns[rows, :], 0.0)
        code = jnp.sum(code, axis=1, keepdims=True)
        high = jnp.floor(code * (1.0 / 256.0))
        hit = jnp.where(place == code - 256.0 * high, 1.0, 0.0).astype(bf16)
        picks = [hit * jnp.where(high == j, 1.0, 0.0).astype(bf16) for j in range(tiles)]
        picked.append(jnp.concatenate(picks, axis=1))
    found = [dot(pick, book[0]) for pick in picked]
    for rows, row in zip(blocks, found):
        left = residue[rows, :] - factor * row
        residue[rows, :] = left
        steps[level, rows, :] = factor * left

    @pl.when(level == LEVELS - 1)
    def _():
        for top in range(0, count, ROWS):
            rows = slice(top, top + ROWS)
            total = jnp.zeros((ROWS, depth), f32)
            for index in reversed(range(LEVELS)):
                total = total + steps[index, rows, :]
                carried[index, rows, :] = total.astype(bf16)


def fetch_call(active, codes, latent, book):
    count, depth = latent.shape
    entries = book.shape[1]
    return pl.pallas_call(
        fetch_kernel,
        grid=(LEVELS,),
        in_specs=[
            smem(),
            whole(codes.shape),
            whole(latent.shape),
            pl.BlockSpec((1, entries, depth), lambda i: (i, 0, 0)),
        ],
        out_specs=whole((LEVELS, count, depth)),
        out_shape=jax.ShapeDtypeStruct((LEVELS, count, depth), bf16),
        scratch_shapes=[
            pltpu.VMEM((count, depth), f32),
            pltpu.VMEM((LEVELS, count, depth), f32),
            pltpu.VMEM((count, LEVELS), f32),
        ],
        compiler_params=params(48),
        cost_estimate=cost(4, 13),
        name="fetch_codes",
    )(active, codes, latent, book)


def spread_kernel(first, codes, carried, keep, send):
    count = carried.shape[1]
    half = keep.shape[1]
    level = pl.program_id(0) + first
    code = codes[pl.ds(LEVELS + level, 1), :]
    high = code >> 8
    place = lax.broadcasted_iota(jnp.int32, (256, count), 0)
    hit = jnp.where(place == (code & 255), -1.0, 0.0).astype(bf16)
    for j in range(2 * half // 256):
        pick = hit * jnp.where(high == j, 1.0, 0.0).astype(bf16)
        out, inner = (keep, send)[j * 256 // half], j * 256 % half
        out[0, inner : inner + 256, :] = dot(pick, carried[0]).astype(bf16)


def spread_call(first, levels, codes, carried, entries):
    _, count, depth = carried.shape
    half = entries // 2
    return pl.pallas_call(
        lambda *refs: spread_kernel(first, *refs),
        grid=(levels,),
        in_specs=[
            whole(codes.shape),
            pl.BlockSpec((1, count, depth), lambda i: (i + first, 0, 0)),
        ],
        out_specs=[pl.BlockSpec((1, half, depth), lambda i: (i, 0, 0))] * 2,
        out_shape=[jax.ShapeDtypeStruct((levels, half, depth), bf16)] * 2,
        compiler_params=params(16),
        cost_estimate=cost(1, 5),
        name="spread_codes",
    )(codes, carried)


def backward_kernel(
    dests_a, rowmap_a, dests_b, rowmap_b, carried, branch_second, slope, after_first, branch_first, normed, hidden, low_out, mixed,
    scales, weights,
    out_after, out_mixed, sums, keep_a, send_a, keep_b, send_b,
    grad_pre, kept_hidden, kept_carried, grad_branch, flipped,
):
    step = pl.program_id(0)
    last_step = pl.num_programs(0) - 1
    width = after_first.shape[1]
    units = slope.shape[1]
    proj = 2 * units
    last = proj + carried.shape[2]
    chunk = 512
    rows = pl.ds(pl.multiple_of(step * ROWS, ROWS), ROWS)

    @pl.when(step == 0)
    def _():
        sums[...] = jnp.zeros(sums.shape, f32)

    grad_after = dot_nt(carried[0], weights[:, proj:last])
    sums[5:6, :] += column_sum(grad_after * branch_second[...].astype(f32))
    low = (grad_after * scales[5:6, :]).astype(bf16)
    grad_normed = jnp.zeros(grad_after.shape, f32)
    for left in range(0, units, chunk):
        grad_hidden = dot(low, weights[:, units + left : units + left + chunk])
        part = (grad_hidden * slope[:, left : left + chunk].astype(f32)).astype(bf16)
        grad_pre[rows, left : left + chunk] = part
        grad_normed = grad_normed + dot_nt(part, weights[:, left : left + chunk])
    normal, rstd = centre_rows(after_first[...])
    sums[2:3, :] += column_sum(grad_normed * normal)
    sums[3:4, :] += column_sum(grad_normed)
    grad_first = grad_after + norm_back(normal, rstd, scales[2:3, :], grad_normed)
    out_after[...] = grad_first
    sums[4:5, :] += column_sum(grad_first * branch_first[...].astype(f32))
    low_first = (grad_first * scales[4:5, :]).astype(bf16)
    grad_branch[rows, :] = low_first
    out_mixed[...] = dot_nt(low_first, weights[:, last : last + width]).astype(bf16)
    kept_hidden[rows, :] = hidden[...]
    kept_carried[rows, :] = carried[0]
    for index, block in enumerate((normed[...], low_out[...])):
        store_flipped(dests_a, rowmap_a, block, flipped.at[index], rows)
    for index, block in enumerate((low, mixed[...])):
        store_flipped(dests_b, rowmap_b, block, flipped.at[2 + index], rows)

    @pl.when(step == last_step)
    def _():
        for left in range(0, units, chunk):
            lanes = slice(left, left + chunk)
            store_halves(dot(flipped[0], grad_pre[:, lanes]), keep_a, send_a, lanes)
            store_halves(dot(flipped[2], kept_hidden[:, lanes]), keep_b, send_b, lanes)
        rest = slice(units, keep_a.shape[2])
        store_halves(dot(flipped[1], kept_carried[...]), keep_a, send_a, rest)
        rest = slice(units, keep_b.shape[2])
        store_halves(dot(flipped[3], grad_branch[...]), keep_b, send_b, rest)


def backward_call(
    orders, carried, branch_second, slope, after_first, branch_first, normed, hidden, low_out,
    mixed, scales, weights,
):
    count, width = after_first.shape
    units, depth = slope.shape[1], carried.shape[2]
    row = lambda size: pl.BlockSpec((ROWS, size), lambda i: (i, 0))
    pieces = [(1, width // 2, units + extra) for extra in (depth, depth, width, width)]
    (_, rowmap_a, dests_a), (_, rowmap_b, dests_b) = orders
    return pl.pallas_call(
        backward_kernel,
        grid=(count // ROWS,),
        in_specs=[smem(), whole(rowmap_a.shape)] * 2
        + [pl.BlockSpec((1, ROWS, depth), lambda i: (0, i, 0))]
        + [row(width), row(units), row(width), row(width), row(width), row(units), row(width)]
        + [row(width), whole(scales.shape), whole(weights.shape)],
        out_specs=[row(width), row(width), whole((8, width))] + [whole(piece) for piece in pieces],
        out_shape=[
            jax.ShapeDtypeStruct((count, width), f32),
            jax.ShapeDtypeStruct((count, width), bf16),
            jax.ShapeDtypeStruct((8, width), f32),
        ]
        + [jax.ShapeDtypeStruct(piece, bf16) for piece in pieces],
        scratch_shapes=[
            pltpu.VMEM((count, units), bf16),
            pltpu.VMEM((count, units), bf16),
            pltpu.VMEM((count, depth), bf16),
            pltpu.VMEM((count, width), bf16),
            pltpu.VMEM((4, width, count), bf16),
        ],
        compiler_params=params(56),
        cost_estimate=cost(2, 25),
        name="feed_back",
    )(
        dests_a, rowmap_a, dests_b, rowmap_b, carried, branch_second, slope, after_first, branch_first, normed, hidden,
        low_out, mixed, scales, weights,
    )


def attend_back_kernel(pieces, *refs):
    k_refs, v_refs = refs[:pieces], refs[pieces : 2 * pieces]
    (q, grad, logsum, bias, cosine, sine, start_k, start_v,
     grad_q, grad_k, grad_v, halo, k, v) = refs[2 * pieces :]
    step = pl.program_id(0)

    @pl.when(step == 0)
    def _():
        for index in range(pieces):
            rows = slice(index * MARGIN, (index + 1) * MARGIN)
            k[rows, :] = k_refs[index][...]
            v[rows, :] = v_refs[index][...]
        grad_k[:MARGIN, :] = start_k[...]
        grad_v[:MARGIN, :] = start_v[...]
        grad_k[MARGIN:, :] = jnp.zeros_like(grad_k[MARGIN:, :])
        grad_v[MARGIN:, :] = jnp.zeros_like(grad_v[MARGIN:, :])

    start = pl.multiple_of(step * QROWS, QROWS)
    keys = pl.ds(start, SPAN)
    allowed = jnp.concatenate([bias[0], bias[0]], axis=1)
    lane = lax.broadcasted_iota(jnp.int32, (QROWS, 128), 1)
    pairs = [slice(left, left + 128) for left in range(0, q.shape[1], 128)]
    records = [
        jnp.concatenate([logsum[h : h + 1, :], logsum[h + 1 : h + 2, :]], axis=1)
        for h in range(0, HEADS, 2)
    ]
    scores = [dot(k[keys, lanes], head_columns(flip(q[:, lanes]))) + allowed for lanes in pairs]
    grads = [dot(v[keys, lanes], head_columns(flip(grad[:, lanes]))) for lanes in pairs]
    weights = [jnp.exp(score - record) for score, record in zip(scores, records)]
    products = [weight * part for weight, part in zip(weights, grads)]
    inners = [column_sum(product) for product in products]
    grad_scores = [
        (product - weight * inner).astype(bf16)
        for product, weight, inner in zip(products, weights, inners)
    ]
    low = [weight.astype(bf16) for weight in weights]
    for lanes, weight in zip(pairs, low):
        grad_v[keys, lanes] += dot(weight, head_rows(grad[:, lanes]))
    for lanes, part in zip(pairs, grad_scores):
        grad_k[keys, lanes] += dot(part, head_rows(q[:, lanes]))
    joined = [dot(part, k[keys, lanes], ((0,), (0,))) for lanes, part in zip(pairs, grad_scores)]
    back = -sine[...]
    for lanes, part in zip(pairs, joined):
        flat = jnp.where(lane < 64, part[:QROWS], part[QROWS:]) * 0.125
        grad_q[:, lanes] = turn(flat, cosine[...], back).astype(bf16)

    @pl.when(step == pl.num_programs(0) - 1)
    def _():
        halo[:MARGIN, :] = grad_k[:MARGIN, :].astype(bf16)
        halo[MARGIN:, :] = grad_v[:MARGIN, :].astype(bf16)


def attend_back_call(offset, blocks, q, k, v, grad, logsum, bias, cosine, sine, start_k, start_v):
    width = q.shape[1]
    keys = blocks * QROWS + MARGIN
    lead = MARGIN // QROWS
    pieces = keys // MARGIN
    there = lambda i: (i + offset, 0)
    table = lambda i: (i + offset + lead, 0)
    fixed = lambda index: pl.BlockSpec((MARGIN, width), lambda i: (index, 0))
    return pl.pallas_call(
        lambda *refs: attend_back_kernel(pieces, *refs),
        grid=(blocks,),
        in_specs=[fixed(offset // lead + index) for index in range(pieces)] * 2
        + [
            pl.BlockSpec((QROWS, width), there),
            pl.BlockSpec((QROWS, width), there),
            pl.BlockSpec((HEADS, QROWS), lambda i: (0, i + offset)),
            pl.BlockSpec((1, SPAN, QROWS), lambda i: (i + offset, 0, 0)),
            pl.BlockSpec((QROWS, 128), table),
            pl.BlockSpec((QROWS, 128), table),
            fixed(start_k.shape[0] // MARGIN - 1),
            fixed(start_v.shape[0] // MARGIN - 1),
        ],
        out_specs=[
            pl.BlockSpec((QROWS, width), lambda i: (i, 0)),
            whole((keys, width)),
            whole((keys, width)),
            whole((2 * MARGIN, width)),
        ],
        out_shape=[
            jax.ShapeDtypeStruct((blocks * QROWS, width), bf16),
            jax.ShapeDtypeStruct((keys, width), f32),
            jax.ShapeDtypeStruct((keys, width), f32),
            jax.ShapeDtypeStruct((2 * MARGIN, width), bf16),
        ],
        scratch_shapes=[
            pltpu.VMEM((keys, width), bf16),
            pltpu.VMEM((keys, width), bf16),
        ],
        compiler_params=params(20),
        cost_estimate=cost(0 if offset > 0 else 8, 2 * blocks),
        name="attend_back",
    )(*[k] * pieces, *[v] * pieces, q, grad, logsum, bias, cosine, sine, start_k, start_v)


def finish_kernel(
    dests, rowmap, inputs, normed, q_a, q_b, q_c, k_a, k_b, v_a, v_b, halo, cosine, sine,
    grad_after, scales, sums_second, weights,
    out, keep_a, send_a, keep_b, send_b, flipped, turned_q, turned_k, turned_v, sums, tail,
):
    step = pl.program_id(0)
    last = pl.num_programs(0) - 1
    width = normed.shape[1]

    @pl.when(step == 0)
    def _():
        sums[...] = jnp.zeros(sums.shape, f32)
        sums[:8, :] = sums_second[...]
        left = 0
        for piece in (q_a, q_b, q_c):
            turned_q[left : left + piece.shape[0], :] = piece[...]
            left += piece.shape[0]

    rows = pl.ds(pl.multiple_of(step * ROWS, ROWS), ROWS)
    near = jnp.where(step == last, 1.0, 0.0).astype(f32)
    part_k = jnp.where(step == 0, k_a[...], k_b[...]) + near * halo[:MARGIN, :].astype(f32)
    part_v = jnp.where(step == 0, v_a[...], v_b[...]) + near * halo[MARGIN:, :].astype(f32)
    turned = turn(part_k, cosine[...], -sine[...]).astype(bf16)
    turned_k[rows, :] = turned
    value = part_v.astype(bf16)
    turned_v[rows, :] = value
    grad = dot_nt(turned_q[rows, :], weights[:, :width])
    grad = grad + dot_nt(turned, weights[:, width : 2 * width])
    grad = grad + dot_nt(value, weights[:, 2 * width : 3 * width])
    normal, rstd = centre_rows(inputs[...].astype(f32))
    sums[0:1, :] += column_sum(grad * normal)
    sums[1:2, :] += column_sum(grad)
    out[...] = grad_after[...] + norm_back(normal, rstd, scales[0:1, :], grad)

    store_flipped(dests, rowmap, normed[...], flipped, rows)

    @pl.when(step == last)
    def _():
        store_flipped(dests, rowmap, sums[...], tail, slice(None))
        parts = [dot(flipped[...], ref[...]).astype(bf16) for ref in (turned_q, turned_k, turned_v)]
        joined = jnp.concatenate(parts + [tail[...]], axis=1)
        split = keep_a.shape[2]
        half = keep_a.shape[1]
        keep_a[0], send_a[0] = joined[:half, :split], joined[half:, :split]
        keep_b[0], send_b[0] = joined[:half, split:], joined[half:, split:]


def finish_call(
    order, inputs, normed, grad_q, grad_k, grad_v, halo, cosine, sine,
    grad_after, scales, sums_second, weights,
):
    count, width = normed.shape
    _, rowmap, dests = order
    columns = 3 * width + 256
    row = pl.BlockSpec((ROWS, width), lambda i: (i, 0))
    first = pl.BlockSpec((ROWS, width), lambda i: (0, 0))
    rest = pl.BlockSpec((ROWS, width), lambda i: (jnp.maximum(i - 1, 0), 0))
    table = pl.BlockSpec((ROWS, 128), lambda i: (i + MARGIN // ROWS, 0))
    half = columns // 256 * 128
    shapes = [jax.ShapeDtypeStruct((count, width), f32)] + [
        jax.ShapeDtypeStruct((1, width // 2, size), bf16)
        for size in (half, half, columns - half, columns - half)
    ]
    return pl.pallas_call(
        finish_kernel,
        grid=(count // ROWS,),
        in_specs=[smem(), whole(rowmap.shape), row, row]
        + [whole(piece.shape) for piece in grad_q]
        + [first, rest, first, rest]
        + [whole(halo.shape), table, table, row]
        + [whole(scales.shape), whole(sums_second.shape), whole(weights.shape)],
        out_specs=[row] + [whole(shape.shape) for shape in shapes[1:]],
        out_shape=shapes,
        scratch_shapes=[
            pltpu.VMEM((width, count), bf16),
            pltpu.VMEM((count, width), bf16),
            pltpu.VMEM((count, width), bf16),
            pltpu.VMEM((count, width), bf16),
            pltpu.VMEM((256, width), f32),
            pltpu.VMEM((width, 256), bf16),
        ],
        compiler_params=params(32),
        cost_estimate=cost(0, 10),
        name="finish_rows",
    )(
        dests, rowmap, inputs, normed, *grad_q, *grad_k, *grad_v, halo, cosine, sine,
        grad_after, scales, sums_second, weights,
    )


def adam_update(master, first, second, gradient, factor, rate):
    clipped = gradient * factor
    momentum = beta_first * first + (1.0 - beta_first) * clipped
    variance = beta_second * second + (1.0 - beta_second) * clipped * clipped
    corrected = momentum / (1.0 - beta_first**STEP)
    divisor = jnp.sqrt(variance / (1.0 - beta_second**STEP)) + adam_floor
    updated = master - rate * (corrected / divisor + weight_decay * master)
    return (momentum, variance, updated, updated.astype(bf16))


def full_sum(values):
    return jnp.sum(jnp.sum(values, axis=0, keepdims=True), axis=1, keepdims=True)


def book_kernel(keep, *refs):
    parts, (out, length) = refs[:-2], refs[-2:]
    total = keep[...]
    for part in parts:
        total = total + part[...].astype(f32)
    out[...] = total
    length[...] = full_sum(jnp.sum(total * total, axis=0))


def book_call(keep, parts):
    return pl.pallas_call(
        book_kernel,
        grid=(1,),
        in_specs=[whole(keep.shape)] * (1 + len(parts)),
        out_specs=[whole(keep.shape), whole((1, 1))],
        out_shape=[
            jax.ShapeDtypeStruct(keep.shape, f32),
            jax.ShapeDtypeStruct((1, 1), f32),
        ],
        compiler_params=params(16),
        cost_estimate=cost(BOOK_SHARE, 1),
        name="book_sums",
    )(keep, *parts)


def total_kernel(groups, squares, *refs):
    outs, shared = refs[-1 - len(groups) : -1], refs[-1]
    length = squares[...]
    base = 0
    for size, out in zip(groups, outs):
        total = refs[base][0]
        for part in refs[base + 1 : base + size]:
            total = total + part[0].astype(f32)
        base += size
        out[...] = total
        length = length + full_sum(total * total)
    shared[...] = jnp.broadcast_to(length, shared.shape)


def total_call(squares, groups, count):
    operands = [array for keep, parts in groups for array in (keep, *parts)]
    sizes = [1 + len(parts) for _, parts in groups]
    shapes = [keep.shape[1:] for keep, _ in groups] + [(count, 128)]
    return pl.pallas_call(
        lambda *refs: total_kernel(sizes, *refs),
        grid=(1,),
        in_specs=[whole((1, 1))] + [whole(operand.shape) for operand in operands],
        out_specs=[whole(shape) for shape in shapes],
        out_shape=[jax.ShapeDtypeStruct(shape, f32) for shape in shapes],
        compiler_params=params(16),
        cost_estimate=cost(0, 1),
        name="last_sums",
    )(squares, *operands)


def adam_kernel(shared, grad_feed, grad_qkv, grad_book, *refs):
    masters, firsts, seconds = refs[0:15:3], refs[1:15:3], refs[2:15:3]
    norm_ref = refs[15]
    outs = [refs[16 + 4 * group : 20 + 4 * group] for group in range(5)]
    norm = jnp.sqrt(jnp.sum(shared[:, 0:1], axis=0, keepdims=True))
    norm_ref[...] = norm
    factor = clip_level / jnp.maximum(norm, clip_level)

    def update(group, index, gradient):
        results = adam_update(
            masters[group][index], firsts[group][index], seconds[group][index],
            gradient, factor, group_rates[group],
        )
        for out, result in zip(outs[group], results):
            out[index] = result

    width = (grad_qkv.shape[1] - 256) // 3
    units = masters[1].shape[2]
    depth = masters[2].shape[1]
    for k in range(3):
        update(0, k, grad_qkv[:, k * width : (k + 1) * width])
    middle = units + depth
    update(1, 0, grad_feed[:, :units])
    update(2, Ellipsis, grad_feed[:, units:middle])
    update(1, 1, grad_feed[:, middle : middle + units])
    update(0, 3, grad_feed[:, middle + units :])
    for level in range(LEVELS):
        update(3, level, grad_book[level])
    update(4, Ellipsis, grad_qkv[:, 3 * width :].T[:6])


def adam_call(shared, gradients, states):
    operands = [shared, *gradients] + [array for group in states for array in group]
    shapes = [jax.ShapeDtypeStruct((1, 1), f32)] + [
        jax.ShapeDtypeStruct(group[0].shape, kind)
        for group in states
        for kind in (f32, f32, f32, bf16)
    ]
    return pl.pallas_call(
        adam_kernel,
        grid=(1,),
        in_specs=[whole(operand.shape) for operand in operands],
        out_specs=[whole(shape.shape) for shape in shapes],
        out_shape=shapes,
        compiler_params=params(40),
        cost_estimate=cost(3, 2),
        name="adam_step",
    )(*operands)


def turn_tables(positions, depth):
    half = depth // 2
    freqs = jnp.exp(-math.log(10000.0) * jnp.arange(half, dtype=f32) * 2.0 / depth)
    angles = positions.astype(f32)[:, None] * freqs[None, :]
    cosine, sine = jnp.cos(angles), jnp.sin(angles)
    return (
        jnp.concatenate([cosine] * 4, axis=1),
        jnp.concatenate([-sine, sine, -sine, sine], axis=1),
    )


def score_bias(count, offset):
    block = jnp.arange(count // QROWS, dtype=jnp.int32)[:, None, None]
    key_place = jnp.arange(SPAN, dtype=jnp.int32)[None, :, None]
    query_place = jnp.arange(QROWS, dtype=jnp.int32)[None, None, :]
    distance = MARGIN + query_place - key_place
    reach = offset + block * QROWS + key_place - MARGIN
    allowed = (distance >= 0) & (distance <= WINDOW) & (reach >= 0)
    return jnp.where(allowed, 0.0, masked_score).astype(f32)


def body(
    inputs, codes, levels,
    attention_master, attention_first, attention_second,
    feedforward_master, feedforward_first, feedforward_second,
    projection_master, projection_first, projection_second,
    codebook_master, codebook_first, codebook_second,
    scales_master, scales_first, scales_second,
):
    spans = lax.axis_size("tm")
    devices = lax.axis_size("clip") * spans
    me = lax.axis_index("clip") * spans + lax.axis_index("tm")
    frame_count, width = inputs.shape
    units = feedforward_master.shape[2]
    depth = projection_master.shape[1]
    rows = projection_master.shape[0]
    entries = codebook_master.shape[1] * devices

    early, feed, book = lower_call(
        attention_master, feedforward_master, projection_master, codebook_master, scales_master
    )
    mid = LEVELS // 2
    book = lax.all_gather(book, AXES, axis=1, tiled=True)
    stages = len(digit_plan(devices, 3))
    split_stages = len(digit_plan(devices, 4))
    halo = lax.ppermute(
        inputs[frame_count - MARGIN :], "tm", [(i, i + 1) for i in range(spans - 1)]
    )
    for stage in reversed(range(2, len(digit_plan(devices, 2)))):
        early = join(early, gather_swaps(early, devices, 2, stage))
    mark = early
    for stage in reversed(range(4, split_stages)):
        feed = join(feed, after(gather_swaps(feed, devices, 4, stage), early))
    offset = lax.axis_index("tm") * frame_count
    positions = after(offset, mark) - MARGIN + jnp.arange(frame_count + MARGIN, dtype=jnp.int32)
    cosine, sine = turn_tables(positions, width // HEADS)
    bias = score_bias(frame_count, offset)
    def order(kind):
        owners = jnp.asarray(device_of_places(devices, kind)) ^ me
        starts = (owners * rows).astype(jnp.int32)
        if rows % 16 == 0:
            places = place_of(jnp.arange(devices, dtype=jnp.int32) ^ me, devices, kind)
            return starts, jnp.zeros((1, 128), jnp.int32), (places * rows).astype(jnp.int32)
        rowmap = (starts[:, None] + jnp.arange(rows, dtype=jnp.int32)[None, :]).reshape(1, width)
        return starts, rowmap, starts

    orders = {kind: order(kind) for kind in range(2, 6)}
    share = entries // devices
    owners = (codes // share) ^ me
    places = jnp.where(
        jnp.arange(LEVELS)[None, :] < mid,
        place_of(owners, devices, 4),
        place_of(owners, devices, 5),
    )
    places = (places * share + codes % share).astype(jnp.int32)
    flat_codes = jnp.concatenate([codes.T, places.T], axis=0)
    flat_codes, orders = after((flat_codes, orders), mark)
    ready = (cosine, sine, bias, flat_codes, orders)
    early = join(early, after(gather_swaps(early, devices, 2, 1), ready))
    come = after(gather_swaps(feed, devices, 4, 3), early)
    early_pieces = (early, swap(early, devices, 1))
    feed_a, feed_b = join(feed, come, (units, feed.shape[1] - units), 10)
    come_a = gather_swaps(feed_a, devices, 4, 2)
    come_b = gather_swaps(feed_b, devices, 5, 2)

    normed_first, q, k, v, scales, qkv_weights = qkv_call(
        *orders[2][:2], halo, inputs, early_pieces, cosine, sine
    )
    come_a, come_b = after((come_a, come_b), q)
    feed_a, feed_b = join(feed_a, come_a), join(feed_b, come_b)
    come_a = gather_swaps(feed_a, devices, 4, 1)
    come_b = gather_swaps(feed_b, devices, 5, 1)
    mixed, logsum = attend_call(q, after(k, feed_a, feed_b), v, bias)
    come_a, come_b = after((come_a, come_b), mixed)
    feed_a, feed_b = join(feed_a, come_a), join(feed_b, come_b)
    feed_pieces = (feed_a, swap(feed_a, devices, 1), feed_b, swap(feed_b, devices, 1))
    (
        branch_first, after_first, normed_second, hidden, slope, branch_second, low_out, latent,
        feed_weights,
    ) = forward_call((orders[4][:2], orders[5][:2]), inputs, mixed, scales, feed_pieces, units, depth)

    carried = fetch_call(levels, flat_codes, latent, book)
    keep_high, send_high = spread_call(mid, mid, flat_codes, carried, entries)
    come_high = swap_parts([send_high], devices, 5, 0)
    carried = after(carried, keep_high)
    keep_low, send_low = spread_call(0, mid, flat_codes, carried, entries)
    come_low = swap_parts([send_low], devices, 4, 0)
    high = reduce_split(keep_high, after(come_high, keep_low), devices, 5, 1, 0, bf16)
    low = reduce_split(keep_low, after(come_low, high[0]), devices, 4, 1, 0, bf16)

    grad_after, grad_mixed, sums_second, keep_a, send_a, keep_b, send_b = backward_call(
        (orders[4], orders[5]), after(carried, high[0], low[0]), branch_second, slope, after_first, branch_first,
        normed_second, hidden, low_out, mixed, scales, feed_weights,
    )
    come_a = swap_parts([send_a], devices, 4, 0)
    come_b = swap_parts([send_b], devices, 5, 0)
    come_low, come_high = after((low[1], high[1]), keep_a)
    low, high = pair_split((low[0], come_low), (high[0], come_high), devices, (4, 5), 2)

    lead = MARGIN // QROWS
    blocks = frame_count // QROWS
    zeros = jnp.zeros((MARGIN, width), f32)
    fixed = (logsum, bias, cosine, sine)
    grad_mixed = after(grad_mixed, low[0])
    q_a, k_a, v_a, halo = attend_back_call(0, lead, q, k, v, grad_mixed, *fixed, zeros, zeros)
    halo = lax.ppermute(halo, "tm", [(i + 1, i) for i in range(spans - 1)])
    come_a, come_b = after((come_a, come_b), k_a)
    keep_a, come_a = reduce_split(keep_a, come_a, devices, 4, 1)
    keep_b, come_b = reduce_split(keep_b, come_b, devices, 5, 1)
    grad_mixed = after(grad_mixed, keep_a, keep_b)
    q_b, k_b, v_b, _ = attend_back_call(lead, lead, q, k, v, grad_mixed, *fixed, k_a, v_a)
    come_low, come_high = after((low[1], high[1]), k_b)
    keep_book, come_book = stack_split((low[0], come_low), (high[0], come_high), devices, 4, 3)
    grad_mixed = after(grad_mixed, keep_book)
    q_c, k_c, v_c, _ = attend_back_call(
        2 * lead, blocks - 2 * lead, q, k, v, grad_mixed, *fixed, k_b, v_b
    )
    come_book, come_a, come_b = after((come_book, come_a, come_b), k_c)
    keep_a, come_a = reduce_split(keep_a, come_a, devices, 4, 2)
    keep_b, come_b = reduce_split(keep_b, come_b, devices, 5, 2)
    for stage in range(4, split_stages):
        keep_book, come_book = reduce_split(keep_book, come_book, devices, 4, stage)
    input_gradient, qkv_a, send_a, qkv_b, send_b = finish_call(
        orders[2], inputs, normed_first, (q_a, q_b, q_c),
        (k_b, after(k_c, keep_book, keep_a, keep_b)), (v_b, v_c), halo, cosine, sine, grad_after,
        scales, sums_second, qkv_weights,
    )
    send_a = swap_parts([send_a], devices, 2, 0)
    send_b = swap_parts([send_b], devices, 2, 0)
    grad_book, squares = book_call(keep_book, after(come_book, qkv_a))
    come_a, come_b = after((come_a, come_b), grad_book)
    keep_feed, come_feed = merge_split(
        ((keep_a, come_a), (keep_b, come_b)), devices, 4, 3, FEED_SHARE
    )
    send_a, send_b = after((send_a, send_b), keep_feed)
    keep_qkv, come_qkv = merge_split(((qkv_a, send_a), (qkv_b, send_b)), devices, 2, 1)
    for stage in range(4, split_stages):
        keep_feed, come_feed = reduce_split(keep_feed, come_feed, devices, 4, stage)
    for stage in range(2, len(digit_plan(devices, 2))):
        keep_qkv, come_qkv = reduce_split(keep_qkv, come_qkv, devices, 2, stage)
    grad_feed, grad_qkv, shared = total_call(
        squares, ((keep_feed, come_feed), (keep_qkv, come_qkv)), devices
    )

    shared = lax.all_to_all(shared, AXES, 0, 0, tiled=True)
    gradient_norm, *updated = adam_call(
        shared,
        (grad_feed, grad_qkv, grad_book),
        (
            (attention_master, attention_first, attention_second),
            (feedforward_master, feedforward_first, feedforward_second),
            (projection_master, projection_first, projection_second),
            (codebook_master, codebook_first, codebook_second),
            (scales_master, scales_first, scales_second),
        ),
    )
    return (latent, input_gradient, gradient_norm[0, 0], *updated)


def solution(mesh):
    rows = P(AXES, None)
    middle = P(None, AXES, None)
    scale = P(None, AXES)
    in_specs = (rows, rows, P("clip")) + (middle,) * 6 + (rows,) * 3 + (middle,) * 3 + (scale,) * 3
    out_specs = (rows, rows, P()) + (middle,) * 8 + (rows,) * 4 + (middle,) * 4 + (scale,) * 4
    return jax.shard_map(body, mesh=mesh, in_specs=in_specs, out_specs=out_specs, check_vma=False)
```

```python
import math

import jax
import jax.numpy as jnp
import numpy as np
from jax import lax
from jax.experimental import pallas as pl
from jax.experimental.pallas import tpu as pltpu
from jax.sharding import PartitionSpec as P

HEADS = 8
LEVELS = 8
WINDOW = 250
STEP = 10
AXES = ("clip", "tm")

clip_level = 1.0
beta_first = 0.9
beta_second = 0.95
adam_floor = 1e-08
weight_decay = 0.1
group_rates = (0.05, 0.03, 0.05, 0.5, 0.5)
masked_score = -1e30

f32 = jnp.float32
bf16 = jnp.bfloat16
MARGIN = (WINDOW + 127) // 128 * 128
QROWS = 128
SPAN = QROWS + MARGIN
ROWS = 256
MIB = 1 << 20
FEED_SHARE, BOOK_SHARE = 4, 2


def dot(left, right, contract=((1,), (0,))):
    return lax.dot_general(left, right, (contract, ((), ())), preferred_element_type=f32)


def dot_nt(left, right):
    return dot(left, right, ((1,), (1,)))


def flip(block):
    return block.astype(f32).T.astype(bf16)


def params(mib):
    return pltpu.CompilerParams(vmem_limit_bytes=mib * MIB)


def whole(shape):
    return pl.BlockSpec(tuple(shape), lambda *_: (0,) * len(shape))


def smem():
    return pl.BlockSpec(memory_space=pltpu.SMEM)


def cost(share, length=1):
    return pl.CostEstimate(flops=int(share * 500000000), bytes_accessed=length * 3 * MIB, transcendentals=0)


def after(value, *earlier):
    return lax.optimization_barrier((value, earlier))[0]


def digit_plan(count, kind):
    bits = count.bit_length() - 1
    middle = [(1, 4)] if kind < 4 else [(1, 2), (2, 2)] if kind == 4 else [(2, 2), (1, 2)]
    plan, shift = [(0, 2)] + middle, 3
    while shift < bits:
        width = min(2, bits - shift) if kind == 2 else 1
        plan.append((shift, 1 << width))
        shift += width
    return plan


def swap(block, count, mask):
    return lax.ppermute(block, AXES, [(i, i ^ mask) for i in range(count)])


def gather_swaps(block, count, kind, stage):
    shift, radix = digit_plan(count, kind)[stage]
    return [swap(block, count, k << shift) for k in range(1, radix)]


def join_kernel(count, widths, *refs):
    outs = refs[count:]
    top = 0
    for part in refs[:count]:
        rows, left = part.shape[0], 0
        for out, width in zip(outs, widths):
            out[top : top + rows, :] = part[:, left : left + width]
            left += width
        top += rows


def join(block, others, widths=None, share=0):
    parts = [block, *others]
    rows, columns = block.shape
    widths = widths or (columns,)
    if rows % 16:
        whole_block = jnp.concatenate(parts, axis=0)
        edges = [sum(widths[:index]) for index in range(len(widths) + 1)]
        outs = [whole_block[:, left:right] for left, right in zip(edges, edges[1:])]
    else:
        outs = pl.pallas_call(
            lambda *refs: join_kernel(len(parts), widths, *refs),
            grid=(1,),
            in_specs=[whole(part.shape) for part in parts],
            out_specs=[whole((len(parts) * rows, width)) for width in widths],
            out_shape=[
                jax.ShapeDtypeStruct((len(parts) * rows, width), block.dtype) for width in widths
            ],
            compiler_params=params(16),
            cost_estimate=cost(share, 1),
            name="join_rows",
        )(*parts)
    return outs[0] if len(widths) == 1 else outs


def place_of(device, count, kind):
    place, weight = 0, 1
    for shift, radix in reversed(digit_plan(count, kind)):
        place = place + ((device >> shift) & (radix - 1)) * weight
        weight *= radix
    return place


def device_of_places(count, kind):
    table = np.zeros(count, np.int32)
    for device in range(count):
        table[place_of(device, count, kind)] = device
    return table


def swap_parts(parts, count, kind, stage):
    shift, _ = digit_plan(count, kind)[stage]
    return [swap(part, count, (k + 1) << shift) for k, part in enumerate(parts)]


def reduce_add(keep, parts):
    total = keep.astype(f32)
    for part in parts:
        total = total + part.astype(f32)
    return total


def split_kernel(radix, *refs):
    outs, operands = refs[-radix:], refs[:-radix]
    total = operands[0][...].astype(f32)
    for operand in operands[1:]:
        total = total + operand[...].astype(f32)
    size = total.shape[1] // radix
    for k, out in enumerate(outs):
        out[...] = total[:, k * size : (k + 1) * size, :].astype(out.dtype)


def reduce_split(keep, parts, count, kind, stage, share=0, held=f32):
    _, radix = digit_plan(count, kind)[stage]
    lead, rows, columns = keep.shape
    size = rows // radix
    if lead > 1:
        steps, block, index = lead, (1, rows, columns), lambda i: (i, 0, 0)
    else:
        steps = 2 if columns % 256 == 0 else 1
        block, index = (1, rows, columns // steps), lambda i: (0, 0, i)
    shares = (block[0], size, block[2])
    kinds = [held] + [bf16] * (radix - 1)
    outs = pl.pallas_call(
        lambda *refs: split_kernel(radix, *refs),
        grid=(steps,),
        in_specs=[pl.BlockSpec(block, index)] * (1 + len(parts)),
        out_specs=[pl.BlockSpec(shares, index)] * radix,
        out_shape=[jax.ShapeDtypeStruct((lead, size, columns), kind) for kind in kinds],
        compiler_params=params(20),
        cost_estimate=cost(share, 1),
        name="split_sums",
    )(keep, *parts)
    return outs[0], swap_parts(outs[1:], count, kind, stage)


def merge_kernel(radix, groups, *refs):
    outs = refs[-radix:]
    base = left = 0
    for size in groups:
        total = refs[base][...].astype(f32)
        for operand in refs[base + 1 : base + size]:
            total = total + operand[...].astype(f32)
        base += size
        rows = total.shape[1] // radix
        for k, out in enumerate(outs):
            share = total[:, k * rows : (k + 1) * rows, :].astype(out.dtype)
            out[:, :, left : left + total.shape[2]] = share
        left += total.shape[2]


def merge_split(groups, count, kind, stage, share=0):
    _, radix = digit_plan(count, kind)[stage]
    operands = [array for keep, parts in groups for array in (keep, *parts)]
    _, rows, _ = groups[0][0].shape
    shape = (1, rows // radix, sum(keep.shape[2] for keep, _ in groups))
    sizes = [1 + len(parts) for _, parts in groups]
    kinds = [f32] + [bf16] * (radix - 1)
    outs = pl.pallas_call(
        lambda *refs: merge_kernel(radix, sizes, *refs),
        grid=(1,),
        in_specs=[whole(operand.shape) for operand in operands],
        out_specs=[whole(shape)] * radix,
        out_shape=[jax.ShapeDtypeStruct(shape, kind) for kind in kinds],
        compiler_params=params(20),
        cost_estimate=cost(share, 1),
        name="split_sums",
    )(*operands)
    return outs[0], swap_parts(outs[1:], count, kind, stage)


def stack_kernel(radix, half, *refs):
    outs, operands = refs[-radix:], refs[:-radix]
    size = operands[0].shape[1] // radix

    def add(parts):
        total = sum(part[...].astype(f32) for part in parts)
        for k, out in enumerate(outs):
            out[...] = total[:, k * size : (k + 1) * size, :].astype(out.dtype)

    @pl.when(pl.program_id(0) < half)
    def _():
        add(operands[: len(operands) // 2])

    @pl.when(pl.program_id(0) >= half)
    def _():
        add(operands[len(operands) // 2 :])


def stack_split(low, high, count, kind, stage, share=0):
    _, radix = digit_plan(count, kind)[stage]
    operands = [low[0], *low[1], high[0], *high[1]]
    half, rows, columns = low[0].shape
    kinds = [f32] + [bf16] * (radix - 1)
    block = (1, rows, columns)
    below = pl.BlockSpec(block, lambda i: (jnp.minimum(i, half - 1), 0, 0))
    above = pl.BlockSpec(block, lambda i: (jnp.maximum(i - half, 0), 0, 0))
    outs = pl.pallas_call(
        lambda *refs: stack_kernel(radix, half, *refs),
        grid=(2 * half,),
        in_specs=[below] * (1 + len(low[1])) + [above] * (1 + len(high[1])),
        out_specs=[pl.BlockSpec((1, rows // radix, columns), lambda i: (i, 0, 0))] * radix,
        out_shape=[
            jax.ShapeDtypeStruct((2 * half, rows // radix, columns), kind) for kind in kinds
        ],
        compiler_params=params(20),
        cost_estimate=cost(share, 2),
        name="split_sums",
    )(*operands)
    return outs[0], swap_parts(outs[1:], count, kind, stage)


def one_hot_rows(rowmap, size):
    place = lax.broadcasted_iota(jnp.int32, (size, size), 0)
    return jnp.where(place == rowmap, 1.0, 0.0).astype(bf16)


def unpack_rows(starts_ref, rowmap_ref, pieces, out_ref):
    half = pieces[0].shape[0]
    count = starts_ref.shape[0]
    rows = 2 * half // count
    if rows % 16 == 0:
        for place in range(count):
            piece = pieces[place * rows // half]
            inner = place * rows % half
            start = pl.multiple_of(starts_ref[place], rows)
            out_ref[pl.ds(start, rows), :] = piece[inner : inner + rows, :]
    else:
        spread = one_hot_rows(rowmap_ref[0:1, :], 2 * half)
        columns = out_ref.shape[1]
        for left in range(0, columns, 128):
            joined = jnp.concatenate([p[:, left : left + 128] for p in pieces], axis=0)
            out_ref[:, left : left + 128] = dot(spread, joined).astype(bf16)


def store_flipped(dests_ref, rowmap_ref, block, out_ref, lanes):
    flipped = flip(block)
    size = flipped.shape[0]
    count = dests_ref.shape[0]
    rows = size // count
    if rows % 16 == 0:
        for index in range(count):
            start = pl.multiple_of(dests_ref[index], rows)
            out_ref[pl.ds(start, rows), lanes] = flipped[index * rows : (index + 1) * rows]
    else:
        spread = one_hot_rows(rowmap_ref[0:1, :], size)
        out_ref[:, lanes] = dot(spread, flipped, ((0,), (0,))).astype(bf16)


def store_halves(values, keep, send, lanes):
    half = keep.shape[1]
    keep[0, :, lanes] = values[:half].astype(bf16)
    send[0, :, lanes] = values[half:].astype(bf16)


def centre_rows(values):
    centred = values - jnp.mean(values, axis=-1, keepdims=True)
    spread = jnp.mean(centred * centred, axis=-1, keepdims=True)
    rstd = lax.rsqrt(spread + 1e-05)
    return centred * rstd, rstd


def norm_back(normal, rstd, gain, grad):
    inner = grad * gain
    first = jnp.mean(inner, axis=-1, keepdims=True)
    second = jnp.mean(inner * normal, axis=-1, keepdims=True)
    return rstd * (inner - first - normal * second)


def column_sum(values):
    return jnp.sum(values, axis=0, keepdims=True)


def turn(values, cosine, sine):
    lanes = values.shape[1]
    ahead = pltpu.roll(values, lanes - 32, 1)
    behind = pltpu.roll(values, 32, 1)
    lane = lax.broadcasted_iota(jnp.int32, values.shape, 1)
    partner = jnp.where(lane % 64 < 32, ahead, behind)
    repeats = lanes // cosine.shape[1]
    if repeats > 1:
        cosine = jnp.concatenate([cosine] * repeats, axis=1)
        sine = jnp.concatenate([sine] * repeats, axis=1)
    return values * cosine + partner * sine


def head_columns(flipped):
    zero = jnp.zeros((64, flipped.shape[1]), flipped.dtype)
    return jnp.concatenate(
        [
            jnp.concatenate([flipped[:64], zero], axis=1),
            jnp.concatenate([zero, flipped[64:]], axis=1),
        ],
        axis=0,
    )


def head_rows(block):
    lane = lax.broadcasted_iota(jnp.int32, block.shape, 1)
    zero = jnp.zeros_like(block)
    return jnp.concatenate(
        [jnp.where(lane < 64, block, zero), jnp.where(lane < 64, zero, block)], axis=0
    )


def lower_kernel(attention, feed, projection, book, scales, early, later, low_book, work):
    width = attention.shape[2]
    units = feed.shape[2]
    rows = attention.shape[1]
    for k in range(3):
        early[:, k * width : (k + 1) * width] = attention[k].astype(bf16)
    work[...] = jnp.zeros(work.shape, f32)
    work[: scales.shape[0], :rows] = scales[...]
    early[:, 3 * width :] = work[...].T[:rows].astype(bf16)
    for k in range(2):
        later[:, k * units : (k + 1) * units] = feed[k].astype(bf16)
    last = 2 * units + projection.shape[1]
    later[:, 2 * units : last] = projection[...].astype(bf16)
    later[:, last:] = attention[3].astype(bf16)
    low_book[...] = book[...].astype(bf16)


def lower_call(attention, feed, projection, book, scales):
    _, rows, width = attention.shape
    columns = 2 * feed.shape[2] + projection.shape[1] + width
    shapes = ((rows, 3 * width + 128), (rows, columns), book.shape)
    operands = (attention, feed, projection, book, scales)
    return pl.pallas_call(
        lower_kernel,
        grid=(1,),
        in_specs=[whole(operand.shape) for operand in operands],
        out_specs=[whole(shape) for shape in shapes],
        out_shape=[jax.ShapeDtypeStruct(shape, bf16) for shape in shapes],
        scratch_shapes=[pltpu.VMEM((128, 128), f32)],
        compiler_params=params(62),
        cost_estimate=cost(0, 1),
        name="lower_weights",
    )(*operands)


def qkv_kernel(
    starts, rowmap, halo, inputs, piece_a, piece_b, cosine, sine, normed, q, k, v, scales, weights
):
    step = pl.program_id(0)
    width = inputs.shape[1]

    @pl.when(step == 0)
    def _():
        unpack_rows(starts, rowmap, (piece_a, piece_b), weights)
        scales[...] = weights[:, 3 * width :].astype(f32).T[:8]

    frames = jnp.where(step == 0, halo[...].astype(f32), inputs[...].astype(f32))
    normal, _ = centre_rows(frames)
    low = (normal * scales[0:1, :] + scales[1:2, :]).astype(bf16)
    normed[...] = low
    turned = turn(dot(low, weights[:, :width]), cosine[...], sine[...])
    q[...] = (turned.astype(bf16).astype(f32) * 0.125).astype(bf16)
    k[...] = turn(dot(low, weights[:, width : 2 * width]), cosine[...], sine[...]).astype(bf16)
    v[...] = dot(low, weights[:, 2 * width : 3 * width]).astype(bf16)


def qkv_call(starts, rowmap, halo, inputs, pieces, cosine, sine):
    count, width = inputs.shape
    columns = pieces[0].shape[1]
    steps = count // ROWS + 1
    late = lambda i: (jnp.maximum(i - 1, 0), 0)
    here = lambda i: (i, 0)
    return pl.pallas_call(
        qkv_kernel,
        grid=(steps,),
        in_specs=[
            smem(),
            whole(rowmap.shape),
            whole(halo.shape),
            pl.BlockSpec((ROWS, width), late),
            whole(pieces[0].shape),
            whole(pieces[1].shape),
            pl.BlockSpec((ROWS, 128), here),
            pl.BlockSpec((ROWS, 128), here),
        ],
        out_specs=[
            pl.BlockSpec((ROWS, width), late),
            pl.BlockSpec((ROWS, width), late),
            pl.BlockSpec((ROWS, width), here),
            pl.BlockSpec((ROWS, width), here),
            whole((8, width)),
            whole((width, columns)),
        ],
        out_shape=[
            jax.ShapeDtypeStruct((count, width), bf16),
            jax.ShapeDtypeStruct((count, width), bf16),
            jax.ShapeDtypeStruct((count + MARGIN, width), bf16),
            jax.ShapeDtypeStruct((count + MARGIN, width), bf16),
            jax.ShapeDtypeStruct((8, width), f32),
            jax.ShapeDtypeStruct((width, columns), bf16),
        ],
        compiler_params=params(32),
        cost_estimate=cost(4, 8),
        name="project_rows",
    )(starts, rowmap, halo, inputs, *pieces, cosine, sine)


def attend_kernel(q, k, v, bias, mixed, logsum):
    step = pl.program_id(0)
    start = pl.multiple_of(step * QROWS, QROWS)
    keys = pl.ds(start, SPAN)
    allowed = jnp.concatenate([bias[0], bias[0]], axis=1)
    lane = lax.broadcasted_iota(jnp.int32, (QROWS, 128), 1)
    pairs = [slice(left, left + 128) for left in range(0, q.shape[1], 128)]
    columns = [head_columns(flip(q[:, lanes])) for lanes in pairs]
    scores = [dot(k[keys, lanes], column) + allowed for lanes, column in zip(pairs, columns)]
    highest = [jnp.max(score, axis=0, keepdims=True) for score in scores]
    raised = [jnp.exp(score - high) for score, high in zip(scores, highest)]
    totals = [column_sum(part) for part in raised]
    weights = [(part * (1.0 / total)).astype(bf16) for part, total in zip(raised, totals)]
    outputs = [
        dot(weight, v[keys, lanes], ((0,), (0,))) for weight, lanes in zip(weights, pairs)
    ]
    rows = []
    for lanes, output, high, total in zip(pairs, outputs, highest, totals):
        mixed[:, lanes] = jnp.where(lane < 64, output[:QROWS], output[QROWS:]).astype(bf16)
        record = high + jnp.log(total)
        rows += [record[:, :QROWS], record[:, QROWS:]]
    logsum[...] = jnp.concatenate(rows, axis=0)


def attend_call(q, k, v, bias):
    count, width = q.shape
    return pl.pallas_call(
        attend_kernel,
        grid=(count // QROWS,),
        in_specs=[
            pl.BlockSpec((QROWS, width), lambda i: (i, 0)),
            whole(k.shape),
            whole(v.shape),
            pl.BlockSpec((1, SPAN, QROWS), lambda i: (i, 0, 0)),
        ],
        out_specs=[
            pl.BlockSpec((QROWS, width), lambda i: (i, 0)),
            pl.BlockSpec((HEADS, QROWS), lambda i: (0, i)),
        ],
        out_shape=[
            jax.ShapeDtypeStruct((count, width), bf16),
            jax.ShapeDtypeStruct((HEADS, count), f32),
        ],
        compiler_params=params(24),
        cost_estimate=cost(4, 14),
        name="attend_rows",
    )(q, k, v, bias)


def forward_kernel(
    starts_a, rowmap_a, starts_b, rowmap_b, inputs, mixed, scales, own_a, other_a, own_b, other_b,
    branch_first, after_first, normed, hidden, slope, branch_second, low_out, latent, again, weights,
):
    step = pl.program_id(0)
    width = inputs.shape[1]
    units = hidden.shape[1]

    @pl.when(step == 0)
    def _():
        unpack_rows(starts_a, rowmap_a, (own_a, other_a), weights.at[:, :units])
        unpack_rows(starts_b, rowmap_b, (own_b, other_b), weights.at[:, units:])

    up, down = 0, units
    proj = 2 * units
    last = proj + latent.shape[1]
    first = dot(mixed[...], weights[:, last : last + width])
    branch_first[...] = first.astype(bf16)
    after = inputs[...].astype(f32) + scales[4:5, :] * first
    after_first[...] = after
    normal, _ = centre_rows(after)
    low = (normal * scales[2:3, :] + scales[3:4, :]).astype(bf16)
    normed[...] = low
    chunk = 512
    lefts = range(0, units, chunk)
    pres = [dot(low, weights[:, up + left : up + left + chunk]) for left in lefts]
    for left, pre in zip(lefts, pres):
        share = 0.5 + 0.5 * lax.erf(pre * (1.0 / math.sqrt(2.0)))
        bell = jnp.exp(-0.5 * pre * pre) * (1.0 / math.sqrt(2.0 * math.pi))
        hidden[:, left : left + chunk] = (pre * share).astype(bf16)
        slope[:, left : left + chunk] = (share + pre * bell).astype(bf16)
    second = dot_nt(hidden[...], weights[:, down : down + units])
    branch_second[...] = second.astype(bf16)
    rounded = (after + scales[5:6, :] * second).astype(bf16)
    low_out[...] = rounded
    result = dot(rounded, weights[:, proj:last])
    latent[...] = result
    again[...] = result


def forward_call(orders, inputs, mixed, scales, pieces, units, depth):
    count, width = inputs.shape
    columns = pieces[0].shape[1] + pieces[2].shape[1]
    row = lambda size: pl.BlockSpec((ROWS, size), lambda i: (i, 0))
    kept = ((width, bf16), (width, f32), (width, bf16), (units, bf16), (units, bf16),
            (width, bf16), (width, bf16), (depth, f32), (depth, f32))
    (starts_a, rowmap_a), (starts_b, rowmap_b) = orders
    return pl.pallas_call(
        forward_kernel,
        grid=(count // ROWS,),
        in_specs=[smem(), whole(rowmap_a.shape)] * 2
        + [row(width), row(width), whole(scales.shape)]
        + [whole(piece.shape) for piece in pieces],
        out_specs=[row(size) for size, _ in kept] + [whole((width, columns))],
        out_shape=[jax.ShapeDtypeStruct((count, size), kind) for size, kind in kept]
        + [jax.ShapeDtypeStruct((width, columns), bf16)],
        compiler_params=params(56),
        cost_estimate=cost(4, 17),
        name="feed_rows",
    )(starts_a, rowmap_a, starts_b, rowmap_b, inputs, mixed, scales, *pieces)


def fetch_kernel(active, codes, latent, book, carried, residue, steps, columns):
    level = pl.program_id(0)
    count, depth = latent.shape
    tiles = book.shape[1] // 256

    @pl.when(level == 0)
    def _():
        residue[...] = latent[...]
        columns[...] = codes[:LEVELS, :].astype(f32).T

    factor = jnp.where(level < active[0], 1.0, 0.0).astype(f32)
    lane = lax.broadcasted_iota(jnp.int32, (ROWS, LEVELS), 1)
    place = lax.broadcasted_iota(jnp.int32, (ROWS, 256), 1).astype(f32)
    blocks = [slice(top, top + ROWS) for top in range(0, count, ROWS)]
    picked = []
    for rows in blocks:
        code = jnp.where(lane == level, columns[rows, :], 0.0)
        code = jnp.sum(code, axis=1, keepdims=True)
        high = jnp.floor(code * (1.0 / 256.0))
        hit = jnp.where(place == code - 256.0 * high, 1.0, 0.0).astype(bf16)
        picks = [hit * jnp.where(high == j, 1.0, 0.0).astype(bf16) for j in range(tiles)]
        picked.append(jnp.concatenate(picks, axis=1))
    found = [dot(pick, book[0]) for pick in picked]
    for rows, row in zip(blocks, found):
        left = residue[rows, :] - factor * row
        residue[rows, :] = left
        steps[level, rows, :] = factor * left

    @pl.when(level == LEVELS - 1)
    def _():
        for top in range(0, count, ROWS):
            rows = slice(top, top + ROWS)
            total = jnp.zeros((ROWS, depth), f32)
            for index in reversed(range(LEVELS)):
                total = total + steps[index, rows, :]
                carried[index, rows, :] = total.astype(bf16)


def fetch_call(active, codes, latent, book):
    count, depth = latent.shape
    entries = book.shape[1]
    return pl.pallas_call(
        fetch_kernel,
        grid=(LEVELS,),
        in_specs=[
            smem(),
            whole(codes.shape),
            whole(latent.shape),
            pl.BlockSpec((1, entries, depth), lambda i: (i, 0, 0)),
        ],
        out_specs=whole((LEVELS, count, depth)),
        out_shape=jax.ShapeDtypeStruct((LEVELS, count, depth), bf16),
        scratch_shapes=[
            pltpu.VMEM((count, depth), f32),
            pltpu.VMEM((LEVELS, count, depth), f32),
            pltpu.VMEM((count, LEVELS), f32),
        ],
        compiler_params=params(48),
        cost_estimate=cost(4, 13),
        name="fetch_codes",
    )(active, codes, latent, book)


def spread_kernel(first, codes, carried, keep, send):
    count = carried.shape[1]
    half = keep.shape[1]
    level = pl.program_id(0) + first
    code = codes[pl.ds(LEVELS + level, 1), :]
    high = code >> 8
    place = lax.broadcasted_iota(jnp.int32, (256, count), 0)
    hit = jnp.where(place == (code & 255), -1.0, 0.0).astype(bf16)
    for j in range(2 * half // 256):
        pick = hit * jnp.where(high == j, 1.0, 0.0).astype(bf16)
        out, inner = (keep, send)[j * 256 // half], j * 256 % half
        out[0, inner : inner + 256, :] = dot(pick, carried[0]).astype(bf16)


def spread_call(first, levels, codes, carried, entries):
    _, count, depth = carried.shape
    half = entries // 2
    return pl.pallas_call(
        lambda *refs: spread_kernel(first, *refs),
        grid=(levels,),
        in_specs=[
            whole(codes.shape),
            pl.BlockSpec((1, count, depth), lambda i: (i + first, 0, 0)),
        ],
        out_specs=[pl.BlockSpec((1, half, depth), lambda i: (i, 0, 0))] * 2,
        out_shape=[jax.ShapeDtypeStruct((levels, half, depth), bf16)] * 2,
        compiler_params=params(16),
        cost_estimate=cost(1, 5),
        name="spread_codes",
    )(codes, carried)


def backward_kernel(
    dests_a, rowmap_a, dests_b, rowmap_b, carried, branch_second, slope, after_first, branch_first, normed, hidden, low_out, mixed,
    scales, weights,
    out_after, out_mixed, sums, keep_a, send_a, keep_b, send_b,
    grad_pre, kept_hidden, kept_carried, grad_branch, flipped,
):
    step = pl.program_id(0)
    last_step = pl.num_programs(0) - 1
    width = after_first.shape[1]
    units = slope.shape[1]
    proj = 2 * units
    last = proj + carried.shape[2]
    chunk = 512
    rows = pl.ds(pl.multiple_of(step * ROWS, ROWS), ROWS)

    @pl.when(step == 0)
    def _():
        sums[...] = jnp.zeros(sums.shape, f32)

    grad_after = dot_nt(carried[0], weights[:, proj:last])
    sums[5:6, :] += column_sum(grad_after * branch_second[...].astype(f32))
    low = (grad_after * scales[5:6, :]).astype(bf16)
    grad_normed = jnp.zeros(grad_after.shape, f32)
    for left in range(0, units, chunk):
        grad_hidden = dot(low, weights[:, units + left : units + left + chunk])
        part = (grad_hidden * slope[:, left : left + chunk].astype(f32)).astype(bf16)
        grad_pre[rows, left : left + chunk] = part
        grad_normed = grad_normed + dot_nt(part, weights[:, left : left + chunk])
    normal, rstd = centre_rows(after_first[...])
    sums[2:3, :] += column_sum(grad_normed * normal)
    sums[3:4, :] += column_sum(grad_normed)
    grad_first = grad_after + norm_back(normal, rstd, scales[2:3, :], grad_normed)
    out_after[...] = grad_first
    sums[4:5, :] += column_sum(grad_first * branch_first[...].astype(f32))
    low_first = (grad_first * scales[4:5, :]).astype(bf16)
    grad_branch[rows, :] = low_first
    out_mixed[...] = dot_nt(low_first, weights[:, last : last + width]).astype(bf16)
    kept_hidden[rows, :] = hidden[...]
    kept_carried[rows, :] = carried[0]
    for index, block in enumerate((normed[...], low_out[...])):
        store_flipped(dests_a, rowmap_a, block, flipped.at[index], rows)
    for index, block in enumerate((low, mixed[...])):
        store_flipped(dests_b, rowmap_b, block, flipped.at[2 + index], rows)

    @pl.when(step == last_step)
    def _():
        for left in range(0, units, chunk):
            lanes = slice(left, left + chunk)
            store_halves(dot(flipped[0], grad_pre[:, lanes]), keep_a, send_a, lanes)
            store_halves(dot(flipped[2], kept_hidden[:, lanes]), keep_b, send_b, lanes)
        rest = slice(units, keep_a.shape[2])
        store_halves(dot(flipped[1], kept_carried[...]), keep_a, send_a, rest)
        rest = slice(units, keep_b.shape[2])
        store_halves(dot(flipped[3], grad_branch[...]), keep_b, send_b, rest)


def backward_call(
    orders, carried, branch_second, slope, after_first, branch_first, normed, hidden, low_out,
    mixed, scales, weights,
):
    count, width = after_first.shape
    units, depth = slope.shape[1], carried.shape[2]
    row = lambda size: pl.BlockSpec((ROWS, size), lambda i: (i, 0))
    pieces = [(1, width // 2, units + extra) for extra in (depth, depth, width, width)]
    (_, rowmap_a, dests_a), (_, rowmap_b, dests_b) = orders
    return pl.pallas_call(
        backward_kernel,
        grid=(count // ROWS,),
        in_specs=[smem(), whole(rowmap_a.shape)] * 2
        + [pl.BlockSpec((1, ROWS, depth), lambda i: (0, i, 0))]
        + [row(width), row(units), row(width), row(width), row(width), row(units), row(width)]
        + [row(width), whole(scales.shape), whole(weights.shape)],
        out_specs=[row(width), row(width), whole((8, width))] + [whole(piece) for piece in pieces],
        out_shape=[
            jax.ShapeDtypeStruct((count, width), f32),
            jax.ShapeDtypeStruct((count, width), bf16),
            jax.ShapeDtypeStruct((8, width), f32),
        ]
        + [jax.ShapeDtypeStruct(piece, bf16) for piece in pieces],
        scratch_shapes=[
            pltpu.VMEM((count, units), bf16),
            pltpu.VMEM((count, units), bf16),
            pltpu.VMEM((count, depth), bf16),
            pltpu.VMEM((count, width), bf16),
            pltpu.VMEM((4, width, count), bf16),
        ],
        compiler_params=params(56),
        cost_estimate=cost(2, 25),
        name="feed_back",
    )(
        dests_a, rowmap_a, dests_b, rowmap_b, carried, branch_second, slope, after_first, branch_first, normed, hidden,
        low_out, mixed, scales, weights,
    )


def attend_back_kernel(pieces, *refs):
    k_refs, v_refs = refs[:pieces], refs[pieces : 2 * pieces]
    (q, grad, logsum, bias, cosine, sine, start_k, start_v,
     grad_q, grad_k, grad_v, halo, k, v) = refs[2 * pieces :]
    step = pl.program_id(0)

    @pl.when(step == 0)
    def _():
        for index in range(pieces):
            rows = slice(index * MARGIN, (index + 1) * MARGIN)
            k[rows, :] = k_refs[index][...]
            v[rows, :] = v_refs[index][...]
        grad_k[:MARGIN, :] = start_k[...]
        grad_v[:MARGIN, :] = start_v[...]
        grad_k[MARGIN:, :] = jnp.zeros_like(grad_k[MARGIN:, :])
        grad_v[MARGIN:, :] = jnp.zeros_like(grad_v[MARGIN:, :])

    start = pl.multiple_of(step * QROWS, QROWS)
    keys = pl.ds(start, SPAN)
    allowed = jnp.concatenate([bias[0], bias[0]], axis=1)
    lane = lax.broadcasted_iota(jnp.int32, (QROWS, 128), 1)
    pairs = [slice(left, left + 128) for left in range(0, q.shape[1], 128)]
    records = [
        jnp.concatenate([logsum[h : h + 1, :], logsum[h + 1 : h + 2, :]], axis=1)
        for h in range(0, HEADS, 2)
    ]
    scores = [dot(k[keys, lanes], head_columns(flip(q[:, lanes]))) + allowed for lanes in pairs]
    grads = [dot(v[keys, lanes], head_columns(flip(grad[:, lanes]))) for lanes in pairs]
    weights = [jnp.exp(score - record) for score, record in zip(scores, records)]
    products = [weight * part for weight, part in zip(weights, grads)]
    inners = [column_sum(product) for product in products]
    grad_scores = [
        (product - weight * inner).astype(bf16)
        for product, weight, inner in zip(products, weights, inners)
    ]
    low = [weight.astype(bf16) for weight in weights]
    for lanes, weight in zip(pairs, low):
        grad_v[keys, lanes] += dot(weight, head_rows(grad[:, lanes]))
    for lanes, part in zip(pairs, grad_scores):
        grad_k[keys, lanes] += dot(part, head_rows(q[:, lanes]))
    joined = [dot(part, k[keys, lanes], ((0,), (0,))) for lanes, part in zip(pairs, grad_scores)]
    back = -sine[...]
    for lanes, part in zip(pairs, joined):
        flat = jnp.where(lane < 64, part[:QROWS], part[QROWS:]) * 0.125
        grad_q[:, lanes] = turn(flat, cosine[...], back).astype(bf16)

    @pl.when(step == pl.num_programs(0) - 1)
    def _():
        halo[:MARGIN, :] = grad_k[:MARGIN, :].astype(bf16)
        halo[MARGIN:, :] = grad_v[:MARGIN, :].astype(bf16)


def attend_back_call(offset, blocks, q, k, v, grad, logsum, bias, cosine, sine, start_k, start_v):
    width = q.shape[1]
    keys = blocks * QROWS + MARGIN
    lead = MARGIN // QROWS
    pieces = keys // MARGIN
    there = lambda i: (i + offset, 0)
    table = lambda i: (i + offset + lead, 0)
    fixed = lambda index: pl.BlockSpec((MARGIN, width), lambda i: (index, 0))
    return pl.pallas_call(
        lambda *refs: attend_back_kernel(pieces, *refs),
        grid=(blocks,),
        in_specs=[fixed(offset // lead + index) for index in range(pieces)] * 2
        + [
            pl.BlockSpec((QROWS, width), there),
            pl.BlockSpec((QROWS, width), there),
            pl.BlockSpec((HEADS, QROWS), lambda i: (0, i + offset)),
            pl.BlockSpec((1, SPAN, QROWS), lambda i: (i + offset, 0, 0)),
            pl.BlockSpec((QROWS, 128), table),
            pl.BlockSpec((QROWS, 128), table),
            fixed(start_k.shape[0] // MARGIN - 1),
            fixed(start_v.shape[0] // MARGIN - 1),
        ],
        out_specs=[
            pl.BlockSpec((QROWS, width), lambda i: (i, 0)),
            whole((keys, width)),
            whole((keys, width)),
            whole((2 * MARGIN, width)),
        ],
        out_shape=[
            jax.ShapeDtypeStruct((blocks * QROWS, width), bf16),
            jax.ShapeDtypeStruct((keys, width), f32),
            jax.ShapeDtypeStruct((keys, width), f32),
            jax.ShapeDtypeStruct((2 * MARGIN, width), bf16),
        ],
        scratch_shapes=[
            pltpu.VMEM((keys, width), bf16),
            pltpu.VMEM((keys, width), bf16),
        ],
        compiler_params=params(20),
        cost_estimate=cost(0 if offset > 0 else 8, 2 * blocks),
        name="attend_back",
    )(*[k] * pieces, *[v] * pieces, q, grad, logsum, bias, cosine, sine, start_k, start_v)


def finish_kernel(
    dests, rowmap, inputs, normed, q_a, q_b, q_c, k_a, k_b, v_a, v_b, halo, cosine, sine,
    grad_after, scales, sums_second, weights,
    out, keep_a, send_a, keep_b, send_b, flipped, turned_q, turned_k, turned_v, sums, tail,
):
    step = pl.program_id(0)
    last = pl.num_programs(0) - 1
    width = normed.shape[1]

    @pl.when(step == 0)
    def _():
        sums[...] = jnp.zeros(sums.shape, f32)
        sums[:8, :] = sums_second[...]
        left = 0
        for piece in (q_a, q_b, q_c):
            turned_q[left : left + piece.shape[0], :] = piece[...]
            left += piece.shape[0]

    rows = pl.ds(pl.multiple_of(step * ROWS, ROWS), ROWS)
    near = jnp.where(step == last, 1.0, 0.0).astype(f32)
    part_k = jnp.where(step == 0, k_a[...], k_b[...]) + near * halo[:MARGIN, :].astype(f32)
    part_v = jnp.where(step == 0, v_a[...], v_b[...]) + near * halo[MARGIN:, :].astype(f32)
    turned = turn(part_k, cosine[...], -sine[...]).astype(bf16)
    turned_k[rows, :] = turned
    value = part_v.astype(bf16)
    turned_v[rows, :] = value
    grad = dot_nt(turned_q[rows, :], weights[:, :width])
    grad = grad + dot_nt(turned, weights[:, width : 2 * width])
    grad = grad + dot_nt(value, weights[:, 2 * width : 3 * width])
    normal, rstd = centre_rows(inputs[...].astype(f32))
    sums[0:1, :] += column_sum(grad * normal)
    sums[1:2, :] += column_sum(grad)
    out[...] = grad_after[...] + norm_back(normal, rstd, scales[0:1, :], grad)

    store_flipped(dests, rowmap, normed[...], flipped, rows)

    @pl.when(step == last)
    def _():
        store_flipped(dests, rowmap, sums[...], tail, slice(None))
        parts = [dot(flipped[...], ref[...]).astype(bf16) for ref in (turned_q, turned_k, turned_v)]
        joined = jnp.concatenate(parts + [tail[...]], axis=1)
        split = keep_a.shape[2]
        half = keep_a.shape[1]
        keep_a[0], send_a[0] = joined[:half, :split], joined[half:, :split]
        keep_b[0], send_b[0] = joined[:half, split:], joined[half:, split:]


def finish_call(
    order, inputs, normed, grad_q, grad_k, grad_v, halo, cosine, sine,
    grad_after, scales, sums_second, weights,
):
    count, width = normed.shape
    _, rowmap, dests = order
    columns = 3 * width + 128
    row = pl.BlockSpec((ROWS, width), lambda i: (i, 0))
    first = pl.BlockSpec((ROWS, width), lambda i: (0, 0))
    rest = pl.BlockSpec((ROWS, width), lambda i: (jnp.maximum(i - 1, 0), 0))
    table = pl.BlockSpec((ROWS, 128), lambda i: (i + MARGIN // ROWS, 0))
    half = columns // 256 * 128
    shapes = [jax.ShapeDtypeStruct((count, width), f32)] + [
        jax.ShapeDtypeStruct((1, width // 2, size), bf16)
        for size in (half, half, columns - half, columns - half)
    ]
    return pl.pallas_call(
        finish_kernel,
        grid=(count // ROWS,),
        in_specs=[smem(), whole(rowmap.shape), row, row]
        + [whole(piece.shape) for piece in grad_q]
        + [first, rest, first, rest]
        + [whole(halo.shape), table, table, row]
        + [whole(scales.shape), whole(sums_second.shape), whole(weights.shape)],
        out_specs=[row] + [whole(shape.shape) for shape in shapes[1:]],
        out_shape=shapes,
        scratch_shapes=[
            pltpu.VMEM((width, count), bf16),
            pltpu.VMEM((count, width), bf16),
            pltpu.VMEM((count, width), bf16),
            pltpu.VMEM((count, width), bf16),
            pltpu.VMEM((128, width), f32),
            pltpu.VMEM((width, 128), bf16),
        ],
        compiler_params=params(32),
        cost_estimate=cost(0, 10),
        name="finish_rows",
    )(
        dests, rowmap, inputs, normed, *grad_q, *grad_k, *grad_v, halo, cosine, sine,
        grad_after, scales, sums_second, weights,
    )


def adam_update(master, first, second, gradient, factor, rate):
    clipped = gradient * factor
    momentum = beta_first * first + (1.0 - beta_first) * clipped
    variance = beta_second * second + (1.0 - beta_second) * clipped * clipped
    corrected = momentum / (1.0 - beta_first**STEP)
    divisor = jnp.sqrt(variance / (1.0 - beta_second**STEP)) + adam_floor
    updated = master - rate * (corrected / divisor + weight_decay * master)
    return (momentum, variance, updated, updated.astype(bf16))


def full_sum(values):
    return jnp.sum(jnp.sum(values, axis=0, keepdims=True), axis=1, keepdims=True)


def book_kernel(keep, *refs):
    parts, (out, length) = refs[:-2], refs[-2:]
    total = keep[...]
    for part in parts:
        total = total + part[...].astype(f32)
    out[...] = total
    length[...] = full_sum(jnp.sum(total * total, axis=0))


def book_call(keep, parts):
    return pl.pallas_call(
        book_kernel,
        grid=(1,),
        in_specs=[whole(keep.shape)] * (1 + len(parts)),
        out_specs=[whole(keep.shape), whole((1, 1))],
        out_shape=[
            jax.ShapeDtypeStruct(keep.shape, f32),
            jax.ShapeDtypeStruct((1, 1), f32),
        ],
        compiler_params=params(16),
        cost_estimate=cost(BOOK_SHARE, 1),
        name="book_sums",
    )(keep, *parts)


def total_kernel(groups, squares, *refs):
    outs, shared = refs[-1 - len(groups) : -1], refs[-1]
    length = squares[...]
    base = 0
    for size, out in zip(groups, outs):
        total = refs[base][0]
        for part in refs[base + 1 : base + size]:
            total = total + part[0].astype(f32)
        base += size
        out[...] = total
        length = length + full_sum(total * total)
    shared[...] = jnp.broadcast_to(length, shared.shape)


def total_call(squares, groups, count):
    operands = [array for keep, parts in groups for array in (keep, *parts)]
    sizes = [1 + len(parts) for _, parts in groups]
    shapes = [keep.shape[1:] for keep, _ in groups] + [(count, 128)]
    return pl.pallas_call(
        lambda *refs: total_kernel(sizes, *refs),
        grid=(1,),
        in_specs=[whole((1, 1))] + [whole(operand.shape) for operand in operands],
        out_specs=[whole(shape) for shape in shapes],
        out_shape=[jax.ShapeDtypeStruct(shape, f32) for shape in shapes],
        compiler_params=params(16),
        cost_estimate=cost(0, 1),
        name="last_sums",
    )(squares, *operands)


def adam_kernel(shared, grad_feed, grad_qkv, grad_book, *refs):
    masters, firsts, seconds = refs[0:15:3], refs[1:15:3], refs[2:15:3]
    norm_ref = refs[15]
    outs = [refs[16 + 4 * group : 20 + 4 * group] for group in range(5)]
    norm = jnp.sqrt(jnp.sum(shared[:, 0:1], axis=0, keepdims=True))
    norm_ref[...] = norm
    factor = clip_level / jnp.maximum(norm, clip_level)

    def update(group, index, gradient):
        results = adam_update(
            masters[group][index], firsts[group][index], seconds[group][index],
            gradient, factor, group_rates[group],
        )
        for out, result in zip(outs[group], results):
            out[index] = result

    width = (grad_qkv.shape[1] - 128) // 3
    units = masters[1].shape[2]
    depth = masters[2].shape[1]
    for k in range(3):
        update(0, k, grad_qkv[:, k * width : (k + 1) * width])
    middle = units + depth
    update(1, 0, grad_feed[:, :units])
    update(2, Ellipsis, grad_feed[:, units:middle])
    update(1, 1, grad_feed[:, middle : middle + units])
    update(0, 3, grad_feed[:, middle + units :])
    for level in range(LEVELS):
        update(3, level, grad_book[level])
    update(4, Ellipsis, grad_qkv[:, 3 * width :].T[:6])


def adam_call(shared, gradients, states):
    operands = [shared, *gradients] + [array for group in states for array in group]
    shapes = [jax.ShapeDtypeStruct((1, 1), f32)] + [
        jax.ShapeDtypeStruct(group[0].shape, kind)
        for group in states
        for kind in (f32, f32, f32, bf16)
    ]
    return pl.pallas_call(
        adam_kernel,
        grid=(1,),
        in_specs=[whole(operand.shape) for operand in operands],
        out_specs=[whole(shape.shape) for shape in shapes],
        out_shape=shapes,
        compiler_params=params(40),
        cost_estimate=cost(3, 2),
        name="adam_step",
    )(*operands)


def turn_tables(positions, depth):
    half = depth // 2
    freqs = jnp.exp(-math.log(10000.0) * jnp.arange(half, dtype=f32) * 2.0 / depth)
    angles = positions.astype(f32)[:, None] * freqs[None, :]
    cosine, sine = jnp.cos(angles), jnp.sin(angles)
    return (
        jnp.concatenate([cosine] * 4, axis=1),
        jnp.concatenate([-sine, sine, -sine, sine], axis=1),
    )


def score_bias(count, offset):
    block = jnp.arange(count // QROWS, dtype=jnp.int32)[:, None, None]
    key_place = jnp.arange(SPAN, dtype=jnp.int32)[None, :, None]
    query_place = jnp.arange(QROWS, dtype=jnp.int32)[None, None, :]
    distance = MARGIN + query_place - key_place
    reach = offset + block * QROWS + key_place - MARGIN
    allowed = (distance >= 0) & (distance <= WINDOW) & (reach >= 0)
    return jnp.where(allowed, 0.0, masked_score).astype(f32)


def body(
    inputs, codes, levels,
    attention_master, attention_first, attention_second,
    feedforward_master, feedforward_first, feedforward_second,
    projection_master, projection_first, projection_second,
    codebook_master, codebook_first, codebook_second,
    scales_master, scales_first, scales_second,
):
    spans = lax.axis_size("tm")
    devices = lax.axis_size("clip") * spans
    me = lax.axis_index("clip") * spans + lax.axis_index("tm")
    frame_count, width = inputs.shape
    units = feedforward_master.shape[2]
    depth = projection_master.shape[1]
    rows = projection_master.shape[0]
    entries = codebook_master.shape[1] * devices

    early, feed, book = lower_call(
        attention_master, feedforward_master, projection_master, codebook_master, scales_master
    )
    mid = LEVELS // 2
    book = lax.all_gather(book, AXES, axis=1, tiled=True)
    stages = len(digit_plan(devices, 3))
    split_stages = len(digit_plan(devices, 4))
    halo = lax.ppermute(
        inputs[frame_count - MARGIN :], "tm", [(i, i + 1) for i in range(spans - 1)]
    )
    for stage in reversed(range(2, len(digit_plan(devices, 2)))):
        early = join(early, gather_swaps(early, devices, 2, stage))
    mark = early
    for stage in reversed(range(4, split_stages)):
        feed = join(feed, after(gather_swaps(feed, devices, 4, stage), early))
    offset = lax.axis_index("tm") * frame_count
    positions = after(offset, mark) - MARGIN + jnp.arange(frame_count + MARGIN, dtype=jnp.int32)
    cosine, sine = turn_tables(positions, width // HEADS)
    bias = score_bias(frame_count, after(offset, mark))
    def order(kind):
        owners = jnp.asarray(device_of_places(devices, kind)) ^ after(me, mark)
        starts = (owners * rows).astype(jnp.int32)
        if rows % 16 == 0:
            places = place_of(jnp.arange(devices, dtype=jnp.int32) ^ after(me, mark), devices, kind)
            return starts, jnp.zeros((1, 128), jnp.int32), (places * rows).astype(jnp.int32)
        rowmap = (starts[:, None] + jnp.arange(rows, dtype=jnp.int32)[None, :]).reshape(1, width)
        return starts, rowmap, starts

    orders = {kind: order(kind) for kind in range(2, 6)}
    share = entries // devices
    late_codes, late_me = after((codes, me), mark)
    owners = (late_codes // share) ^ late_me
    places = jnp.where(
        jnp.arange(LEVELS)[None, :] < mid,
        place_of(owners, devices, 4),
        place_of(owners, devices, 5),
    )
    places = (places * share + late_codes % share).astype(jnp.int32)
    flat_codes = jnp.concatenate([late_codes.T, places.T], axis=0)
    flat_codes, orders = after((flat_codes, orders), mark)
    ready = (cosine, sine, bias, flat_codes, orders)
    early = join(early, after(gather_swaps(early, devices, 2, 1), ready))
    come = after(gather_swaps(feed, devices, 4, 3), early)
    early_pieces = (early, swap(early, devices, 1))
    feed_a, feed_b = join(feed, come, (units, feed.shape[1] - units), 10)
    come_a = gather_swaps(feed_a, devices, 4, 2)
    come_b = gather_swaps(feed_b, devices, 5, 2)

    normed_first, q, k, v, scales, qkv_weights = qkv_call(
        *orders[2][:2], halo, inputs, early_pieces, cosine, sine
    )
    come_a, come_b = after((come_a, come_b), q)
    feed_a, feed_b = join(feed_a, come_a), join(feed_b, come_b)
    come_a = gather_swaps(feed_a, devices, 4, 1)
    come_b = gather_swaps(feed_b, devices, 5, 1)
    mixed, logsum = attend_call(q, after(k, feed_a, feed_b), v, bias)
    come_a, come_b = after((come_a, come_b), mixed)
    feed_a, feed_b = join(feed_a, come_a), join(feed_b, come_b)
    feed_pieces = (feed_a, swap(feed_a, devices, 1), feed_b, swap(feed_b, devices, 1))
    (
        branch_first, after_first, normed_second, hidden, slope, branch_second, low_out, latent,
        latent_again, feed_weights,
    ) = forward_call((orders[4][:2], orders[5][:2]), inputs, mixed, scales, feed_pieces, units, depth)

    carried = fetch_call(levels, flat_codes, latent_again, book)
    keep_high, send_high = spread_call(mid, mid, flat_codes, carried, entries)
    come_high = swap_parts([send_high], devices, 5, 0)
    carried = after(carried, keep_high)
    keep_low, send_low = spread_call(0, mid, flat_codes, carried, entries)
    come_low = swap_parts([send_low], devices, 4, 0)
    high = reduce_split(keep_high, after(come_high, keep_low), devices, 5, 1, 0, bf16)
    low = reduce_split(keep_low, after(come_low, high[0]), devices, 4, 1, 0, bf16)

    grad_after, grad_mixed, sums_second, keep_a, send_a, keep_b, send_b = backward_call(
        (orders[4], orders[5]), after(carried, high[0], low[0]), branch_second, slope, after_first, branch_first,
        normed_second, hidden, low_out, mixed, scales, feed_weights,
    )
    come_a = swap_parts([send_a], devices, 4, 0)
    come_b = swap_parts([send_b], devices, 5, 0)
    high = reduce_split(high[0], after(high[1], keep_a), devices, 5, 2, 2)
    low = reduce_split(low[0], after(low[1], high[0]), devices, 4, 2)

    lead = MARGIN // QROWS
    blocks = frame_count // QROWS
    zeros = jnp.zeros((MARGIN, width), f32)
    fixed = (logsum, bias, cosine, sine)
    grad_mixed = after(grad_mixed, low[0])
    q_a, k_a, v_a, halo = attend_back_call(0, lead, q, k, v, grad_mixed, *fixed, zeros, zeros)
    halo = lax.ppermute(halo, "tm", [(i + 1, i) for i in range(spans - 1)])
    come_a, come_b = after((come_a, come_b), k_a)
    keep_a, come_a = reduce_split(keep_a, come_a, devices, 4, 1)
    keep_b, come_b = reduce_split(keep_b, come_b, devices, 5, 1)
    grad_mixed = after(grad_mixed, keep_a, keep_b)
    q_b, k_b, v_b, _ = attend_back_call(lead, lead, q, k, v, grad_mixed, *fixed, k_a, v_a)
    come_low, come_high = after((low[1], high[1]), k_b)
    keep_book, come_book = stack_split((low[0], come_low), (high[0], come_high), devices, 4, 3)
    grad_mixed = after(grad_mixed, keep_book)
    q_c, k_c, v_c, _ = attend_back_call(
        2 * lead, blocks - 2 * lead, q, k, v, grad_mixed, *fixed, k_b, v_b
    )
    come_book, come_a, come_b = after((come_book, come_a, come_b), k_c)
    keep_a, come_a = reduce_split(keep_a, come_a, devices, 4, 2)
    keep_b, come_b = reduce_split(keep_b, come_b, devices, 5, 2)
    for stage in range(4, split_stages):
        keep_book, come_book = reduce_split(keep_book, come_book, devices, 4, stage)
    input_gradient, qkv_a, send_a, qkv_b, send_b = finish_call(
        orders[2], inputs, normed_first, (q_a, q_b, q_c),
        (k_b, after(k_c, keep_book, keep_a, keep_b)), (v_b, v_c), halo, cosine, sine, grad_after,
        scales, sums_second, qkv_weights,
    )
    send_a = swap_parts([send_a], devices, 2, 0)
    send_b = swap_parts([send_b], devices, 2, 0)
    grad_book, squares = book_call(keep_book, after(come_book, qkv_a))
    come_a, come_b = after((come_a, come_b), grad_book)
    keep_feed, come_feed = merge_split(
        ((keep_a, come_a), (keep_b, come_b)), devices, 4, 3, FEED_SHARE
    )
    send_a, send_b = after((send_a, send_b), keep_feed)
    keep_qkv, come_qkv = merge_split(((qkv_a, send_a), (qkv_b, send_b)), devices, 2, 1)
    for stage in range(4, split_stages):
        keep_feed, come_feed = reduce_split(keep_feed, come_feed, devices, 4, stage)
    for stage in range(2, len(digit_plan(devices, 2))):
        keep_qkv, come_qkv = reduce_split(keep_qkv, come_qkv, devices, 2, stage)
    grad_feed, grad_qkv, shared = total_call(
        squares, ((keep_feed, come_feed), (keep_qkv, come_qkv)), devices
    )

    shared = lax.all_to_all(shared, AXES, 0, 0, tiled=True)
    gradient_norm, *updated = adam_call(
        shared,
        (grad_feed, grad_qkv, grad_book),
        (
            (attention_master, attention_first, attention_second),
            (feedforward_master, feedforward_first, feedforward_second),
            (projection_master, projection_first, projection_second),
            (codebook_master, codebook_first, codebook_second),
            (scales_master, scales_first, scales_second),
        ),
    )
    return (latent, input_gradient, gradient_norm[0, 0], *updated)


def solution(mesh):
    rows = P(AXES, None)
    middle = P(None, AXES, None)
    scale = P(None, AXES)
    in_specs = (rows, rows, P("clip")) + (middle,) * 6 + (rows,) * 3 + (middle,) * 3 + (scale,) * 3
    out_specs = (rows, rows, P()) + (middle,) * 8 + (rows,) * 4 + (middle,) * 4 + (scale,) * 4
    return jax.shard_map(body, mesh=mesh, in_specs=in_specs, out_specs=out_specs, check_vma=False)
```

```python
import math

import jax
import jax.numpy as jnp
import numpy as np
from jax import lax
from jax.experimental import pallas as pl
from jax.experimental.pallas import tpu as pltpu
from jax.sharding import PartitionSpec as P

HEADS = 8
LEVELS = 8
WINDOW = 250
STEP = 10
AXES = ("clip", "tm")

clip_level = 1.0
beta_first = 0.9
beta_second = 0.95
adam_floor = 1e-08
weight_decay = 0.1
group_rates = (0.05, 0.03, 0.05, 0.5, 0.5)
masked_score = -1e30

f32 = jnp.float32
bf16 = jnp.bfloat16
MARGIN = (WINDOW + 127) // 128 * 128
QROWS = 128
SPAN = QROWS + MARGIN
ROWS = 256
MIB = 1 << 20
FEED_SHARE, BOOK_SHARE = 4, 2


def dot(left, right, contract=((1,), (0,))):
    return lax.dot_general(left, right, (contract, ((), ())), preferred_element_type=f32)


def dot_nt(left, right):
    return dot(left, right, ((1,), (1,)))


def flip(block):
    return block.astype(f32).T.astype(bf16)


def params(mib):
    return pltpu.CompilerParams(vmem_limit_bytes=mib * MIB)


def whole(shape):
    return pl.BlockSpec(tuple(shape), lambda *_: (0,) * len(shape))


def smem():
    return pl.BlockSpec(memory_space=pltpu.SMEM)


def cost(share, length=1):
    return pl.CostEstimate(flops=int(share * 500000000), bytes_accessed=length * 3 * MIB, transcendentals=0)


def after(value, *earlier):
    return lax.optimization_barrier((value, earlier))[0]


def digit_plan(count, kind):
    bits = count.bit_length() - 1
    middle = [(1, 4)] if kind < 4 else [(1, 2), (2, 2)] if kind == 4 else [(2, 2), (1, 2)]
    plan, shift = [(0, 2)] + middle, 3
    while shift < bits:
        width = min(2, bits - shift) if kind == 2 else 1
        plan.append((shift, 1 << width))
        shift += width
    return plan


def swap(block, count, mask):
    return lax.ppermute(block, AXES, [(i, i ^ mask) for i in range(count)])


def gather_swaps(block, count, kind, stage):
    shift, radix = digit_plan(count, kind)[stage]
    return [swap(block, count, k << shift) for k in range(1, radix)]


def join_kernel(count, widths, *refs):
    outs = refs[count:]
    top = 0
    for part in refs[:count]:
        rows, left = part.shape[0], 0
        for out, width in zip(outs, widths):
            out[top : top + rows, :] = part[:, left : left + width]
            left += width
        top += rows


def join(block, others, widths=None, share=0):
    parts = [block, *others]
    rows, columns = block.shape
    widths = widths or (columns,)
    if rows % 16:
        whole_block = jnp.concatenate(parts, axis=0)
        edges = [sum(widths[:index]) for index in range(len(widths) + 1)]
        outs = [whole_block[:, left:right] for left, right in zip(edges, edges[1:])]
    else:
        outs = pl.pallas_call(
            lambda *refs: join_kernel(len(parts), widths, *refs),
            grid=(1,),
            in_specs=[whole(part.shape) for part in parts],
            out_specs=[whole((len(parts) * rows, width)) for width in widths],
            out_shape=[
                jax.ShapeDtypeStruct((len(parts) * rows, width), block.dtype) for width in widths
            ],
            compiler_params=params(16),
            cost_estimate=cost(share, 1),
            name="join_rows",
        )(*parts)
    return outs[0] if len(widths) == 1 else outs


def place_of(device, count, kind):
    place, weight = 0, 1
    for shift, radix in reversed(digit_plan(count, kind)):
        place = place + ((device >> shift) & (radix - 1)) * weight
        weight *= radix
    return place


def device_of_places(count, kind):
    table = np.zeros(count, np.int32)
    for device in range(count):
        table[place_of(device, count, kind)] = device
    return table


def swap_parts(parts, count, kind, stage):
    shift, _ = digit_plan(count, kind)[stage]
    return [swap(part, count, (k + 1) << shift) for k, part in enumerate(parts)]


def reduce_add(keep, parts):
    total = keep.astype(f32)
    for part in parts:
        total = total + part.astype(f32)
    return total


def split_kernel(radix, *refs):
    outs, operands = refs[-radix:], refs[:-radix]
    total = operands[0][...].astype(f32)
    for operand in operands[1:]:
        total = total + operand[...].astype(f32)
    size = total.shape[1] // radix
    for k, out in enumerate(outs):
        out[...] = total[:, k * size : (k + 1) * size, :].astype(out.dtype)


def reduce_split(keep, parts, count, kind, stage, share=0, held=f32):
    _, radix = digit_plan(count, kind)[stage]
    lead, rows, columns = keep.shape
    size = rows // radix
    if lead > 1:
        group = 2 if held == bf16 else 1
        steps, block, index = lead // group, (group, rows, columns), lambda i: (i, 0, 0)
    else:
        steps = 2 if columns % 256 == 0 else 1
        block, index = (1, rows, columns // steps), lambda i: (0, 0, i)
    shares = (block[0], size, block[2])
    kinds = [held] + [bf16] * (radix - 1)
    outs = pl.pallas_call(
        lambda *refs: split_kernel(radix, *refs),
        grid=(steps,),
        in_specs=[pl.BlockSpec(block, index)] * (1 + len(parts)),
        out_specs=[pl.BlockSpec(shares, index)] * radix,
        out_shape=[jax.ShapeDtypeStruct((lead, size, columns), kind) for kind in kinds],
        compiler_params=params(20),
        cost_estimate=cost(share, 1),
        name="split_sums",
    )(keep, *parts)
    return outs[0], swap_parts(outs[1:], count, kind, stage)


def merge_kernel(radix, groups, *refs):
    outs = refs[-radix:]
    base = left = 0
    for size in groups:
        total = refs[base][...].astype(f32)
        for operand in refs[base + 1 : base + size]:
            total = total + operand[...].astype(f32)
        base += size
        rows = total.shape[1] // radix
        for k, out in enumerate(outs):
            share = total[:, k * rows : (k + 1) * rows, :].astype(out.dtype)
            out[:, :, left : left + total.shape[2]] = share
        left += total.shape[2]


def merge_split(groups, count, kind, stage, share=0):
    _, radix = digit_plan(count, kind)[stage]
    operands = [array for keep, parts in groups for array in (keep, *parts)]
    _, rows, _ = groups[0][0].shape
    shape = (1, rows // radix, sum(keep.shape[2] for keep, _ in groups))
    sizes = [1 + len(parts) for _, parts in groups]
    kinds = [f32] + [bf16] * (radix - 1)
    outs = pl.pallas_call(
        lambda *refs: merge_kernel(radix, sizes, *refs),
        grid=(1,),
        in_specs=[whole(operand.shape) for operand in operands],
        out_specs=[whole(shape)] * radix,
        out_shape=[jax.ShapeDtypeStruct(shape, kind) for kind in kinds],
        compiler_params=params(20),
        cost_estimate=cost(share, 1),
        name="split_sums",
    )(*operands)
    return outs[0], swap_parts(outs[1:], count, kind, stage)


def stack_kernel(radix, half, *refs):
    outs, operands = refs[-radix:], refs[:-radix]
    size = operands[0].shape[1] // radix

    def add(parts):
        total = sum(part[...].astype(f32) for part in parts)
        for k, out in enumerate(outs):
            out[...] = total[:, k * size : (k + 1) * size, :].astype(out.dtype)

    @pl.when(pl.program_id(0) < half)
    def _():
        add(operands[: len(operands) // 2])

    @pl.when(pl.program_id(0) >= half)
    def _():
        add(operands[len(operands) // 2 :])


def stack_split(low, high, count, kind, stage, share=0):
    _, radix = digit_plan(count, kind)[stage]
    operands = [low[0], *low[1], high[0], *high[1]]
    half, rows, columns = low[0].shape
    kinds = [f32] + [bf16] * (radix - 1)
    block = (1, rows, columns)
    below = pl.BlockSpec(block, lambda i: (jnp.minimum(i, half - 1), 0, 0))
    above = pl.BlockSpec(block, lambda i: (jnp.maximum(i - half, 0), 0, 0))
    outs = pl.pallas_call(
        lambda *refs: stack_kernel(radix, half, *refs),
        grid=(2 * half,),
        in_specs=[below] * (1 + len(low[1])) + [above] * (1 + len(high[1])),
        out_specs=[pl.BlockSpec((1, rows // radix, columns), lambda i: (i, 0, 0))] * radix,
        out_shape=[
            jax.ShapeDtypeStruct((2 * half, rows // radix, columns), kind) for kind in kinds
        ],
        compiler_params=params(20),
        cost_estimate=cost(share, 2),
        name="split_sums",
    )(*operands)
    return outs[0], swap_parts(outs[1:], count, kind, stage)


def one_hot_rows(rowmap, size):
    place = lax.broadcasted_iota(jnp.int32, (size, size), 0)
    return jnp.where(place == rowmap, 1.0, 0.0).astype(bf16)


def unpack_rows(starts_ref, rowmap_ref, pieces, out_ref):
    half = pieces[0].shape[0]
    count = starts_ref.shape[0]
    rows = 2 * half // count
    if rows % 16 == 0:
        for place in range(count):
            piece = pieces[place * rows // half]
            inner = place * rows % half
            start = pl.multiple_of(starts_ref[place], rows)
            out_ref[pl.ds(start, rows), :] = piece[inner : inner + rows, :]
    else:
        spread = one_hot_rows(rowmap_ref[0:1, :], 2 * half)
        columns = out_ref.shape[1]
        for left in range(0, columns, 128):
            joined = jnp.concatenate([p[:, left : left + 128] for p in pieces], axis=0)
            out_ref[:, left : left + 128] = dot(spread, joined).astype(bf16)


def store_flipped(dests_ref, rowmap_ref, block, out_ref, lanes):
    flipped = flip(block)
    size = flipped.shape[0]
    count = dests_ref.shape[0]
    rows = size // count
    if rows % 16 == 0:
        for index in range(count):
            start = pl.multiple_of(dests_ref[index], rows)
            out_ref[pl.ds(start, rows), lanes] = flipped[index * rows : (index + 1) * rows]
    else:
        spread = one_hot_rows(rowmap_ref[0:1, :], size)
        out_ref[:, lanes] = dot(spread, flipped, ((0,), (0,))).astype(bf16)


def store_halves(values, keep, send, lanes):
    half = keep.shape[1]
    keep[0, :, lanes] = values[:half].astype(bf16)
    send[0, :, lanes] = values[half:].astype(bf16)


def centre_rows(values):
    centred = values - jnp.mean(values, axis=-1, keepdims=True)
    spread = jnp.mean(centred * centred, axis=-1, keepdims=True)
    rstd = lax.rsqrt(spread + 1e-05)
    return centred * rstd, rstd


def norm_back(normal, rstd, gain, grad):
    inner = grad * gain
    first = jnp.mean(inner, axis=-1, keepdims=True)
    second = jnp.mean(inner * normal, axis=-1, keepdims=True)
    return rstd * (inner - first - normal * second)


def column_sum(values):
    return jnp.sum(values, axis=0, keepdims=True)


def turn(values, cosine, sine):
    lanes = values.shape[1]
    ahead = pltpu.roll(values, lanes - 32, 1)
    behind = pltpu.roll(values, 32, 1)
    lane = lax.broadcasted_iota(jnp.int32, values.shape, 1)
    partner = jnp.where(lane % 64 < 32, ahead, behind)
    repeats = lanes // cosine.shape[1]
    if repeats > 1:
        cosine = jnp.concatenate([cosine] * repeats, axis=1)
        sine = jnp.concatenate([sine] * repeats, axis=1)
    return values * cosine + partner * sine


def head_columns(flipped):
    zero = jnp.zeros((64, flipped.shape[1]), flipped.dtype)
    return jnp.concatenate(
        [
            jnp.concatenate([flipped[:64], zero], axis=1),
            jnp.concatenate([zero, flipped[64:]], axis=1),
        ],
        axis=0,
    )


def head_rows(block):
    lane = lax.broadcasted_iota(jnp.int32, block.shape, 1)
    zero = jnp.zeros_like(block)
    return jnp.concatenate(
        [jnp.where(lane < 64, block, zero), jnp.where(lane < 64, zero, block)], axis=0
    )


def lower_kernel(attention, feed, projection, book, scales, early, later, low_book, work):
    width = attention.shape[2]
    units = feed.shape[2]
    rows = attention.shape[1]
    for k in range(3):
        early[:, k * width : (k + 1) * width] = attention[k].astype(bf16)
    work[...] = jnp.zeros(work.shape, f32)
    work[: scales.shape[0], :rows] = scales[...]
    early[:, 3 * width :] = work[...].T[:rows].astype(bf16)
    for k in range(2):
        later[:, k * units : (k + 1) * units] = feed[k].astype(bf16)
    last = 2 * units + projection.shape[1]
    later[:, 2 * units : last] = projection[...].astype(bf16)
    later[:, last:] = attention[3].astype(bf16)
    low_book[...] = book[...].astype(bf16)


def lower_call(attention, feed, projection, book, scales):
    _, rows, width = attention.shape
    columns = 2 * feed.shape[2] + projection.shape[1] + width
    shapes = ((rows, 3 * width + 128), (rows, columns), book.shape)
    operands = (attention, feed, projection, book, scales)
    return pl.pallas_call(
        lower_kernel,
        grid=(1,),
        in_specs=[whole(operand.shape) for operand in operands],
        out_specs=[whole(shape) for shape in shapes],
        out_shape=[jax.ShapeDtypeStruct(shape, bf16) for shape in shapes],
        scratch_shapes=[pltpu.VMEM((128, 128), f32)],
        compiler_params=params(62),
        cost_estimate=cost(0, 1),
        name="lower_weights",
    )(*operands)


def qkv_kernel(
    starts, rowmap, halo, inputs, piece_a, piece_b, cosine, sine, normed, q, k, v, scales, weights
):
    step = pl.program_id(0)
    width = inputs.shape[1]

    @pl.when(step == 0)
    def _():
        unpack_rows(starts, rowmap, (piece_a, piece_b), weights)
        scales[...] = weights[:, 3 * width :].astype(f32).T[:8]

    frames = jnp.where(step == 0, halo[...].astype(f32), inputs[...].astype(f32))
    normal, _ = centre_rows(frames)
    low = (normal * scales[0:1, :] + scales[1:2, :]).astype(bf16)
    normed[...] = low
    turned = turn(dot(low, weights[:, :width]), cosine[...], sine[...])
    q[...] = (turned.astype(bf16).astype(f32) * 0.125).astype(bf16)
    k[...] = turn(dot(low, weights[:, width : 2 * width]), cosine[...], sine[...]).astype(bf16)
    v[...] = dot(low, weights[:, 2 * width : 3 * width]).astype(bf16)


def qkv_call(starts, rowmap, halo, inputs, pieces, cosine, sine):
    count, width = inputs.shape
    columns = pieces[0].shape[1]
    steps = count // ROWS + 1
    late = lambda i: (jnp.maximum(i - 1, 0), 0)
    here = lambda i: (i, 0)
    return pl.pallas_call(
        qkv_kernel,
        grid=(steps,),
        in_specs=[
            smem(),
            whole(rowmap.shape),
            whole(halo.shape),
            pl.BlockSpec((ROWS, width), late),
            whole(pieces[0].shape),
            whole(pieces[1].shape),
            pl.BlockSpec((ROWS, 128), here),
            pl.BlockSpec((ROWS, 128), here),
        ],
        out_specs=[
            pl.BlockSpec((ROWS, width), late),
            pl.BlockSpec((ROWS, width), late),
            pl.BlockSpec((ROWS, width), here),
            pl.BlockSpec((ROWS, width), here),
            whole((8, width)),
            whole((width, columns)),
        ],
        out_shape=[
            jax.ShapeDtypeStruct((count, width), bf16),
            jax.ShapeDtypeStruct((count, width), bf16),
            jax.ShapeDtypeStruct((count + MARGIN, width), bf16),
            jax.ShapeDtypeStruct((count + MARGIN, width), bf16),
            jax.ShapeDtypeStruct((8, width), f32),
            jax.ShapeDtypeStruct((width, columns), bf16),
        ],
        compiler_params=params(32),
        cost_estimate=cost(4, 8),
        name="project_rows",
    )(starts, rowmap, halo, inputs, *pieces, cosine, sine)


def attend_kernel(q, k, v, bias, mixed, logsum):
    step = pl.program_id(0)
    start = pl.multiple_of(step * QROWS, QROWS)
    keys = pl.ds(start, SPAN)
    allowed = jnp.concatenate([bias[0], bias[0]], axis=1)
    lane = lax.broadcasted_iota(jnp.int32, (QROWS, 128), 1)
    pairs = [slice(left, left + 128) for left in range(0, q.shape[1], 128)]
    columns = [head_columns(flip(q[:, lanes])) for lanes in pairs]
    scores = [dot(k[keys, lanes], column) + allowed for lanes, column in zip(pairs, columns)]
    highest = [jnp.max(score, axis=0, keepdims=True) for score in scores]
    raised = [jnp.exp(score - high) for score, high in zip(scores, highest)]
    totals = [column_sum(part) for part in raised]
    weights = [(part * (1.0 / total)).astype(bf16) for part, total in zip(raised, totals)]
    outputs = [
        dot(weight, v[keys, lanes], ((0,), (0,))) for weight, lanes in zip(weights, pairs)
    ]
    rows = []
    for lanes, output, high, total in zip(pairs, outputs, highest, totals):
        mixed[:, lanes] = jnp.where(lane < 64, output[:QROWS], output[QROWS:]).astype(bf16)
        record = high + jnp.log(total)
        rows += [record[:, :QROWS], record[:, QROWS:]]
    logsum[...] = jnp.concatenate(rows, axis=0)


def attend_call(q, k, v, bias):
    count, width = q.shape
    return pl.pallas_call(
        attend_kernel,
        grid=(count // QROWS,),
        in_specs=[
            pl.BlockSpec((QROWS, width), lambda i: (i, 0)),
            whole(k.shape),
            whole(v.shape),
            pl.BlockSpec((1, SPAN, QROWS), lambda i: (i, 0, 0)),
        ],
        out_specs=[
            pl.BlockSpec((QROWS, width), lambda i: (i, 0)),
            pl.BlockSpec((HEADS, QROWS), lambda i: (0, i)),
        ],
        out_shape=[
            jax.ShapeDtypeStruct((count, width), bf16),
            jax.ShapeDtypeStruct((HEADS, count), f32),
        ],
        compiler_params=params(24),
        cost_estimate=cost(4, 14),
        name="attend_rows",
    )(q, k, v, bias)


def forward_kernel(
    starts_a, rowmap_a, starts_b, rowmap_b, inputs, mixed, scales, own_a, other_a, own_b, other_b,
    branch_first, after_first, normed, hidden, slope, branch_second, low_out, latent, again, weights,
):
    step = pl.program_id(0)
    width = inputs.shape[1]
    units = hidden.shape[1]

    @pl.when(step == 0)
    def _():
        unpack_rows(starts_a, rowmap_a, (own_a, other_a), weights.at[:, :units])
        unpack_rows(starts_b, rowmap_b, (own_b, other_b), weights.at[:, units:])

    up, down = 0, units
    proj = 2 * units
    last = proj + latent.shape[1]
    first = dot(mixed[...], weights[:, last : last + width])
    branch_first[...] = first.astype(bf16)
    after = inputs[...].astype(f32) + scales[4:5, :] * first
    after_first[...] = after
    normal, _ = centre_rows(after)
    low = (normal * scales[2:3, :] + scales[3:4, :]).astype(bf16)
    normed[...] = low
    chunk = 512
    lefts = range(0, units, chunk)
    pres = [dot(low, weights[:, up + left : up + left + chunk]) for left in lefts]
    for left, pre in zip(lefts, pres):
        share = 0.5 + 0.5 * lax.erf(pre * (1.0 / math.sqrt(2.0)))
        bell = jnp.exp(-0.5 * pre * pre) * (1.0 / math.sqrt(2.0 * math.pi))
        hidden[:, left : left + chunk] = (pre * share).astype(bf16)
        slope[:, left : left + chunk] = (share + pre * bell).astype(bf16)
    second = dot_nt(hidden[...], weights[:, down : down + units])
    branch_second[...] = second.astype(bf16)
    rounded = (after + scales[5:6, :] * second).astype(bf16)
    low_out[...] = rounded
    result = dot(rounded, weights[:, proj:last])
    latent[...] = result
    again[...] = result


def forward_call(orders, inputs, mixed, scales, pieces, units, depth):
    count, width = inputs.shape
    columns = pieces[0].shape[1] + pieces[2].shape[1]
    row = lambda size: pl.BlockSpec((ROWS, size), lambda i: (i, 0))
    kept = ((width, bf16), (width, f32), (width, bf16), (units, bf16), (units, bf16),
            (width, bf16), (width, bf16), (depth, f32), (depth, f32))
    (starts_a, rowmap_a), (starts_b, rowmap_b) = orders
    return pl.pallas_call(
        forward_kernel,
        grid=(count // ROWS,),
        in_specs=[smem(), whole(rowmap_a.shape)] * 2
        + [row(width), row(width), whole(scales.shape)]
        + [whole(piece.shape) for piece in pieces],
        out_specs=[row(size) for size, _ in kept] + [whole((width, columns))],
        out_shape=[jax.ShapeDtypeStruct((count, size), kind) for size, kind in kept]
        + [jax.ShapeDtypeStruct((width, columns), bf16)],
        compiler_params=params(56),
        cost_estimate=cost(4, 17),
        name="feed_rows",
    )(starts_a, rowmap_a, starts_b, rowmap_b, inputs, mixed, scales, *pieces)


def fetch_kernel(active, codes, latent, book, carried, residue, steps, columns):
    level = pl.program_id(0)
    count, depth = latent.shape
    tiles = book.shape[1] // 256

    @pl.when(level == 0)
    def _():
        residue[...] = latent[...]
        columns[...] = codes[:LEVELS, :].astype(f32).T

    factor = jnp.where(level < active[0], 1.0, 0.0).astype(f32)
    lane = lax.broadcasted_iota(jnp.int32, (ROWS, LEVELS), 1)
    place = lax.broadcasted_iota(jnp.int32, (ROWS, 256), 1).astype(f32)
    blocks = [slice(top, top + ROWS) for top in range(0, count, ROWS)]
    picked = []
    for rows in blocks:
        code = jnp.where(lane == level, columns[rows, :], 0.0)
        code = jnp.sum(code, axis=1, keepdims=True)
        high = jnp.floor(code * (1.0 / 256.0))
        hit = jnp.where(place == code - 256.0 * high, 1.0, 0.0).astype(bf16)
        picks = [hit * jnp.where(high == j, 1.0, 0.0).astype(bf16) for j in range(tiles)]
        picked.append(jnp.concatenate(picks, axis=1))
    found = [dot(pick, book[0]) for pick in picked]
    for rows, row in zip(blocks, found):
        left = residue[rows, :] - factor * row
        residue[rows, :] = left
        steps[level, rows, :] = factor * left

    @pl.when(level == LEVELS - 1)
    def _():
        for top in range(0, count, ROWS):
            rows = slice(top, top + ROWS)
            total = jnp.zeros((ROWS, depth), f32)
            for index in reversed(range(LEVELS)):
                total = total + steps[index, rows, :]
                carried[index, rows, :] = total.astype(bf16)


def fetch_call(active, codes, latent, book):
    count, depth = latent.shape
    entries = book.shape[1]
    return pl.pallas_call(
        fetch_kernel,
        grid=(LEVELS,),
        in_specs=[
            smem(),
            whole(codes.shape),
            whole(latent.shape),
            pl.BlockSpec((1, entries, depth), lambda i: (i, 0, 0)),
        ],
        out_specs=whole((LEVELS, count, depth)),
        out_shape=jax.ShapeDtypeStruct((LEVELS, count, depth), bf16),
        scratch_shapes=[
            pltpu.VMEM((count, depth), f32),
            pltpu.VMEM((LEVELS, count, depth), f32),
            pltpu.VMEM((count, LEVELS), f32),
        ],
        compiler_params=params(48),
        cost_estimate=cost(4, 13),
        name="fetch_codes",
    )(active, codes, latent, book)


def spread_kernel(first, codes, carried, keep, send):
    count = carried.shape[1]
    half = keep.shape[1]
    level = pl.program_id(0) + first
    code = codes[pl.ds(LEVELS + level, 1), :]
    high = code >> 8
    place = lax.broadcasted_iota(jnp.int32, (256, count), 0)
    hit = jnp.where(place == (code & 255), -1.0, 0.0).astype(bf16)
    for j in range(2 * half // 256):
        pick = hit * jnp.where(high == j, 1.0, 0.0).astype(bf16)
        out, inner = (keep, send)[j * 256 // half], j * 256 % half
        out[0, inner : inner + 256, :] = dot(pick, carried[0]).astype(bf16)


def spread_call(first, levels, codes, carried, entries):
    _, count, depth = carried.shape
    half = entries // 2
    return pl.pallas_call(
        lambda *refs: spread_kernel(first, *refs),
        grid=(levels,),
        in_specs=[
            whole(codes.shape),
            pl.BlockSpec((1, count, depth), lambda i: (i + first, 0, 0)),
        ],
        out_specs=[pl.BlockSpec((1, half, depth), lambda i: (i, 0, 0))] * 2,
        out_shape=[jax.ShapeDtypeStruct((levels, half, depth), bf16)] * 2,
        compiler_params=params(16),
        cost_estimate=cost(1, 5),
        name="spread_codes",
    )(codes, carried)


def backward_kernel(
    dests_a, rowmap_a, dests_b, rowmap_b, carried, branch_second, slope, after_first, branch_first, normed, hidden, low_out, mixed,
    scales, weights,
    out_after, out_mixed, sums, keep_a, send_a, keep_b, send_b,
    grad_pre, kept_hidden, kept_carried, grad_branch, flipped,
):
    step = pl.program_id(0)
    last_step = pl.num_programs(0) - 1
    width = after_first.shape[1]
    units = slope.shape[1]
    proj = 2 * units
    last = proj + carried.shape[2]
    chunk = 512
    rows = pl.ds(pl.multiple_of(step * ROWS, ROWS), ROWS)

    @pl.when(step == 0)
    def _():
        sums[...] = jnp.zeros(sums.shape, f32)

    grad_after = dot_nt(carried[0], weights[:, proj:last])
    sums[5:6, :] += column_sum(grad_after * branch_second[...].astype(f32))
    low = (grad_after * scales[5:6, :]).astype(bf16)
    grad_normed = jnp.zeros(grad_after.shape, f32)
    for left in range(0, units, chunk):
        grad_hidden = dot(low, weights[:, units + left : units + left + chunk])
        part = (grad_hidden * slope[:, left : left + chunk].astype(f32)).astype(bf16)
        grad_pre[rows, left : left + chunk] = part
        grad_normed = grad_normed + dot_nt(part, weights[:, left : left + chunk])
    normal, rstd = centre_rows(after_first[...])
    sums[2:3, :] += column_sum(grad_normed * normal)
    sums[3:4, :] += column_sum(grad_normed)
    grad_first = grad_after + norm_back(normal, rstd, scales[2:3, :], grad_normed)
    out_after[...] = grad_first.astype(bf16)
    sums[4:5, :] += column_sum(grad_first * branch_first[...].astype(f32))
    low_first = (grad_first * scales[4:5, :]).astype(bf16)
    grad_branch[rows, :] = low_first
    out_mixed[...] = dot_nt(low_first, weights[:, last : last + width]).astype(bf16)
    kept_hidden[rows, :] = hidden[...]
    kept_carried[rows, :] = carried[0]
    for index, block in enumerate((normed[...], low_out[...])):
        store_flipped(dests_a, rowmap_a, block, flipped.at[index], rows)
    for index, block in enumerate((low, mixed[...])):
        store_flipped(dests_b, rowmap_b, block, flipped.at[2 + index], rows)

    @pl.when(step == last_step)
    def _():
        for left in range(0, units, chunk):
            lanes = slice(left, left + chunk)
            store_halves(dot(flipped[0], grad_pre[:, lanes]), keep_a, send_a, lanes)
            store_halves(dot(flipped[2], kept_hidden[:, lanes]), keep_b, send_b, lanes)
        rest = slice(units, keep_a.shape[2])
        store_halves(dot(flipped[1], kept_carried[...]), keep_a, send_a, rest)
        rest = slice(units, keep_b.shape[2])
        store_halves(dot(flipped[3], grad_branch[...]), keep_b, send_b, rest)


def backward_call(
    orders, carried, branch_second, slope, after_first, branch_first, normed, hidden, low_out,
    mixed, scales, weights,
):
    count, width = after_first.shape
    units, depth = slope.shape[1], carried.shape[2]
    row = lambda size: pl.BlockSpec((ROWS, size), lambda i: (i, 0))
    pieces = [(1, width // 2, units + extra) for extra in (depth, depth, width, width)]
    (_, rowmap_a, dests_a), (_, rowmap_b, dests_b) = orders
    return pl.pallas_call(
        backward_kernel,
        grid=(count // ROWS,),
        in_specs=[smem(), whole(rowmap_a.shape)] * 2
        + [pl.BlockSpec((1, ROWS, depth), lambda i: (0, i, 0))]
        + [row(width), row(units), row(width), row(width), row(width), row(units), row(width)]
        + [row(width), whole(scales.shape), whole(weights.shape)],
        out_specs=[row(width), row(width), whole((8, width))] + [whole(piece) for piece in pieces],
        out_shape=[
            jax.ShapeDtypeStruct((count, width), bf16),
            jax.ShapeDtypeStruct((count, width), bf16),
            jax.ShapeDtypeStruct((8, width), f32),
        ]
        + [jax.ShapeDtypeStruct(piece, bf16) for piece in pieces],
        scratch_shapes=[
            pltpu.VMEM((count, units), bf16),
            pltpu.VMEM((count, units), bf16),
            pltpu.VMEM((count, depth), bf16),
            pltpu.VMEM((count, width), bf16),
            pltpu.VMEM((4, width, count), bf16),
        ],
        compiler_params=params(56),
        cost_estimate=cost(2, 25),
        name="feed_back",
    )(
        dests_a, rowmap_a, dests_b, rowmap_b, carried, branch_second, slope, after_first, branch_first, normed, hidden,
        low_out, mixed, scales, weights,
    )


def attend_back_kernel(pieces, *refs):
    k_refs, v_refs = refs[:pieces], refs[pieces : 2 * pieces]
    (q, grad, logsum, bias, cosine, sine, start_k, start_v,
     grad_q, grad_k, grad_v, halo, k, v) = refs[2 * pieces :]
    step = pl.program_id(0)

    @pl.when(step == 0)
    def _():
        for index in range(pieces):
            rows = slice(index * MARGIN, (index + 1) * MARGIN)
            k[rows, :] = k_refs[index][...]
            v[rows, :] = v_refs[index][...]
        grad_k[:MARGIN, :] = start_k[...]
        grad_v[:MARGIN, :] = start_v[...]
        grad_k[MARGIN:, :] = jnp.zeros_like(grad_k[MARGIN:, :])
        grad_v[MARGIN:, :] = jnp.zeros_like(grad_v[MARGIN:, :])

    start = pl.multiple_of(step * QROWS, QROWS)
    keys = pl.ds(start, SPAN)
    allowed = jnp.concatenate([bias[0], bias[0]], axis=1)
    lane = lax.broadcasted_iota(jnp.int32, (QROWS, 128), 1)
    pairs = [slice(left, left + 128) for left in range(0, q.shape[1], 128)]
    records = [
        jnp.concatenate([logsum[h : h + 1, :], logsum[h + 1 : h + 2, :]], axis=1)
        for h in range(0, HEADS, 2)
    ]
    scores = [dot(k[keys, lanes], head_columns(flip(q[:, lanes]))) + allowed for lanes in pairs]
    grads = [dot(v[keys, lanes], head_columns(flip(grad[:, lanes]))) for lanes in pairs]
    weights = [jnp.exp(score - record) for score, record in zip(scores, records)]
    products = [weight * part for weight, part in zip(weights, grads)]
    inners = [column_sum(product) for product in products]
    grad_scores = [
        (product - weight * inner).astype(bf16)
        for product, weight, inner in zip(products, weights, inners)
    ]
    low = [weight.astype(bf16) for weight in weights]
    for lanes, weight in zip(pairs, low):
        grad_v[keys, lanes] += dot(weight, head_rows(grad[:, lanes]))
    for lanes, part in zip(pairs, grad_scores):
        grad_k[keys, lanes] += dot(part, head_rows(q[:, lanes]))
    joined = [dot(part, k[keys, lanes], ((0,), (0,))) for lanes, part in zip(pairs, grad_scores)]
    back = -sine[...]
    for lanes, part in zip(pairs, joined):
        flat = jnp.where(lane < 64, part[:QROWS], part[QROWS:]) * 0.125
        grad_q[:, lanes] = turn(flat, cosine[...], back).astype(bf16)

    @pl.when(step == pl.num_programs(0) - 1)
    def _():
        halo[:MARGIN, :] = grad_k[:MARGIN, :].astype(bf16)
        halo[MARGIN:, :] = grad_v[:MARGIN, :].astype(bf16)


def attend_back_call(offset, blocks, q, k, v, grad, logsum, bias, cosine, sine, start_k, start_v):
    width = q.shape[1]
    keys = blocks * QROWS + MARGIN
    lead = MARGIN // QROWS
    pieces = keys // MARGIN
    there = lambda i: (i + offset, 0)
    table = lambda i: (i + offset + lead, 0)
    fixed = lambda index: pl.BlockSpec((MARGIN, width), lambda i: (index, 0))
    return pl.pallas_call(
        lambda *refs: attend_back_kernel(pieces, *refs),
        grid=(blocks,),
        in_specs=[fixed(offset // lead + index) for index in range(pieces)] * 2
        + [
            pl.BlockSpec((QROWS, width), there),
            pl.BlockSpec((QROWS, width), there),
            pl.BlockSpec((HEADS, QROWS), lambda i: (0, i + offset)),
            pl.BlockSpec((1, SPAN, QROWS), lambda i: (i + offset, 0, 0)),
            pl.BlockSpec((QROWS, 128), table),
            pl.BlockSpec((QROWS, 128), table),
            fixed(start_k.shape[0] // MARGIN - 1),
            fixed(start_v.shape[0] // MARGIN - 1),
        ],
        out_specs=[
            pl.BlockSpec((QROWS, width), lambda i: (i, 0)),
            whole((keys, width)),
            whole((keys, width)),
            whole((2 * MARGIN, width)),
        ],
        out_shape=[
            jax.ShapeDtypeStruct((blocks * QROWS, width), bf16),
            jax.ShapeDtypeStruct((keys, width), f32),
            jax.ShapeDtypeStruct((keys, width), f32),
            jax.ShapeDtypeStruct((2 * MARGIN, width), bf16),
        ],
        scratch_shapes=[
            pltpu.VMEM((keys, width), bf16),
            pltpu.VMEM((keys, width), bf16),
        ],
        compiler_params=params(20),
        cost_estimate=cost(0 if offset > 0 else 8, 2 * blocks),
        name="attend_back",
    )(*[k] * pieces, *[v] * pieces, q, grad, logsum, bias, cosine, sine, start_k, start_v)


def finish_kernel(
    dests, rowmap, inputs, normed, q_a, q_b, q_c, k_a, k_b, v_a, v_b, halo, cosine, sine,
    grad_after, scales, sums_second, weights,
    out, keep_a, send_a, keep_b, send_b, flipped, turned_q, turned_k, turned_v, sums, tail,
):
    step = pl.program_id(0)
    last = pl.num_programs(0) - 1
    width = normed.shape[1]

    @pl.when(step == 0)
    def _():
        sums[...] = jnp.zeros(sums.shape, f32)
        sums[:8, :] = sums_second[...]
        left = 0
        for piece in (q_a, q_b, q_c):
            turned_q[left : left + piece.shape[0], :] = piece[...]
            left += piece.shape[0]

    rows = pl.ds(pl.multiple_of(step * ROWS, ROWS), ROWS)
    near = jnp.where(step == last, 1.0, 0.0).astype(f32)
    part_k = jnp.where(step == 0, k_a[...], k_b[...]) + near * halo[:MARGIN, :].astype(f32)
    part_v = jnp.where(step == 0, v_a[...], v_b[...]) + near * halo[MARGIN:, :].astype(f32)
    turned = turn(part_k, cosine[...], -sine[...]).astype(bf16)
    turned_k[rows, :] = turned
    value = part_v.astype(bf16)
    turned_v[rows, :] = value
    grad = dot_nt(turned_q[rows, :], weights[:, :width])
    grad = grad + dot_nt(turned, weights[:, width : 2 * width])
    grad = grad + dot_nt(value, weights[:, 2 * width : 3 * width])
    normal, rstd = centre_rows(inputs[...].astype(f32))
    sums[0:1, :] += column_sum(grad * normal)
    sums[1:2, :] += column_sum(grad)
    out[...] = grad_after[...].astype(f32) + norm_back(normal, rstd, scales[0:1, :], grad)

    store_flipped(dests, rowmap, normed[...], flipped, rows)

    @pl.when(step == last)
    def _():
        store_flipped(dests, rowmap, sums[...], tail, slice(None))
        parts = [dot(flipped[...], ref[...]).astype(bf16) for ref in (turned_q, turned_k, turned_v)]
        joined = jnp.concatenate(parts + [tail[...]], axis=1)
        split = keep_a.shape[2]
        half = keep_a.shape[1]
        keep_a[0], send_a[0] = joined[:half, :split], joined[half:, :split]
        keep_b[0], send_b[0] = joined[:half, split:], joined[half:, split:]


def finish_call(
    order, inputs, normed, grad_q, grad_k, grad_v, halo, cosine, sine,
    grad_after, scales, sums_second, weights,
):
    count, width = normed.shape
    _, rowmap, dests = order
    columns = 3 * width + 128
    row = pl.BlockSpec((ROWS, width), lambda i: (i, 0))
    first = pl.BlockSpec((ROWS, width), lambda i: (0, 0))
    rest = pl.BlockSpec((ROWS, width), lambda i: (jnp.maximum(i - 1, 0), 0))
    table = pl.BlockSpec((ROWS, 128), lambda i: (i + MARGIN // ROWS, 0))
    half = columns // 256 * 128
    shapes = [jax.ShapeDtypeStruct((count, width), f32)] + [
        jax.ShapeDtypeStruct((1, width // 2, size), bf16)
        for size in (half, half, columns - half, columns - half)
    ]
    return pl.pallas_call(
        finish_kernel,
        grid=(count // ROWS,),
        in_specs=[smem(), whole(rowmap.shape), row, row]
        + [whole(piece.shape) for piece in grad_q]
        + [first, rest, first, rest]
        + [whole(halo.shape), table, table, row]
        + [whole(scales.shape), whole(sums_second.shape), whole(weights.shape)],
        out_specs=[row] + [whole(shape.shape) for shape in shapes[1:]],
        out_shape=shapes,
        scratch_shapes=[
            pltpu.VMEM((width, count), bf16),
            pltpu.VMEM((count, width), bf16),
            pltpu.VMEM((count, width), bf16),
            pltpu.VMEM((count, width), bf16),
            pltpu.VMEM((128, width), f32),
            pltpu.VMEM((width, 128), bf16),
        ],
        compiler_params=params(32),
        cost_estimate=cost(0, 10),
        name="finish_rows",
    )(
        dests, rowmap, inputs, normed, *grad_q, *grad_k, *grad_v, halo, cosine, sine,
        grad_after, scales, sums_second, weights,
    )


def adam_update(master, first, second, gradient, factor, rate):
    clipped = gradient * factor
    momentum = beta_first * first + (1.0 - beta_first) * clipped
    variance = beta_second * second + (1.0 - beta_second) * clipped * clipped
    corrected = momentum / (1.0 - beta_first**STEP)
    divisor = jnp.sqrt(variance / (1.0 - beta_second**STEP)) + adam_floor
    updated = master - rate * (corrected / divisor + weight_decay * master)
    return (momentum, variance, updated, updated.astype(bf16))


def full_sum(values):
    return jnp.sum(jnp.sum(values, axis=0, keepdims=True), axis=1, keepdims=True)


def book_kernel(keep, *refs):
    parts, (out, length) = refs[:-2], refs[-2:]
    total = keep[...]
    for part in parts:
        total = total + part[...].astype(f32)
    out[...] = total
    length[...] = full_sum(jnp.sum(total * total, axis=0))


def book_call(keep, parts):
    return pl.pallas_call(
        book_kernel,
        grid=(1,),
        in_specs=[whole(keep.shape)] * (1 + len(parts)),
        out_specs=[whole(keep.shape), whole((1, 1))],
        out_shape=[
            jax.ShapeDtypeStruct(keep.shape, f32),
            jax.ShapeDtypeStruct((1, 1), f32),
        ],
        compiler_params=params(16),
        cost_estimate=cost(BOOK_SHARE, 1),
        name="book_sums",
    )(keep, *parts)


def total_kernel(groups, squares, *refs):
    outs, shared = refs[-1 - len(groups) : -1], refs[-1]
    length = squares[...]
    base = 0
    for size, out in zip(groups, outs):
        total = refs[base][0]
        for part in refs[base + 1 : base + size]:
            total = total + part[0].astype(f32)
        base += size
        out[...] = total
        length = length + full_sum(total * total)
    shared[...] = jnp.broadcast_to(length, shared.shape)


def total_call(squares, groups, count):
    operands = [array for keep, parts in groups for array in (keep, *parts)]
    sizes = [1 + len(parts) for _, parts in groups]
    shapes = [keep.shape[1:] for keep, _ in groups] + [(count, 128)]
    return pl.pallas_call(
        lambda *refs: total_kernel(sizes, *refs),
        grid=(1,),
        in_specs=[whole((1, 1))] + [whole(operand.shape) for operand in operands],
        out_specs=[whole(shape) for shape in shapes],
        out_shape=[jax.ShapeDtypeStruct(shape, f32) for shape in shapes],
        compiler_params=params(16),
        cost_estimate=cost(0, 1),
        name="last_sums",
    )(squares, *operands)


def adam_kernel(shared, grad_feed, grad_qkv, grad_book, *refs):
    masters, firsts, seconds = refs[0:15:3], refs[1:15:3], refs[2:15:3]
    norm_ref = refs[15]
    outs = [refs[16 + 4 * group : 20 + 4 * group] for group in range(5)]
    norm = jnp.sqrt(jnp.sum(shared[:, 0:1], axis=0, keepdims=True))
    norm_ref[...] = norm
    factor = clip_level / jnp.maximum(norm, clip_level)

    def update(group, index, gradient):
        results = adam_update(
            masters[group][index], firsts[group][index], seconds[group][index],
            gradient, factor, group_rates[group],
        )
        for out, result in zip(outs[group], results):
            out[index] = result

    width = (grad_qkv.shape[1] - 128) // 3
    units = masters[1].shape[2]
    depth = masters[2].shape[1]
    for k in range(3):
        update(0, k, grad_qkv[:, k * width : (k + 1) * width])
    middle = units + depth
    update(1, 0, grad_feed[:, :units])
    update(2, Ellipsis, grad_feed[:, units:middle])
    update(1, 1, grad_feed[:, middle : middle + units])
    update(0, 3, grad_feed[:, middle + units :])
    for level in range(LEVELS):
        update(3, level, grad_book[level])
    update(4, Ellipsis, grad_qkv[:, 3 * width :].T[:6])


def adam_call(shared, gradients, states):
    operands = [shared, *gradients] + [array for group in states for array in group]
    shapes = [jax.ShapeDtypeStruct((1, 1), f32)] + [
        jax.ShapeDtypeStruct(group[0].shape, kind)
        for group in states
        for kind in (f32, f32, f32, bf16)
    ]
    return pl.pallas_call(
        adam_kernel,
        grid=(1,),
        in_specs=[whole(operand.shape) for operand in operands],
        out_specs=[whole(shape.shape) for shape in shapes],
        out_shape=shapes,
        compiler_params=params(40),
        cost_estimate=cost(3, 2),
        name="adam_step",
    )(*operands)


def turn_tables(positions, depth):
    half = depth // 2
    freqs = jnp.exp(-math.log(10000.0) * jnp.arange(half, dtype=f32) * 2.0 / depth)
    angles = positions.astype(f32)[:, None] * freqs[None, :]
    cosine, sine = jnp.cos(angles), jnp.sin(angles)
    return (
        jnp.concatenate([cosine] * 4, axis=1),
        jnp.concatenate([-sine, sine, -sine, sine], axis=1),
    )


def score_bias(count, offset):
    block = jnp.arange(count // QROWS, dtype=jnp.int32)[:, None, None]
    key_place = jnp.arange(SPAN, dtype=jnp.int32)[None, :, None]
    query_place = jnp.arange(QROWS, dtype=jnp.int32)[None, None, :]
    distance = MARGIN + query_place - key_place
    reach = offset + block * QROWS + key_place - MARGIN
    allowed = (distance >= 0) & (distance <= WINDOW) & (reach >= 0)
    return jnp.where(allowed, 0.0, masked_score).astype(f32)


def body(
    inputs, codes, levels,
    attention_master, attention_first, attention_second,
    feedforward_master, feedforward_first, feedforward_second,
    projection_master, projection_first, projection_second,
    codebook_master, codebook_first, codebook_second,
    scales_master, scales_first, scales_second,
):
    spans = lax.axis_size("tm")
    devices = lax.axis_size("clip") * spans
    me = lax.axis_index("clip") * spans + lax.axis_index("tm")
    frame_count, width = inputs.shape
    units = feedforward_master.shape[2]
    depth = projection_master.shape[1]
    rows = projection_master.shape[0]
    entries = codebook_master.shape[1] * devices

    early, feed, book = lower_call(
        attention_master, feedforward_master, projection_master, codebook_master, scales_master
    )
    mid = LEVELS // 2
    book = lax.all_gather(book, AXES, axis=1, tiled=True)
    stages = len(digit_plan(devices, 3))
    split_stages = len(digit_plan(devices, 4))
    halo = lax.ppermute(
        inputs[frame_count - MARGIN :], "tm", [(i, i + 1) for i in range(spans - 1)]
    )
    for stage in reversed(range(2, len(digit_plan(devices, 2)))):
        early = join(early, gather_swaps(early, devices, 2, stage))
    mark = early
    for stage in reversed(range(4, split_stages)):
        feed = join(feed, after(gather_swaps(feed, devices, 4, stage), early))
    offset = lax.axis_index("tm") * frame_count
    positions = after(offset, mark) - MARGIN + jnp.arange(frame_count + MARGIN, dtype=jnp.int32)
    cosine, sine = turn_tables(positions, width // HEADS)
    bias = score_bias(frame_count, after(offset, mark))
    def order(kind):
        owners = jnp.asarray(device_of_places(devices, kind)) ^ after(me, mark)
        starts = (owners * rows).astype(jnp.int32)
        if rows % 16 == 0:
            places = place_of(jnp.arange(devices, dtype=jnp.int32) ^ after(me, mark), devices, kind)
            return starts, jnp.zeros((1, 128), jnp.int32), (places * rows).astype(jnp.int32)
        rowmap = (starts[:, None] + jnp.arange(rows, dtype=jnp.int32)[None, :]).reshape(1, width)
        return starts, rowmap, starts

    orders = {kind: order(kind) for kind in range(2, 6)}
    share = entries // devices
    late_codes, late_me = after((codes, me), mark)
    owners = (late_codes // share) ^ late_me
    places = jnp.where(
        jnp.arange(LEVELS)[None, :] < mid,
        place_of(owners, devices, 4),
        place_of(owners, devices, 5),
    )
    places = (places * share + late_codes % share).astype(jnp.int32)
    flat_codes = jnp.concatenate([late_codes.T, places.T], axis=0)
    flat_codes, orders = after((flat_codes, orders), mark)
    ready = (cosine, sine, bias, flat_codes, orders)
    early = join(early, after(gather_swaps(early, devices, 2, 1), ready))
    come = after(gather_swaps(feed, devices, 4, 3), early)
    early_pieces = (early, swap(early, devices, 1))
    feed_a, feed_b = join(feed, come, (units, feed.shape[1] - units), 10)
    come_a = gather_swaps(feed_a, devices, 4, 2)
    come_b = gather_swaps(feed_b, devices, 5, 2)

    normed_first, q, k, v, scales, qkv_weights = qkv_call(
        *orders[2][:2], halo, inputs, early_pieces, cosine, sine
    )
    come_a, come_b = after((come_a, come_b), q)
    feed_a, feed_b = join(feed_a, come_a), join(feed_b, come_b)
    come_a = gather_swaps(feed_a, devices, 4, 1)
    come_b = gather_swaps(feed_b, devices, 5, 1)
    mixed, logsum = attend_call(q, after(k, feed_a, feed_b), v, bias)
    come_a, come_b = after((come_a, come_b), mixed)
    feed_a, feed_b = join(feed_a, come_a), join(feed_b, come_b)
    feed_pieces = (feed_a, swap(feed_a, devices, 1), feed_b, swap(feed_b, devices, 1))
    (
        branch_first, after_first, normed_second, hidden, slope, branch_second, low_out, latent,
        latent_again, feed_weights,
    ) = forward_call((orders[4][:2], orders[5][:2]), inputs, mixed, scales, feed_pieces, units, depth)

    carried = fetch_call(levels, flat_codes, latent_again, book)
    keep_high, send_high = spread_call(mid, mid, flat_codes, carried, entries)
    come_high = swap_parts([send_high], devices, 5, 0)
    carried = after(carried, keep_high)
    keep_low, send_low = spread_call(0, mid, flat_codes, carried, entries)
    come_low = swap_parts([send_low], devices, 4, 0)
    high = reduce_split(keep_high, after(come_high, keep_low), devices, 5, 1, 0, bf16)
    low = reduce_split(keep_low, after(come_low, high[0]), devices, 4, 1, 0, bf16)

    grad_after, grad_mixed, sums_second, keep_a, send_a, keep_b, send_b = backward_call(
        (orders[4], orders[5]), after(carried, high[0], low[0]), branch_second, slope, after_first, branch_first,
        normed_second, hidden, low_out, mixed, scales, feed_weights,
    )
    come_a = swap_parts([send_a], devices, 4, 0)
    come_b = swap_parts([send_b], devices, 5, 0)
    high = reduce_split(high[0], after(high[1], keep_a), devices, 5, 2, 2)
    low = reduce_split(low[0], after(low[1], high[0]), devices, 4, 2)

    lead = MARGIN // QROWS
    blocks = frame_count // QROWS
    zeros = jnp.zeros((MARGIN, width), f32)
    fixed = (logsum, bias, cosine, sine)
    grad_mixed = after(grad_mixed, low[0])
    q_a, k_a, v_a, halo = attend_back_call(0, lead, q, k, v, grad_mixed, *fixed, zeros, zeros)
    halo = lax.ppermute(halo, "tm", [(i + 1, i) for i in range(spans - 1)])
    come_a, come_b = after((come_a, come_b), k_a)
    keep_a, come_a = reduce_split(keep_a, come_a, devices, 4, 1)
    keep_b, come_b = reduce_split(keep_b, come_b, devices, 5, 1)
    grad_mixed = after(grad_mixed, keep_a, keep_b)
    q_b, k_b, v_b, _ = attend_back_call(lead, lead, q, k, v, grad_mixed, *fixed, k_a, v_a)
    come_low, come_high = after((low[1], high[1]), k_b)
    keep_book, come_book = stack_split((low[0], come_low), (high[0], come_high), devices, 4, 3)
    grad_mixed = after(grad_mixed, keep_book)
    q_c, k_c, v_c, _ = attend_back_call(
        2 * lead, blocks - 2 * lead, q, k, v, grad_mixed, *fixed, k_b, v_b
    )
    come_book, come_a, come_b = after((come_book, come_a, come_b), k_c)
    keep_a, come_a = reduce_split(keep_a, come_a, devices, 4, 2)
    keep_b, come_b = reduce_split(keep_b, come_b, devices, 5, 2)
    for stage in range(4, split_stages):
        keep_book, come_book = reduce_split(keep_book, come_book, devices, 4, stage)
    input_gradient, qkv_a, send_a, qkv_b, send_b = finish_call(
        orders[2], inputs, normed_first, (q_a, q_b, q_c),
        (k_b, after(k_c, keep_book, keep_a, keep_b)), (v_b, v_c), halo, cosine, sine, grad_after,
        scales, sums_second, qkv_weights,
    )
    send_a = swap_parts([send_a], devices, 2, 0)
    send_b = swap_parts([send_b], devices, 2, 0)
    grad_book, squares = book_call(keep_book, after(come_book, qkv_a))
    come_a, come_b = after((come_a, come_b), grad_book)
    keep_feed, come_feed = merge_split(
        ((keep_a, come_a), (keep_b, come_b)), devices, 4, 3, FEED_SHARE
    )
    send_a, send_b = after((send_a, send_b), keep_feed)
    keep_qkv, come_qkv = merge_split(((qkv_a, send_a), (qkv_b, send_b)), devices, 2, 1)
    for stage in range(4, split_stages):
        keep_feed, come_feed = reduce_split(keep_feed, come_feed, devices, 4, stage)
    for stage in range(2, len(digit_plan(devices, 2))):
        keep_qkv, come_qkv = reduce_split(keep_qkv, come_qkv, devices, 2, stage)
    grad_feed, grad_qkv, shared = total_call(
        squares, ((keep_feed, come_feed), (keep_qkv, come_qkv)), devices
    )

    shared = lax.all_to_all(shared, AXES, 0, 0, tiled=True)
    gradient_norm, *updated = adam_call(
        shared,
        (grad_feed, grad_qkv, grad_book),
        (
            (attention_master, attention_first, attention_second),
            (feedforward_master, feedforward_first, feedforward_second),
            (projection_master, projection_first, projection_second),
            (codebook_master, codebook_first, codebook_second),
            (scales_master, scales_first, scales_second),
        ),
    )
    return (latent, input_gradient, gradient_norm[0, 0], *updated)


def solution(mesh):
    rows = P(AXES, None)
    middle = P(None, AXES, None)
    scale = P(None, AXES)
    in_specs = (rows, rows, P("clip")) + (middle,) * 6 + (rows,) * 3 + (middle,) * 3 + (scale,) * 3
    out_specs = (rows, rows, P()) + (middle,) * 8 + (rows,) * 4 + (middle,) * 4 + (scale,) * 4
    return jax.shard_map(body, mesh=mesh, in_specs=in_specs, out_specs=out_specs, check_vma=False)
```

```python
import math

import jax
import jax.numpy as jnp
import numpy as np
from jax import lax
from jax.experimental import pallas as pl
from jax.experimental.pallas import tpu as pltpu
from jax.sharding import PartitionSpec as P

HEADS = 8
LEVELS = 8
WINDOW = 250
STEP = 10
AXES = ("clip", "tm")

clip_level = 1.0
beta_first = 0.9
beta_second = 0.95
adam_floor = 1e-08
weight_decay = 0.1
group_rates = (0.05, 0.03, 0.05, 0.5, 0.5)
masked_score = -1e30

f32 = jnp.float32
bf16 = jnp.bfloat16
MARGIN = (WINDOW + 127) // 128 * 128
QROWS = 128
SPAN = QROWS + MARGIN
ROWS = 256
MIB = 1 << 20
FEED_SHARE, BOOK_SHARE = 4, 2


def dot(left, right, contract=((1,), (0,))):
    return lax.dot_general(left, right, (contract, ((), ())), preferred_element_type=f32)


def dot_nt(left, right):
    return dot(left, right, ((1,), (1,)))


def flip(block):
    return block.astype(f32).T.astype(bf16)


def params(mib):
    return pltpu.CompilerParams(vmem_limit_bytes=mib * MIB)


def whole(shape):
    return pl.BlockSpec(tuple(shape), lambda *_: (0,) * len(shape))


def smem():
    return pl.BlockSpec(memory_space=pltpu.SMEM)


def cost(share, length=1):
    return pl.CostEstimate(flops=int(share * 500000000), bytes_accessed=length * 3 * MIB, transcendentals=0)


def after(value, *earlier):
    return lax.optimization_barrier((value, earlier))[0]


def digit_plan(count, kind):
    bits = count.bit_length() - 1
    middle = [(1, 4)] if kind < 4 else [(1, 2), (2, 2)] if kind == 4 else [(2, 2), (1, 2)]
    plan, shift = [(0, 2)] + middle, 3
    while shift < bits:
        width = min(2, bits - shift) if kind == 2 else 1
        plan.append((shift, 1 << width))
        shift += width
    return plan


def swap(block, count, mask):
    return lax.ppermute(block, AXES, [(i, i ^ mask) for i in range(count)])


def gather_swaps(block, count, kind, stage):
    shift, radix = digit_plan(count, kind)[stage]
    return [swap(block, count, k << shift) for k in range(1, radix)]


def join_kernel(count, widths, *refs):
    outs = refs[count:]
    top = 0
    for part in refs[:count]:
        rows, left = part.shape[0], 0
        for out, width in zip(outs, widths):
            out[top : top + rows, :] = part[:, left : left + width]
            left += width
        top += rows


def join(block, others, widths=None, share=0):
    parts = [block, *others]
    rows, columns = block.shape
    widths = widths or (columns,)
    if rows % 16:
        whole_block = jnp.concatenate(parts, axis=0)
        edges = [sum(widths[:index]) for index in range(len(widths) + 1)]
        outs = [whole_block[:, left:right] for left, right in zip(edges, edges[1:])]
    else:
        outs = pl.pallas_call(
            lambda *refs: join_kernel(len(parts), widths, *refs),
            grid=(1,),
            in_specs=[whole(part.shape) for part in parts],
            out_specs=[whole((len(parts) * rows, width)) for width in widths],
            out_shape=[
                jax.ShapeDtypeStruct((len(parts) * rows, width), block.dtype) for width in widths
            ],
            compiler_params=params(16),
            cost_estimate=cost(share, 1),
            name="join_rows",
        )(*parts)
    return outs[0] if len(widths) == 1 else outs


def place_of(device, count, kind):
    place, weight = 0, 1
    for shift, radix in reversed(digit_plan(count, kind)):
        place = place + ((device >> shift) & (radix - 1)) * weight
        weight *= radix
    return place


def device_of_places(count, kind):
    table = np.zeros(count, np.int32)
    for device in range(count):
        table[place_of(device, count, kind)] = device
    return table


def swap_parts(parts, count, kind, stage):
    shift, _ = digit_plan(count, kind)[stage]
    return [swap(part, count, (k + 1) << shift) for k, part in enumerate(parts)]


def reduce_add(keep, parts):
    total = keep.astype(f32)
    for part in parts:
        total = total + part.astype(f32)
    return total


def split_kernel(radix, *refs):
    outs, operands = refs[-radix:], refs[:-radix]
    total = operands[0][...].astype(f32)
    for operand in operands[1:]:
        total = total + operand[...].astype(f32)
    size = total.shape[1] // radix
    for k, out in enumerate(outs):
        out[...] = total[:, k * size : (k + 1) * size, :].astype(out.dtype)


def reduce_split(keep, parts, count, kind, stage, share=0, held=f32):
    _, radix = digit_plan(count, kind)[stage]
    lead, rows, columns = keep.shape
    size = rows // radix
    if lead > 1:
        group = lead if held == bf16 else 1
        steps, block, index = lead // group, (group, rows, columns), lambda i: (i, 0, 0)
    else:
        steps = 2 if columns % 256 == 0 else 1
        block, index = (1, rows, columns // steps), lambda i: (0, 0, i)
    shares = (block[0], size, block[2])
    kinds = [held] + [bf16] * (radix - 1)
    outs = pl.pallas_call(
        lambda *refs: split_kernel(radix, *refs),
        grid=(steps,),
        in_specs=[pl.BlockSpec(block, index)] * (1 + len(parts)),
        out_specs=[pl.BlockSpec(shares, index)] * radix,
        out_shape=[jax.ShapeDtypeStruct((lead, size, columns), kind) for kind in kinds],
        compiler_params=params(20),
        cost_estimate=cost(share, 1),
        name="split_sums",
    )(keep, *parts)
    return outs[0], swap_parts(outs[1:], count, kind, stage)


def merge_kernel(radix, groups, *refs):
    outs = refs[-radix:]
    base = left = 0
    for size in groups:
        total = refs[base][...].astype(f32)
        for operand in refs[base + 1 : base + size]:
            total = total + operand[...].astype(f32)
        base += size
        rows = total.shape[1] // radix
        for k, out in enumerate(outs):
            share = total[:, k * rows : (k + 1) * rows, :].astype(out.dtype)
            out[:, :, left : left + total.shape[2]] = share
        left += total.shape[2]


def merge_split(groups, count, kind, stage, share=0):
    _, radix = digit_plan(count, kind)[stage]
    operands = [array for keep, parts in groups for array in (keep, *parts)]
    _, rows, _ = groups[0][0].shape
    shape = (1, rows // radix, sum(keep.shape[2] for keep, _ in groups))
    sizes = [1 + len(parts) for _, parts in groups]
    kinds = [f32] + [bf16] * (radix - 1)
    outs = pl.pallas_call(
        lambda *refs: merge_kernel(radix, sizes, *refs),
        grid=(1,),
        in_specs=[whole(operand.shape) for operand in operands],
        out_specs=[whole(shape)] * radix,
        out_shape=[jax.ShapeDtypeStruct(shape, kind) for kind in kinds],
        compiler_params=params(20),
        cost_estimate=cost(share, 1),
        name="split_sums",
    )(*operands)
    return outs[0], swap_parts(outs[1:], count, kind, stage)


def stack_kernel(radix, half, *refs):
    outs, operands = refs[-radix:], refs[:-radix]
    size = operands[0].shape[1] // radix

    def add(parts):
        total = sum(part[...].astype(f32) for part in parts)
        for k, out in enumerate(outs):
            out[...] = total[:, k * size : (k + 1) * size, :].astype(out.dtype)

    @pl.when(pl.program_id(0) < half)
    def _():
        add(operands[: len(operands) // 2])

    @pl.when(pl.program_id(0) >= half)
    def _():
        add(operands[len(operands) // 2 :])


def stack_split(low, high, count, kind, stage, share=0):
    _, radix = digit_plan(count, kind)[stage]
    operands = [low[0], *low[1], high[0], *high[1]]
    half, rows, columns = low[0].shape
    kinds = [f32] + [bf16] * (radix - 1)
    block = (1, rows, columns)
    below = pl.BlockSpec(block, lambda i: (jnp.minimum(i, half - 1), 0, 0))
    above = pl.BlockSpec(block, lambda i: (jnp.maximum(i - half, 0), 0, 0))
    outs = pl.pallas_call(
        lambda *refs: stack_kernel(radix, half, *refs),
        grid=(2 * half,),
        in_specs=[below] * (1 + len(low[1])) + [above] * (1 + len(high[1])),
        out_specs=[pl.BlockSpec((1, rows // radix, columns), lambda i: (i, 0, 0))] * radix,
        out_shape=[
            jax.ShapeDtypeStruct((2 * half, rows // radix, columns), kind) for kind in kinds
        ],
        compiler_params=params(20),
        cost_estimate=cost(share, 2),
        name="split_sums",
    )(*operands)
    return outs[0], swap_parts(outs[1:], count, kind, stage)


def one_hot_rows(rowmap, size):
    place = lax.broadcasted_iota(jnp.int32, (size, size), 0)
    return jnp.where(place == rowmap, 1.0, 0.0).astype(bf16)


def unpack_rows(starts_ref, rowmap_ref, pieces, out_ref):
    half = pieces[0].shape[0]
    count = starts_ref.shape[0]
    rows = 2 * half // count
    if rows % 16 == 0:
        for place in range(count):
            piece = pieces[place * rows // half]
            inner = place * rows % half
            start = pl.multiple_of(starts_ref[place], rows)
            out_ref[pl.ds(start, rows), :] = piece[inner : inner + rows, :]
    else:
        spread = one_hot_rows(rowmap_ref[0:1, :], 2 * half)
        columns = out_ref.shape[1]
        for left in range(0, columns, 128):
            joined = jnp.concatenate([p[:, left : left + 128] for p in pieces], axis=0)
            out_ref[:, left : left + 128] = dot(spread, joined).astype(bf16)


def store_flipped(dests_ref, rowmap_ref, block, out_ref, lanes):
    flipped = flip(block)
    size = flipped.shape[0]
    count = dests_ref.shape[0]
    rows = size // count
    if rows % 16 == 0:
        for index in range(count):
            start = pl.multiple_of(dests_ref[index], rows)
            out_ref[pl.ds(start, rows), lanes] = flipped[index * rows : (index + 1) * rows]
    else:
        spread = one_hot_rows(rowmap_ref[0:1, :], size)
        out_ref[:, lanes] = dot(spread, flipped, ((0,), (0,))).astype(bf16)


def store_halves(values, keep, send, lanes):
    half = keep.shape[1]
    keep[0, :, lanes] = values[:half].astype(bf16)
    send[0, :, lanes] = values[half:].astype(bf16)


def centre_rows(values):
    centred = values - jnp.mean(values, axis=-1, keepdims=True)
    spread = jnp.mean(centred * centred, axis=-1, keepdims=True)
    rstd = lax.rsqrt(spread + 1e-05)
    return centred * rstd, rstd


def norm_back(normal, rstd, gain, grad):
    inner = grad * gain
    first = jnp.mean(inner, axis=-1, keepdims=True)
    second = jnp.mean(inner * normal, axis=-1, keepdims=True)
    return rstd * (inner - first - normal * second)


def column_sum(values):
    return jnp.sum(values, axis=0, keepdims=True)


def turn(values, cosine, sine):
    lanes = values.shape[1]
    ahead = pltpu.roll(values, lanes - 32, 1)
    behind = pltpu.roll(values, 32, 1)
    lane = lax.broadcasted_iota(jnp.int32, values.shape, 1)
    partner = jnp.where(lane % 64 < 32, ahead, behind)
    repeats = lanes // cosine.shape[1]
    if repeats > 1:
        cosine = jnp.concatenate([cosine] * repeats, axis=1)
        sine = jnp.concatenate([sine] * repeats, axis=1)
    return values * cosine + partner * sine


def head_columns(flipped):
    zero = jnp.zeros((64, flipped.shape[1]), flipped.dtype)
    return jnp.concatenate(
        [
            jnp.concatenate([flipped[:64], zero], axis=1),
            jnp.concatenate([zero, flipped[64:]], axis=1),
        ],
        axis=0,
    )


def head_rows(block):
    lane = lax.broadcasted_iota(jnp.int32, block.shape, 1)
    zero = jnp.zeros_like(block)
    return jnp.concatenate(
        [jnp.where(lane < 64, block, zero), jnp.where(lane < 64, zero, block)], axis=0
    )


def lower_kernel(attention, feed, projection, book, scales, early, later, low_book, work):
    width = attention.shape[2]
    units = feed.shape[2]
    rows = attention.shape[1]
    for k in range(3):
        early[:, k * width : (k + 1) * width] = attention[k].astype(bf16)
    work[...] = jnp.zeros(work.shape, f32)
    work[: scales.shape[0], :rows] = scales[...]
    early[:, 3 * width :] = work[...].T[:rows].astype(bf16)
    for k in range(2):
        later[:, k * units : (k + 1) * units] = feed[k].astype(bf16)
    last = 2 * units + projection.shape[1]
    later[:, 2 * units : last] = projection[...].astype(bf16)
    later[:, last:] = attention[3].astype(bf16)
    low_book[...] = book[...].astype(bf16)


def lower_call(attention, feed, projection, book, scales):
    _, rows, width = attention.shape
    columns = 2 * feed.shape[2] + projection.shape[1] + width
    shapes = ((rows, 3 * width + 128), (rows, columns), book.shape)
    operands = (attention, feed, projection, book, scales)
    return pl.pallas_call(
        lower_kernel,
        grid=(1,),
        in_specs=[whole(operand.shape) for operand in operands],
        out_specs=[whole(shape) for shape in shapes],
        out_shape=[jax.ShapeDtypeStruct(shape, bf16) for shape in shapes],
        scratch_shapes=[pltpu.VMEM((128, 128), f32)],
        compiler_params=params(62),
        cost_estimate=cost(0, 1),
        name="lower_weights",
    )(*operands)


def qkv_kernel(
    starts, rowmap, halo, inputs, piece_a, piece_b, cosine, sine, normed, q, k, v, scales, weights
):
    step = pl.program_id(0)
    width = inputs.shape[1]

    @pl.when(step == 0)
    def _():
        unpack_rows(starts, rowmap, (piece_a, piece_b), weights)
        scales[...] = weights[:, 3 * width :].astype(f32).T[:8]

    frames = jnp.where(step == 0, halo[...].astype(f32), inputs[...].astype(f32))
    normal, _ = centre_rows(frames)
    low = (normal * scales[0:1, :] + scales[1:2, :]).astype(bf16)
    normed[...] = low
    turned = turn(dot(low, weights[:, :width]), cosine[...], sine[...])
    q[...] = (turned.astype(bf16).astype(f32) * 0.125).astype(bf16)
    k[...] = turn(dot(low, weights[:, width : 2 * width]), cosine[...], sine[...]).astype(bf16)
    v[...] = dot(low, weights[:, 2 * width : 3 * width]).astype(bf16)


def qkv_call(starts, rowmap, halo, inputs, pieces, cosine, sine):
    count, width = inputs.shape
    columns = pieces[0].shape[1]
    steps = count // ROWS + 1
    late = lambda i: (jnp.maximum(i - 1, 0), 0)
    here = lambda i: (i, 0)
    return pl.pallas_call(
        qkv_kernel,
        grid=(steps,),
        in_specs=[
            smem(),
            whole(rowmap.shape),
            whole(halo.shape),
            pl.BlockSpec((ROWS, width), late),
            whole(pieces[0].shape),
            whole(pieces[1].shape),
            pl.BlockSpec((ROWS, 128), here),
            pl.BlockSpec((ROWS, 128), here),
        ],
        out_specs=[
            pl.BlockSpec((ROWS, width), late),
            pl.BlockSpec((ROWS, width), late),
            pl.BlockSpec((ROWS, width), here),
            pl.BlockSpec((ROWS, width), here),
            whole((8, width)),
            whole((width, columns)),
        ],
        out_shape=[
            jax.ShapeDtypeStruct((count, width), bf16),
            jax.ShapeDtypeStruct((count, width), bf16),
            jax.ShapeDtypeStruct((count + MARGIN, width), bf16),
            jax.ShapeDtypeStruct((count + MARGIN, width), bf16),
            jax.ShapeDtypeStruct((8, width), f32),
            jax.ShapeDtypeStruct((width, columns), bf16),
        ],
        compiler_params=params(32),
        cost_estimate=cost(4, 8),
        name="project_rows",
    )(starts, rowmap, halo, inputs, *pieces, cosine, sine)


def attend_kernel(q, k, v, bias, mixed, logsum):
    step = pl.program_id(0)
    start = pl.multiple_of(step * QROWS, QROWS)
    keys = pl.ds(start, SPAN)
    allowed = jnp.concatenate([bias[0], bias[0]], axis=1)
    lane = lax.broadcasted_iota(jnp.int32, (QROWS, 128), 1)
    pairs = [slice(left, left + 128) for left in range(0, q.shape[1], 128)]
    columns = [head_columns(flip(q[:, lanes])) for lanes in pairs]
    scores = [dot(k[keys, lanes], column) + allowed for lanes, column in zip(pairs, columns)]
    highest = [jnp.max(score, axis=0, keepdims=True) for score in scores]
    raised = [jnp.exp(score - high) for score, high in zip(scores, highest)]
    totals = [column_sum(part) for part in raised]
    weights = [(part * (1.0 / total)).astype(bf16) for part, total in zip(raised, totals)]
    outputs = [
        dot(weight, v[keys, lanes], ((0,), (0,))) for weight, lanes in zip(weights, pairs)
    ]
    rows = []
    for lanes, output, high, total in zip(pairs, outputs, highest, totals):
        mixed[:, lanes] = jnp.where(lane < 64, output[:QROWS], output[QROWS:]).astype(bf16)
        record = high + jnp.log(total)
        rows += [record[:, :QROWS], record[:, QROWS:]]
    logsum[...] = jnp.concatenate(rows, axis=0)


def attend_call(q, k, v, bias):
    count, width = q.shape
    return pl.pallas_call(
        attend_kernel,
        grid=(count // QROWS,),
        in_specs=[
            pl.BlockSpec((QROWS, width), lambda i: (i, 0)),
            whole(k.shape),
            whole(v.shape),
            pl.BlockSpec((1, SPAN, QROWS), lambda i: (i, 0, 0)),
        ],
        out_specs=[
            pl.BlockSpec((QROWS, width), lambda i: (i, 0)),
            pl.BlockSpec((HEADS, QROWS), lambda i: (0, i)),
        ],
        out_shape=[
            jax.ShapeDtypeStruct((count, width), bf16),
            jax.ShapeDtypeStruct((HEADS, count), f32),
        ],
        compiler_params=params(24),
        cost_estimate=cost(4, 14),
        name="attend_rows",
    )(q, k, v, bias)


def forward_kernel(
    starts_a, rowmap_a, starts_b, rowmap_b, inputs, mixed, scales, own_a, other_a, own_b, other_b,
    branch_first, after_first, normed, hidden, slope, branch_second, low_out, latent, again, weights,
):
    step = pl.program_id(0)
    width = inputs.shape[1]
    units = hidden.shape[1]

    @pl.when(step == 0)
    def _():
        unpack_rows(starts_a, rowmap_a, (own_a, other_a), weights.at[:, :units])
        unpack_rows(starts_b, rowmap_b, (own_b, other_b), weights.at[:, units:])

    up, down = 0, units
    proj = 2 * units
    last = proj + latent.shape[1]
    first = dot(mixed[...], weights[:, last : last + width])
    branch_first[...] = first.astype(bf16)
    after = inputs[...].astype(f32) + scales[4:5, :] * first
    after_first[...] = after
    normal, _ = centre_rows(after)
    low = (normal * scales[2:3, :] + scales[3:4, :]).astype(bf16)
    normed[...] = low
    chunk = 512
    lefts = range(0, units, chunk)
    pres = [dot(low, weights[:, up + left : up + left + chunk]) for left in lefts]
    for left, pre in zip(lefts, pres):
        share = 0.5 + 0.5 * lax.erf(pre * (1.0 / math.sqrt(2.0)))
        bell = jnp.exp(-0.5 * pre * pre) * (1.0 / math.sqrt(2.0 * math.pi))
        hidden[:, left : left + chunk] = (pre * share).astype(bf16)
        slope[:, left : left + chunk] = (share + pre * bell).astype(bf16)
    second = dot_nt(hidden[...], weights[:, down : down + units])
    branch_second[...] = second.astype(bf16)
    rounded = (after + scales[5:6, :] * second).astype(bf16)
    low_out[...] = rounded
    result = dot(rounded, weights[:, proj:last])
    latent[...] = result
    again[...] = result


def forward_call(orders, inputs, mixed, scales, pieces, units, depth):
    count, width = inputs.shape
    columns = pieces[0].shape[1] + pieces[2].shape[1]
    row = lambda size: pl.BlockSpec((ROWS, size), lambda i: (i, 0))
    kept = ((width, bf16), (width, f32), (width, bf16), (units, bf16), (units, bf16),
            (width, bf16), (width, bf16), (depth, f32), (depth, f32))
    (starts_a, rowmap_a), (starts_b, rowmap_b) = orders
    return pl.pallas_call(
        forward_kernel,
        grid=(count // ROWS,),
        in_specs=[smem(), whole(rowmap_a.shape)] * 2
        + [row(width), row(width), whole(scales.shape)]
        + [whole(piece.shape) for piece in pieces],
        out_specs=[row(size) for size, _ in kept] + [whole((width, columns))],
        out_shape=[jax.ShapeDtypeStruct((count, size), kind) for size, kind in kept]
        + [jax.ShapeDtypeStruct((width, columns), bf16)],
        compiler_params=params(56),
        cost_estimate=cost(4, 17),
        name="feed_rows",
    )(starts_a, rowmap_a, starts_b, rowmap_b, inputs, mixed, scales, *pieces)


def fetch_kernel(active, codes, latent, book, carried, residue, steps, columns):
    level = pl.program_id(0)
    count, depth = latent.shape
    tiles = book.shape[1] // 256

    @pl.when(level == 0)
    def _():
        residue[...] = latent[...]
        columns[...] = codes[:LEVELS, :].astype(f32).T

    factor = jnp.where(level < active[0], 1.0, 0.0).astype(f32)
    lane = lax.broadcasted_iota(jnp.int32, (ROWS, LEVELS), 1)
    place = lax.broadcasted_iota(jnp.int32, (ROWS, 256), 1).astype(f32)
    blocks = [slice(top, top + ROWS) for top in range(0, count, ROWS)]
    picked = []
    for rows in blocks:
        code = jnp.where(lane == level, columns[rows, :], 0.0)
        code = jnp.sum(code, axis=1, keepdims=True)
        high = jnp.floor(code * (1.0 / 256.0))
        hit = jnp.where(place == code - 256.0 * high, 1.0, 0.0).astype(bf16)
        picks = [hit * jnp.where(high == j, 1.0, 0.0).astype(bf16) for j in range(tiles)]
        picked.append(jnp.concatenate(picks, axis=1))
    found = [dot(pick, book[0]) for pick in picked]
    for rows, row in zip(blocks, found):
        left = residue[rows, :] - factor * row
        residue[rows, :] = left
        steps[level, rows, :] = factor * left

    @pl.when(level == LEVELS - 1)
    def _():
        for top in range(0, count, ROWS):
            rows = slice(top, top + ROWS)
            total = jnp.zeros((ROWS, depth), f32)
            for index in reversed(range(LEVELS)):
                total = total + steps[index, rows, :]
                carried[index, rows, :] = total.astype(bf16)


def fetch_call(active, codes, latent, book):
    count, depth = latent.shape
    entries = book.shape[1]
    return pl.pallas_call(
        fetch_kernel,
        grid=(LEVELS,),
        in_specs=[
            smem(),
            whole(codes.shape),
            whole(latent.shape),
            pl.BlockSpec((1, entries, depth), lambda i: (i, 0, 0)),
        ],
        out_specs=whole((LEVELS, count, depth)),
        out_shape=jax.ShapeDtypeStruct((LEVELS, count, depth), bf16),
        scratch_shapes=[
            pltpu.VMEM((count, depth), f32),
            pltpu.VMEM((LEVELS, count, depth), f32),
            pltpu.VMEM((count, LEVELS), f32),
        ],
        compiler_params=params(48),
        cost_estimate=cost(4, 13),
        name="fetch_codes",
    )(active, codes, latent, book)


def spread_kernel(first, codes, carried, keep, send):
    count = carried.shape[1]
    half = keep.shape[1]
    level = pl.program_id(0) + first
    code = codes[pl.ds(LEVELS + level, 1), :]
    high = code >> 8
    place = lax.broadcasted_iota(jnp.int32, (256, count), 0)
    hit = jnp.where(place == (code & 255), -1.0, 0.0).astype(bf16)
    for j in range(2 * half // 256):
        pick = hit * jnp.where(high == j, 1.0, 0.0).astype(bf16)
        out, inner = (keep, send)[j * 256 // half], j * 256 % half
        out[0, inner : inner + 256, :] = dot(pick, carried[0]).astype(bf16)


def spread_call(first, levels, codes, carried, entries):
    _, count, depth = carried.shape
    half = entries // 2
    return pl.pallas_call(
        lambda *refs: spread_kernel(first, *refs),
        grid=(levels,),
        in_specs=[
            whole(codes.shape),
            pl.BlockSpec((1, count, depth), lambda i: (i + first, 0, 0)),
        ],
        out_specs=[pl.BlockSpec((1, half, depth), lambda i: (i, 0, 0))] * 2,
        out_shape=[jax.ShapeDtypeStruct((levels, half, depth), bf16)] * 2,
        compiler_params=params(16),
        cost_estimate=cost(1, 5),
        name="spread_codes",
    )(codes, carried)


def backward_kernel(
    dests_a, rowmap_a, dests_b, rowmap_b, carried, branch_second, slope, after_first, branch_first, normed, hidden, low_out, mixed,
    scales, weights,
    out_after, out_mixed, sums, keep_a, send_a, keep_b, send_b,
    grad_pre, kept_hidden, kept_carried, grad_branch, flipped,
):
    step = pl.program_id(0)
    last_step = pl.num_programs(0) - 1
    width = after_first.shape[1]
    units = slope.shape[1]
    proj = 2 * units
    last = proj + carried.shape[2]
    chunk = 512
    rows = pl.ds(pl.multiple_of(step * ROWS, ROWS), ROWS)

    @pl.when(step == 0)
    def _():
        sums[...] = jnp.zeros(sums.shape, f32)

    grad_after = dot_nt(carried[0], weights[:, proj:last])
    sums[5:6, :] += column_sum(grad_after * branch_second[...].astype(f32))
    low = (grad_after * scales[5:6, :]).astype(bf16)
    grad_normed = jnp.zeros(grad_after.shape, f32)
    for left in range(0, units, chunk):
        grad_hidden = dot(low, weights[:, units + left : units + left + chunk])
        part = (grad_hidden * slope[:, left : left + chunk].astype(f32)).astype(bf16)
        grad_pre[rows, left : left + chunk] = part
        grad_normed = grad_normed + dot_nt(part, weights[:, left : left + chunk])
    normal, rstd = centre_rows(after_first[...])
    sums[2:3, :] += column_sum(grad_normed * normal)
    sums[3:4, :] += column_sum(grad_normed)
    grad_first = grad_after + norm_back(normal, rstd, scales[2:3, :], grad_normed)
    out_after[...] = grad_first.astype(bf16)
    sums[4:5, :] += column_sum(grad_first * branch_first[...].astype(f32))
    low_first = (grad_first * scales[4:5, :]).astype(bf16)
    grad_branch[rows, :] = low_first
    out_mixed[...] = dot_nt(low_first, weights[:, last : last + width]).astype(bf16)
    kept_hidden[rows, :] = hidden[...]
    kept_carried[rows, :] = carried[0]
    for index, block in enumerate((normed[...], low_out[...])):
        store_flipped(dests_a, rowmap_a, block, flipped.at[index], rows)
    for index, block in enumerate((low, mixed[...])):
        store_flipped(dests_b, rowmap_b, block, flipped.at[2 + index], rows)

    @pl.when(step == last_step)
    def _():
        for left in range(0, units, chunk):
            lanes = slice(left, left + chunk)
            store_halves(dot(flipped[0], grad_pre[:, lanes]), keep_a, send_a, lanes)
            store_halves(dot(flipped[2], kept_hidden[:, lanes]), keep_b, send_b, lanes)
        rest = slice(units, keep_a.shape[2])
        store_halves(dot(flipped[1], kept_carried[...]), keep_a, send_a, rest)
        rest = slice(units, keep_b.shape[2])
        store_halves(dot(flipped[3], grad_branch[...]), keep_b, send_b, rest)


def backward_call(
    orders, carried, branch_second, slope, after_first, branch_first, normed, hidden, low_out,
    mixed, scales, weights,
):
    count, width = after_first.shape
    units, depth = slope.shape[1], carried.shape[2]
    row = lambda size: pl.BlockSpec((ROWS, size), lambda i: (i, 0))
    pieces = [(1, width // 2, units + extra) for extra in (depth, depth, width, width)]
    (_, rowmap_a, dests_a), (_, rowmap_b, dests_b) = orders
    return pl.pallas_call(
        backward_kernel,
        grid=(count // ROWS,),
        in_specs=[smem(), whole(rowmap_a.shape)] * 2
        + [pl.BlockSpec((1, ROWS, depth), lambda i: (0, i, 0))]
        + [row(width), row(units), row(width), row(width), row(width), row(units), row(width)]
        + [row(width), whole(scales.shape), whole(weights.shape)],
        out_specs=[row(width), row(width), whole((8, width))] + [whole(piece) for piece in pieces],
        out_shape=[
            jax.ShapeDtypeStruct((count, width), bf16),
            jax.ShapeDtypeStruct((count, width), bf16),
            jax.ShapeDtypeStruct((8, width), f32),
        ]
        + [jax.ShapeDtypeStruct(piece, bf16) for piece in pieces],
        scratch_shapes=[
            pltpu.VMEM((count, units), bf16),
            pltpu.VMEM((count, units), bf16),
            pltpu.VMEM((count, depth), bf16),
            pltpu.VMEM((count, width), bf16),
            pltpu.VMEM((4, width, count), bf16),
        ],
        compiler_params=params(56),
        cost_estimate=cost(2, 25),
        name="feed_back",
    )(
        dests_a, rowmap_a, dests_b, rowmap_b, carried, branch_second, slope, after_first, branch_first, normed, hidden,
        low_out, mixed, scales, weights,
    )


def attend_back_kernel(pieces, *refs):
    k_refs, v_refs = refs[:pieces], refs[pieces : 2 * pieces]
    (q, grad, logsum, bias, cosine, sine, start_k, start_v,
     grad_q, grad_k, grad_v, halo, k, v) = refs[2 * pieces :]
    step = pl.program_id(0)

    @pl.when(step == 0)
    def _():
        for index in range(pieces):
            rows = slice(index * MARGIN, (index + 1) * MARGIN)
            k[rows, :] = k_refs[index][...]
            v[rows, :] = v_refs[index][...]
        grad_k[:MARGIN, :] = start_k[...]
        grad_v[:MARGIN, :] = start_v[...]
        grad_k[MARGIN:, :] = jnp.zeros_like(grad_k[MARGIN:, :])
        grad_v[MARGIN:, :] = jnp.zeros_like(grad_v[MARGIN:, :])

    start = pl.multiple_of(step * QROWS, QROWS)
    keys = pl.ds(start, SPAN)
    allowed = jnp.concatenate([bias[0], bias[0]], axis=1)
    lane = lax.broadcasted_iota(jnp.int32, (QROWS, 128), 1)
    pairs = [slice(left, left + 128) for left in range(0, q.shape[1], 128)]
    records = [
        jnp.concatenate([logsum[h : h + 1, :], logsum[h + 1 : h + 2, :]], axis=1)
        for h in range(0, HEADS, 2)
    ]
    scores = [dot(k[keys, lanes], head_columns(flip(q[:, lanes]))) + allowed for lanes in pairs]
    grads = [dot(v[keys, lanes], head_columns(flip(grad[:, lanes]))) for lanes in pairs]
    weights = [jnp.exp(score - record) for score, record in zip(scores, records)]
    products = [weight * part for weight, part in zip(weights, grads)]
    inners = [column_sum(product) for product in products]
    grad_scores = [
        (product - weight * inner).astype(bf16)
        for product, weight, inner in zip(products, weights, inners)
    ]
    low = [weight.astype(bf16) for weight in weights]
    for lanes, weight in zip(pairs, low):
        grad_v[keys, lanes] += dot(weight, head_rows(grad[:, lanes]))
    for lanes, part in zip(pairs, grad_scores):
        grad_k[keys, lanes] += dot(part, head_rows(q[:, lanes]))
    joined = [dot(part, k[keys, lanes], ((0,), (0,))) for lanes, part in zip(pairs, grad_scores)]
    back = -sine[...]
    for lanes, part in zip(pairs, joined):
        flat = jnp.where(lane < 64, part[:QROWS], part[QROWS:]) * 0.125
        grad_q[:, lanes] = turn(flat, cosine[...], back).astype(bf16)

    @pl.when(step == pl.num_programs(0) - 1)
    def _():
        halo[:MARGIN, :] = grad_k[:MARGIN, :].astype(bf16)
        halo[MARGIN:, :] = grad_v[:MARGIN, :].astype(bf16)


def attend_back_call(offset, blocks, q, k, v, grad, logsum, bias, cosine, sine, start_k, start_v):
    width = q.shape[1]
    keys = blocks * QROWS + MARGIN
    lead = MARGIN // QROWS
    pieces = keys // MARGIN
    there = lambda i: (i + offset, 0)
    table = lambda i: (i + offset + lead, 0)
    fixed = lambda index: pl.BlockSpec((MARGIN, width), lambda i: (index, 0))
    return pl.pallas_call(
        lambda *refs: attend_back_kernel(pieces, *refs),
        grid=(blocks,),
        in_specs=[fixed(offset // lead + index) for index in range(pieces)] * 2
        + [
            pl.BlockSpec((QROWS, width), there),
            pl.BlockSpec((QROWS, width), there),
            pl.BlockSpec((HEADS, QROWS), lambda i: (0, i + offset)),
            pl.BlockSpec((1, SPAN, QROWS), lambda i: (i + offset, 0, 0)),
            pl.BlockSpec((QROWS, 128), table),
            pl.BlockSpec((QROWS, 128), table),
            fixed(start_k.shape[0] // MARGIN - 1),
            fixed(start_v.shape[0] // MARGIN - 1),
        ],
        out_specs=[
            pl.BlockSpec((QROWS, width), lambda i: (i, 0)),
            whole((keys, width)),
            whole((keys, width)),
            whole((2 * MARGIN, width)),
        ],
        out_shape=[
            jax.ShapeDtypeStruct((blocks * QROWS, width), bf16),
            jax.ShapeDtypeStruct((keys, width), f32),
            jax.ShapeDtypeStruct((keys, width), f32),
            jax.ShapeDtypeStruct((2 * MARGIN, width), bf16),
        ],
        scratch_shapes=[
            pltpu.VMEM((keys, width), bf16),
            pltpu.VMEM((keys, width), bf16),
        ],
        compiler_params=params(20),
        cost_estimate=cost(0 if offset > 0 else 8, 2 * blocks),
        name="attend_back",
    )(*[k] * pieces, *[v] * pieces, q, grad, logsum, bias, cosine, sine, start_k, start_v)


def finish_kernel(
    dests, rowmap, inputs, normed, q_a, q_b, q_c, k_a, k_b, v_a, v_b, halo, cosine, sine,
    grad_after, scales, sums_second, weights,
    out, keep_a, send_a, keep_b, send_b, flipped, turned_q, turned_k, turned_v, sums, tail,
):
    step = pl.program_id(0)
    last = pl.num_programs(0) - 1
    width = normed.shape[1]

    @pl.when(step == 0)
    def _():
        sums[...] = jnp.zeros(sums.shape, f32)
        sums[:8, :] = sums_second[...]
        left = 0
        for piece in (q_a, q_b, q_c):
            turned_q[left : left + piece.shape[0], :] = piece[...]
            left += piece.shape[0]

    rows = pl.ds(pl.multiple_of(step * ROWS, ROWS), ROWS)
    near = jnp.where(step == last, 1.0, 0.0).astype(f32)
    part_k = jnp.where(step == 0, k_a[...], k_b[...]) + near * halo[:MARGIN, :].astype(f32)
    part_v = jnp.where(step == 0, v_a[...], v_b[...]) + near * halo[MARGIN:, :].astype(f32)
    turned = turn(part_k, cosine[...], -sine[...]).astype(bf16)
    turned_k[rows, :] = turned
    value = part_v.astype(bf16)
    turned_v[rows, :] = value
    grad = dot_nt(turned_q[rows, :], weights[:, :width])
    grad = grad + dot_nt(turned, weights[:, width : 2 * width])
    grad = grad + dot_nt(value, weights[:, 2 * width : 3 * width])
    normal, rstd = centre_rows(inputs[...].astype(f32))
    sums[0:1, :] += column_sum(grad * normal)
    sums[1:2, :] += column_sum(grad)
    out[...] = grad_after[...].astype(f32) + norm_back(normal, rstd, scales[0:1, :], grad)

    store_flipped(dests, rowmap, normed[...], flipped, rows)

    @pl.when(step == last)
    def _():
        store_flipped(dests, rowmap, sums[...], tail, slice(None))
        parts = [dot(flipped[...], ref[...]).astype(bf16) for ref in (turned_q, turned_k, turned_v)]
        joined = jnp.concatenate(parts + [tail[...]], axis=1)
        split = keep_a.shape[2]
        half = keep_a.shape[1]
        keep_a[0], send_a[0] = joined[:half, :split], joined[half:, :split]
        keep_b[0], send_b[0] = joined[:half, split:], joined[half:, split:]


def finish_call(
    order, inputs, normed, grad_q, grad_k, grad_v, halo, cosine, sine,
    grad_after, scales, sums_second, weights,
):
    count, width = normed.shape
    _, rowmap, dests = order
    columns = 3 * width + 128
    row = pl.BlockSpec((ROWS, width), lambda i: (i, 0))
    first = pl.BlockSpec((ROWS, width), lambda i: (0, 0))
    rest = pl.BlockSpec((ROWS, width), lambda i: (jnp.maximum(i - 1, 0), 0))
    table = pl.BlockSpec((ROWS, 128), lambda i: (i + MARGIN // ROWS, 0))
    half = columns // 256 * 128
    shapes = [jax.ShapeDtypeStruct((count, width), f32)] + [
        jax.ShapeDtypeStruct((1, width // 2, size), bf16)
        for size in (half, half, columns - half, columns - half)
    ]
    return pl.pallas_call(
        finish_kernel,
        grid=(count // ROWS,),
        in_specs=[smem(), whole(rowmap.shape), row, row]
        + [whole(piece.shape) for piece in grad_q]
        + [first, rest, first, rest]
        + [whole(halo.shape), table, table, row]
        + [whole(scales.shape), whole(sums_second.shape), whole(weights.shape)],
        out_specs=[row] + [whole(shape.shape) for shape in shapes[1:]],
        out_shape=shapes,
        scratch_shapes=[
            pltpu.VMEM((width, count), bf16),
            pltpu.VMEM((count, width), bf16),
            pltpu.VMEM((count, width), bf16),
            pltpu.VMEM((count, width), bf16),
            pltpu.VMEM((128, width), f32),
            pltpu.VMEM((width, 128), bf16),
        ],
        compiler_params=params(32),
        cost_estimate=cost(0, 10),
        name="finish_rows",
    )(
        dests, rowmap, inputs, normed, *grad_q, *grad_k, *grad_v, halo, cosine, sine,
        grad_after, scales, sums_second, weights,
    )


def adam_update(master, first, second, gradient, factor, rate):
    clipped = gradient * factor
    momentum = beta_first * first + (1.0 - beta_first) * clipped
    variance = beta_second * second + (1.0 - beta_second) * clipped * clipped
    corrected = momentum / (1.0 - beta_first**STEP)
    divisor = jnp.sqrt(variance / (1.0 - beta_second**STEP)) + adam_floor
    updated = master - rate * (corrected / divisor + weight_decay * master)
    return (momentum, variance, updated, updated.astype(bf16))


def full_sum(values):
    return jnp.sum(jnp.sum(values, axis=0, keepdims=True), axis=1, keepdims=True)


def book_kernel(keep, *refs):
    parts, (out, length) = refs[:-2], refs[-2:]
    total = keep[...]
    for part in parts:
        total = total + part[...].astype(f32)
    out[...] = total
    length[...] = full_sum(jnp.sum(total * total, axis=0))


def book_call(keep, parts):
    return pl.pallas_call(
        book_kernel,
        grid=(1,),
        in_specs=[whole(keep.shape)] * (1 + len(parts)),
        out_specs=[whole(keep.shape), whole((1, 1))],
        out_shape=[
            jax.ShapeDtypeStruct(keep.shape, f32),
            jax.ShapeDtypeStruct((1, 1), f32),
        ],
        compiler_params=params(16),
        cost_estimate=cost(BOOK_SHARE, 1),
        name="book_sums",
    )(keep, *parts)


def total_kernel(groups, squares, *refs):
    outs, shared = refs[-1 - len(groups) : -1], refs[-1]
    length = squares[...]
    base = 0
    for size, out in zip(groups, outs):
        total = refs[base][0]
        for part in refs[base + 1 : base + size]:
            total = total + part[0].astype(f32)
        base += size
        out[...] = total
        length = length + full_sum(total * total)
    shared[...] = jnp.broadcast_to(length, shared.shape)


def total_call(squares, groups, count):
    operands = [array for keep, parts in groups for array in (keep, *parts)]
    sizes = [1 + len(parts) for _, parts in groups]
    shapes = [keep.shape[1:] for keep, _ in groups] + [(count, 128)]
    return pl.pallas_call(
        lambda *refs: total_kernel(sizes, *refs),
        grid=(1,),
        in_specs=[whole((1, 1))] + [whole(operand.shape) for operand in operands],
        out_specs=[whole(shape) for shape in shapes],
        out_shape=[jax.ShapeDtypeStruct(shape, f32) for shape in shapes],
        compiler_params=params(16),
        cost_estimate=cost(0, 1),
        name="last_sums",
    )(squares, *operands)


def adam_kernel(shared, grad_feed, grad_qkv, grad_book, *refs):
    masters, firsts, seconds = refs[0:15:3], refs[1:15:3], refs[2:15:3]
    norm_ref = refs[15]
    outs = [refs[16 + 4 * group : 20 + 4 * group] for group in range(5)]
    norm = jnp.sqrt(jnp.sum(shared[:, 0:1], axis=0, keepdims=True))
    norm_ref[...] = norm
    factor = clip_level / jnp.maximum(norm, clip_level)

    def update(group, index, gradient):
        results = adam_update(
            masters[group][index], firsts[group][index], seconds[group][index],
            gradient, factor, group_rates[group],
        )
        for out, result in zip(outs[group], results):
            out[index] = result

    width = (grad_qkv.shape[1] - 128) // 3
    units = masters[1].shape[2]
    depth = masters[2].shape[1]
    for k in range(3):
        update(0, k, grad_qkv[:, k * width : (k + 1) * width])
    middle = units + depth
    update(1, 0, grad_feed[:, :units])
    update(2, Ellipsis, grad_feed[:, units:middle])
    update(1, 1, grad_feed[:, middle : middle + units])
    update(0, 3, grad_feed[:, middle + units :])
    for level in range(LEVELS):
        update(3, level, grad_book[level])
    update(4, Ellipsis, grad_qkv[:, 3 * width :].T[:6])


def adam_call(shared, gradients, states):
    operands = [shared, *gradients] + [array for group in states for array in group]
    shapes = [jax.ShapeDtypeStruct((1, 1), f32)] + [
        jax.ShapeDtypeStruct(group[0].shape, kind)
        for group in states
        for kind in (f32, f32, f32, bf16)
    ]
    return pl.pallas_call(
        adam_kernel,
        grid=(1,),
        in_specs=[whole(operand.shape) for operand in operands],
        out_specs=[whole(shape.shape) for shape in shapes],
        out_shape=shapes,
        compiler_params=params(40),
        cost_estimate=cost(3, 2),
        name="adam_step",
    )(*operands)


def turn_tables(positions, depth):
    half = depth // 2
    freqs = jnp.exp(-math.log(10000.0) * jnp.arange(half, dtype=f32) * 2.0 / depth)
    angles = positions.astype(f32)[:, None] * freqs[None, :]
    cosine, sine = jnp.cos(angles), jnp.sin(angles)
    return (
        jnp.concatenate([cosine] * 4, axis=1),
        jnp.concatenate([-sine, sine, -sine, sine], axis=1),
    )


def score_bias(count, offset):
    block = jnp.arange(count // QROWS, dtype=jnp.int32)[:, None, None]
    key_place = jnp.arange(SPAN, dtype=jnp.int32)[None, :, None]
    query_place = jnp.arange(QROWS, dtype=jnp.int32)[None, None, :]
    distance = MARGIN + query_place - key_place
    reach = offset + block * QROWS + key_place - MARGIN
    allowed = (distance >= 0) & (distance <= WINDOW) & (reach >= 0)
    return jnp.where(allowed, 0.0, masked_score).astype(f32)


def body(
    inputs, codes, levels,
    attention_master, attention_first, attention_second,
    feedforward_master, feedforward_first, feedforward_second,
    projection_master, projection_first, projection_second,
    codebook_master, codebook_first, codebook_second,
    scales_master, scales_first, scales_second,
):
    spans = lax.axis_size("tm")
    devices = lax.axis_size("clip") * spans
    me = lax.axis_index("clip") * spans + lax.axis_index("tm")
    frame_count, width = inputs.shape
    units = feedforward_master.shape[2]
    depth = projection_master.shape[1]
    rows = projection_master.shape[0]
    entries = codebook_master.shape[1] * devices

    early, feed, book = lower_call(
        attention_master, feedforward_master, projection_master, codebook_master, scales_master
    )
    mid = LEVELS // 2
    book = lax.all_gather(book, AXES, axis=1, tiled=True)
    stages = len(digit_plan(devices, 3))
    split_stages = len(digit_plan(devices, 4))
    halo = lax.ppermute(
        inputs[frame_count - MARGIN :], "tm", [(i, i + 1) for i in range(spans - 1)]
    )
    for stage in reversed(range(2, len(digit_plan(devices, 2)))):
        early = join(early, gather_swaps(early, devices, 2, stage))
    mark = early
    for stage in reversed(range(4, split_stages)):
        feed = join(feed, after(gather_swaps(feed, devices, 4, stage), early))
    offset = lax.axis_index("tm") * frame_count
    positions = after(offset, mark) - MARGIN + jnp.arange(frame_count + MARGIN, dtype=jnp.int32)
    cosine, sine = turn_tables(positions, width // HEADS)
    bias = score_bias(frame_count, after(offset, mark))
    def order(kind):
        owners = jnp.asarray(device_of_places(devices, kind)) ^ after(me, mark)
        starts = (owners * rows).astype(jnp.int32)
        if rows % 16 == 0:
            places = place_of(jnp.arange(devices, dtype=jnp.int32) ^ after(me, mark), devices, kind)
            return starts, jnp.zeros((1, 128), jnp.int32), (places * rows).astype(jnp.int32)
        rowmap = (starts[:, None] + jnp.arange(rows, dtype=jnp.int32)[None, :]).reshape(1, width)
        return starts, rowmap, starts

    orders = {kind: order(kind) for kind in range(2, 6)}
    share = entries // devices
    late_codes, late_me = after((codes, me), mark)
    owners = (late_codes // share) ^ late_me
    places = jnp.where(
        jnp.arange(LEVELS)[None, :] < mid,
        place_of(owners, devices, 4),
        place_of(owners, devices, 5),
    )
    places = (places * share + late_codes % share).astype(jnp.int32)
    flat_codes = jnp.concatenate([late_codes.T, places.T], axis=0)
    flat_codes, orders = after((flat_codes, orders), mark)
    ready = (cosine, sine, bias, flat_codes, orders)
    early = join(early, after(gather_swaps(early, devices, 2, 1), ready))
    come = after(gather_swaps(feed, devices, 4, 3), early)
    early_pieces = (early, swap(early, devices, 1))
    feed_a, feed_b = join(feed, come, (units, feed.shape[1] - units), 10)
    come_a = gather_swaps(feed_a, devices, 4, 2)
    come_b = gather_swaps(feed_b, devices, 5, 2)

    normed_first, q, k, v, scales, qkv_weights = qkv_call(
        *orders[2][:2], halo, inputs, early_pieces, cosine, sine
    )
    come_a, come_b = after((come_a, come_b), q)
    feed_a, feed_b = join(feed_a, come_a), join(feed_b, come_b)
    come_a = gather_swaps(feed_a, devices, 4, 1)
    come_b = gather_swaps(feed_b, devices, 5, 1)
    mixed, logsum = attend_call(q, after(k, feed_a, feed_b), v, bias)
    come_a, come_b = after((come_a, come_b), mixed)
    feed_a, feed_b = join(feed_a, come_a), join(feed_b, come_b)
    feed_pieces = (feed_a, swap(feed_a, devices, 1), feed_b, swap(feed_b, devices, 1))
    (
        branch_first, after_first, normed_second, hidden, slope, branch_second, low_out, latent,
        latent_again, feed_weights,
    ) = forward_call((orders[4][:2], orders[5][:2]), inputs, mixed, scales, feed_pieces, units, depth)

    carried = fetch_call(levels, flat_codes, latent_again, book)
    keep_high, send_high = spread_call(mid, mid, flat_codes, carried, entries)
    come_high = swap_parts([send_high], devices, 5, 0)
    carried = after(carried, keep_high)
    keep_low, send_low = spread_call(0, mid, flat_codes, carried, entries)
    come_low = swap_parts([send_low], devices, 4, 0)
    high = reduce_split(keep_high, after(come_high, keep_low), devices, 5, 1, 0, bf16)
    low = reduce_split(keep_low, after(come_low, high[0]), devices, 4, 1, 0, bf16)

    grad_after, grad_mixed, sums_second, keep_a, send_a, keep_b, send_b = backward_call(
        (orders[4], orders[5]), after(carried, high[0], low[0]), branch_second, slope, after_first, branch_first,
        normed_second, hidden, low_out, mixed, scales, feed_weights,
    )
    come_a = swap_parts([send_a], devices, 4, 0)
    come_b = swap_parts([send_b], devices, 5, 0)
    high = reduce_split(high[0], after(high[1], keep_a), devices, 5, 2, 2)
    low = reduce_split(low[0], after(low[1], high[0]), devices, 4, 2)

    lead = MARGIN // QROWS
    blocks = frame_count // QROWS
    zeros = jnp.zeros((MARGIN, width), f32)
    fixed = (logsum, bias, cosine, sine)
    grad_mixed = after(grad_mixed, low[0])
    q_a, k_a, v_a, halo = attend_back_call(0, lead, q, k, v, grad_mixed, *fixed, zeros, zeros)
    halo = lax.ppermute(halo, "tm", [(i + 1, i) for i in range(spans - 1)])
    come_a, come_b = after((come_a, come_b), k_a)
    keep_a, come_a = reduce_split(keep_a, come_a, devices, 4, 1)
    keep_b, come_b = reduce_split(keep_b, come_b, devices, 5, 1)
    grad_mixed = after(grad_mixed, keep_a, keep_b)
    q_b, k_b, v_b, _ = attend_back_call(lead, lead, q, k, v, grad_mixed, *fixed, k_a, v_a)
    come_low, come_high = after((low[1], high[1]), k_b)
    keep_book, come_book = stack_split((low[0], come_low), (high[0], come_high), devices, 4, 3)
    grad_mixed = after(grad_mixed, keep_book)
    q_c, k_c, v_c, _ = attend_back_call(
        2 * lead, blocks - 2 * lead, q, k, v, grad_mixed, *fixed, k_b, v_b
    )
    come_book, come_a, come_b = after((come_book, come_a, come_b), k_c)
    keep_a, come_a = reduce_split(keep_a, come_a, devices, 4, 2)
    keep_b, come_b = reduce_split(keep_b, come_b, devices, 5, 2)
    for stage in range(4, split_stages):
        keep_book, come_book = reduce_split(keep_book, come_book, devices, 4, stage)
    input_gradient, qkv_a, send_a, qkv_b, send_b = finish_call(
        orders[2], inputs, normed_first, (q_a, q_b, q_c),
        (k_b, after(k_c, keep_book, keep_a, keep_b)), (v_b, v_c), halo, cosine, sine, grad_after,
        scales, sums_second, qkv_weights,
    )
    send_a = swap_parts([send_a], devices, 2, 0)
    send_b = swap_parts([send_b], devices, 2, 0)
    grad_book, squares = book_call(keep_book, after(come_book, qkv_a))
    come_a, come_b = after((come_a, come_b), grad_book)
    keep_feed, come_feed = merge_split(
        ((keep_a, come_a), (keep_b, come_b)), devices, 4, 3, FEED_SHARE
    )
    send_a, send_b = after((send_a, send_b), keep_feed)
    keep_qkv, come_qkv = merge_split(((qkv_a, send_a), (qkv_b, send_b)), devices, 2, 1)
    for stage in range(4, split_stages):
        keep_feed, come_feed = reduce_split(keep_feed, come_feed, devices, 4, stage)
    for stage in range(2, len(digit_plan(devices, 2))):
        keep_qkv, come_qkv = reduce_split(keep_qkv, come_qkv, devices, 2, stage)
    grad_feed, grad_qkv, shared = total_call(
        squares, ((keep_feed, come_feed), (keep_qkv, come_qkv)), devices
    )

    shared = lax.all_to_all(shared, AXES, 0, 0, tiled=True)
    gradient_norm, *updated = adam_call(
        shared,
        (grad_feed, grad_qkv, grad_book),
        (
            (attention_master, attention_first, attention_second),
            (feedforward_master, feedforward_first, feedforward_second),
            (projection_master, projection_first, projection_second),
            (codebook_master, codebook_first, codebook_second),
            (scales_master, scales_first, scales_second),
        ),
    )
    return (latent, input_gradient, gradient_norm[0, 0], *updated)


def solution(mesh):
    rows = P(AXES, None)
    middle = P(None, AXES, None)
    scale = P(None, AXES)
    in_specs = (rows, rows, P("clip")) + (middle,) * 6 + (rows,) * 3 + (middle,) * 3 + (scale,) * 3
    out_specs = (rows, rows, P()) + (middle,) * 8 + (rows,) * 4 + (middle,) * 4 + (scale,) * 4
    return jax.shard_map(body, mesh=mesh, in_specs=in_specs, out_specs=out_specs, check_vma=False)
```
